32 devices in a mesh: loop: 16 (over z, x, core), own: 2 (over y).
Axes of the slice: x: 2, y: 2, z: 4, core: 2. Of those that a mesh axis runs over, the one named last changes fastest.
Arguments:
- factor_start: float32 [4096, 128], P(('loop', 'own')), may hold values from -6 to 6
- activity: float32 [4096], P(('loop', 'own')), may hold values from 0.05 to 2
- word_factors: bfloat16 [16, 8, 128, 128], P('loop'), may hold values from -0.09375 to 0.09375
- sub_factors: bfloat16 [2048, 128], replicated, may hold values from -6 to 6
- ratings: bfloat16 [16, 2, 16, 8, 128, 128], P('loop', 'own'), may hold values from -6 to 6
- user_tile: int32 [16, 2, 16, 8], P('loop', 'own'), may hold values from 0 to 1
- word_tile: int32 [16, 2, 16, 8], P('loop', 'own'), may hold values from 0 to 7
- subreddit: int32 [16, 2, 16, 8], P('loop', 'own'), may hold values from 0 to 2047
- counts: int32 [16, 2, 16], P('loop', 'own'), may hold values from 1 to 8
- runs: int32 [16, 2, 16, 8, 2, 128], P('loop', 'own'), may hold values from 0 to 128, as said below
Outputs:
- solution: float32 [4096, 128], P(('loop', 'own'))
- residual: float32 [4096, 128], P(('loop', 'own'))
The draws below stay inside these ranges and needn't reach their ends.
Inputs may be any that keep to these rules, and one draw needn't show every extreme that they name: runs[..., 0, a] is the first observed column of row a of a block and runs[..., 1, a] the number of observed columns, counted cyclically from it; each block has a row observed in full.
All inputs are finite; a program needn't handle non-finite values.
Results may differ from the reference program's by a relative error of at most 0.03.
Values may be sent and summed in bfloat16 or wider, within the bound.
No kernel may reach another device: no remote copies, remote signals or barrier semaphores. Data moves between devices by JAX's collectives and lax.ppermute only.
A program may use at most 128 MiB of HBM per device.

```python
import math
import jax
import jax.numpy as jnp
from jax import lax

R = 128
TILE = 128
UT = 2
SLOTS = 8
WB = 8
SUBS = 2048
ITERS = 2
U_TOT = 4096
OBS = 4644
N_LOOP = 16
N_OWN = 2


def draw_runs(key, part):
    shape = (N_LOOP, N_OWN, N_LOOP, SLOTS, TILE)
    key_start, key_len, key_pick = jax.random.split(key, 3)
    starts = jax.random.randint(key_start, shape, 0, TILE, dtype=jnp.int32)
    lengths = jax.random.randint(key_len, shape, 1, TILE + 1, dtype=jnp.int32)
    chosen = jax.random.randint(key_pick, shape[:-1] + (1,), 0, TILE, dtype=jnp.int32)
    full_row = jnp.arange(TILE, dtype=jnp.int32) == chosen
    lengths = jnp.where(full_row, TILE, lengths)
    starts = jnp.where(full_row, 0, starts)
    return jnp.stack([starts, lengths], axis=-2).astype(jnp.int32)


def with_ends(values, rng, smallest, largest):
    longest = values.shape.index(max(values.shape))
    spots = []
    for shift in (0, 1):
        where = [jax.random.randint(jax.random.fold_in(rng, axis), (), 0, length) for axis, length in enumerate(values.shape)]
        where[longest] = (where[longest] + shift) % values.shape[longest]
        spots.append(tuple(where))
    return values.at[spots[0]].set(smallest).at[spots[1]].set(largest)


def raised(drawn, rng, source, target, blocks, factor):
    owner, partner = [(jnp.arange(drawn.shape[dim]) // (drawn.shape[dim] // blocks)).reshape([-1 if axis == dim else 1 for axis in range(drawn.ndim)]) for dim in (source, target)]
    chosen = jax.random.permutation(rng, blocks)[partner]
    strong = (owner == chosen) | (owner == (partner + blocks // 2) % blocks)
    return jnp.where(strong, factor * drawn, drawn)


def block_scale(own_key, dims, shards, smallest, top_value):
    level = 1.0
    for axis_at, shards_of in shards:
        heights = jax.random.uniform(jax.random.fold_in(jax.random.fold_in(own_key, 6), axis_at), (shards_of,), jnp.float32, smallest / len(shards), top_value / len(shards))
        level = level * jnp.repeat(jnp.exp(heights), dims[axis_at] // shards_of).reshape((-1,) + (1,) * (len(dims) - 1 - axis_at))
    return level


def normal_values(rng, extent, deviation, most, cuts=(), held_as=jnp.bfloat16):
    drawn = jax.random.normal(rng, extent, jnp.float32) * deviation
    if len(cuts) > 0:
        drawn = block_scale(rng, extent, cuts, -0.22, 0.18) * drawn
    return jnp.clip(drawn, min=-most, max=most).astype(held_as)


def bell_draw_with(key, extent, spread, reach, cuts, heavy, held_as=jnp.bfloat16):
    values = spread * jax.random.normal(key, extent, jnp.float32)
    if cuts:
        values = values * block_scale(key, extent, cuts, -0.22, 0.18)
    return jnp.clip(raised(values, jax.random.fold_in(key, 3), *heavy), -reach, reach).astype(held_as)


def setup_inputs(seed: int = 0) -> dict:
    splits = jax.random.split(jax.random.key(seed), 11)
    return {
        "factor_start": normal_values(splits[0], (U_TOT, R), 1.0, 6.0, ((0, 32),), jnp.float32),
        "activity": jnp.clip(jnp.exp(math.log(2.0) - 3.6888794 * jax.random.uniform(splits[1], (U_TOT,), jnp.float32) ** block_scale(splits[1], (U_TOT,), ((0, 32),), -0.2, 0.2)), 0.05, 2.0),
        "word_factors": normal_values(splits[2], (N_LOOP, WB, TILE, R), OBS ** -0.5, 0.09375, ((0, 16),)),
        "sub_factors": normal_values(splits[3], (SUBS, R), 1.0, 6.0),
        "ratings": bell_draw_with(splits[4], (N_LOOP, N_OWN, N_LOOP, SLOTS, TILE, TILE), 1.0, 6.0, ((0, 16), (1, 2)), (0, 2, 16, 2.0)),
        "user_tile": with_ends(jax.random.randint(splits[5], (N_LOOP, N_OWN, N_LOOP, SLOTS), 0, UT), jax.random.fold_in(splits[5], 1), 0, UT - 1).astype(jnp.int32),
        "word_tile": with_ends(jax.random.randint(splits[6], (N_LOOP, N_OWN, N_LOOP, SLOTS), 0, WB), jax.random.fold_in(splits[6], 1), 0, WB - 1).astype(jnp.int32),
        "subreddit": with_ends(jax.random.randint(splits[7], (N_LOOP, N_OWN, N_LOOP, SLOTS), 0, SUBS), jax.random.fold_in(splits[7], 1), 0, SUBS - 1).astype(jnp.int32),
        "counts": with_ends(jax.random.randint(splits[8], (N_LOOP, N_OWN, N_LOOP), 1, SLOTS + 1), jax.random.fold_in(splits[8], 1), 1, SLOTS).astype(jnp.int32),
        "runs": draw_runs(jax.random.fold_in(splits[10], 71), 0),
    }


ridge = 0.05


def reference(factor_start, activity, word_factors, sub_factors, ratings, user_tile, word_tile, subreddit, counts, runs):
    def data_part(vector, with_values):
        rounded = vector.astype(jnp.bfloat16)
        rounded = lax.optimization_barrier(rounded)
        halves = rounded.astype(jnp.float32).reshape(N_LOOP, UT, TILE, R)

        def one_shard(running, shard):
            word_rows = word_factors[shard][word_tile[shard]]
            sub_rows = sub_factors[subreddit[shard]]
            products = (word_rows.astype(jnp.float32) * sub_rows[..., None, :].astype(jnp.float32)).astype(jnp.bfloat16)
            products = lax.optimization_barrier(products).astype(jnp.float32)
            slot_live = jnp.arange(SLOTS).astype(jnp.int32)[None, None, :] < counts[shard][..., None]
            first_col = runs[shard][..., 0, :]
            run_len = runs[shard][..., 1, :]
            columns = jnp.arange(TILE).astype(jnp.int32)
            observed = (((columns[None, None, None, None, :] - first_col[..., :, None]) % TILE) < run_len[..., :, None]) & slot_live[..., None, None]
            selector = (user_tile[shard][..., None] == jnp.arange(UT).astype(jnp.int32)).astype(jnp.float32)
            picked = jnp.einsum('ogsu,guar->ogsar', selector, halves)
            scores = jnp.einsum('ogsar,ogscr->ogsac', picked, products)
            if with_values:
                scores = ratings[shard].astype(jnp.float32) - scores
            weights = jnp.where(observed, scores, 0.0).astype(jnp.bfloat16)
            weights = lax.optimization_barrier(weights).astype(jnp.float32)
            rows_out = jnp.einsum('ogsac,ogscr->ogsar', weights, products)
            return running + jnp.einsum('ogsu,ogsar->guar', selector, rows_out), None

        start_sum = jnp.zeros((N_LOOP, UT, TILE, R), jnp.float32)
        result, unused = lax.scan(one_shard, start_sum, jnp.arange(N_LOOP).astype(jnp.int32))
        return result.reshape(N_LOOP * UT * TILE, R)

    weight_rows = activity[:, None]
    solution = factor_start
    residual = weight_rows * data_part(solution, True) - ridge * solution
    direction = residual
    norm_now = jnp.sum(residual * residual)
    for iteration in range(ITERS):
        image = weight_rows * data_part(direction, False) + ridge * direction
        step_size = norm_now / jnp.sum(direction * image)
        solution = solution + step_size * direction
        residual = residual - step_size * image
        if iteration + 1 < ITERS:
            norm_next = jnp.sum(residual * residual)
            direction = residual + (norm_next / norm_now) * direction
            norm_now = norm_next
    return solution, residual
```

```python
import jax
import jax.numpy as jnp
from jax import lax
from jax.experimental import pallas as pl
from jax.experimental.pallas import tpu as pltpu
from jax.sharding import PartitionSpec as P

AXES = ("loop", "own")
CHUNK = 4
ridge = 0.05
f32 = jnp.float32
bf16 = jnp.bfloat16


def dot_nt(left, right):
    return lax.dot_general(left, right, (((1,), (1,)), ((), ())), preferred_element_type=f32)


def dot_nn(left, right):
    return jnp.dot(left, right, preferred_element_type=f32)


def mask_columns(first, length, tile):
    column = lax.broadcasted_iota(jnp.int32, (tile, first.shape[-1]), 0)
    inside = ((column - first) & (tile - 1)) < length
    return jnp.where(inside, 1.0, 0.0).astype(bf16)


def rhs_kernel(counts, user_tile, word_tile, ratings, runs, sub_rows, words, out):
    slots, tile = ratings.shape[1], ratings.shape[2]
    tiles = out.shape[1] // tile
    group = pl.program_id(0)
    eye = (
        lax.broadcasted_iota(jnp.int32, (tile, tile), 0)
        == lax.broadcasted_iota(jnp.int32, (tile, tile), 1)
    ).astype(f32).astype(bf16)
    products, weights = [], []
    for s in range(slots):
        block = group * slots + s
        rows = words[word_tile[block]].astype(f32)
        products.append((rows * sub_rows[0, s : s + 1, :]).astype(bf16))
        first = runs[0, 2 * s : 2 * s + 1, :]
        length = runs[0, 2 * s + 1 : 2 * s + 2, :]
        seen = dot_nt(eye, mask_columns(first, length, tile))
        value = seen * ratings[0, s].astype(f32)
        live = s < counts[group]
        parts = []
        for u in range(tiles):
            mine = jnp.where(live & (user_tile[block] == u), 1.0, 0.0)
            parts.append((value * mine).astype(bf16))
        weights.append(jnp.concatenate(parts, axis=0))
    total = dot_nn(jnp.concatenate(weights, axis=1), jnp.concatenate(products, axis=0))
    out[0] = total.astype(out.dtype)


def rhs_partial(ratings, runs, sub_rows, words, counts, user_tile, word_tile, tiles):
    groups, slots, tile, _ = ratings.shape
    rank = words.shape[-1]
    return pl.pallas_call(
        rhs_kernel,
        grid_spec=pltpu.PrefetchScalarGridSpec(
            num_scalar_prefetch=3,
            grid=(groups,),
            in_specs=[
                pl.BlockSpec((1, slots, tile, tile), lambda g, *_: (g, 0, 0, 0)),
                pl.BlockSpec((1, 2 * slots, tile), lambda g, *_: (g, 0, 0)),
                pl.BlockSpec((1, slots, rank), lambda g, *_: (g, 0, 0)),
                pl.BlockSpec(words.shape, lambda g, *_: (0, 0, 0)),
            ],
            out_specs=pl.BlockSpec((1, tiles * tile, rank), lambda g, *_: (g, 0, 0)),
        ),
        out_shape=jax.ShapeDtypeStruct((groups, tiles * tile, rank), bf16),
        compiler_params=pltpu.CompilerParams(vmem_limit_bytes=32 * 2**20),
        cost_estimate=pl.CostEstimate(
            flops=2 * ratings.size * rank * 2, bytes_accessed=2 * ratings.size, transcendentals=0
        ),
        name="rhs",
    )(
        counts,
        user_tile.reshape(-1),
        word_tile.reshape(-1),
        ratings,
        runs.reshape(groups, 2 * slots, tile),
        sub_rows.astype(f32),
        words,
    )


def steps_kernel(
    flags, word_index, start, activity, received, words,
    first_out, second_out, third_out, dots_out,
    chosen, runs, subs, masks, products,
):
    own_rows, rank = start.shape
    sources = received.shape[0]
    tile = words.shape[1]
    slots = flags.shape[0] // sources
    blocks = flags.shape[0]
    cached = products is not None

    def gather_one(src, total):
        runs[pl.ds(pl.multiple_of(src * 2 * slots, 2 * slots), 2 * slots), :] = received[
            src, own_rows : own_rows + 2 * slots, :
        ].astype(f32)
        subs[pl.ds(pl.multiple_of(src * slots, slots), slots), :] = received[
            src, own_rows + 2 * slots : own_rows + 4 * slots, :
        ].astype(f32)[:slots]
        return total + received[src, :own_rows, :].astype(f32)

    rhs = lax.fori_loop(0, sources, gather_one, jnp.zeros((own_rows, rank), f32))

    def choose(j, n):
        chosen[n] = j
        return n + flags[j]

    used = lax.fori_loop(0, blocks, choose, 0)
    chunks = lax.div(used + CHUNK - 1, CHUNK)

    offset = lax.rem(lax.axis_index("own") * own_rows, tile)
    pick = (
        lax.broadcasted_iota(jnp.int32, (own_rows, tile), 0) + offset
        == lax.broadcasted_iota(jnp.int32, (own_rows, tile), 1)
    ).astype(f32).astype(bf16)

    def product(i):
        j = jnp.where(i < used, chosen[jnp.minimum(i, blocks - 1)], 0)
        return j, (words[word_index[j]].astype(f32) * subs[pl.ds(j, 1), :]).astype(bf16)

    def build(chunk, carry):
        parts = []
        for b in range(CHUNK):
            i = chunk * CHUNK + b
            j, block = product(i)
            if cached:
                products[chunk, b * tile : (b + 1) * tile, :] = block
            first = runs[pl.ds(2 * j, 1), :].astype(jnp.int32)
            length = runs[pl.ds(2 * j + 1, 1), :].astype(jnp.int32)
            length = jnp.where(i < used, length, 0)
            parts.append(dot_nt(pick, mask_columns(first, length, tile)).astype(bf16))
        masks[chunk] = jnp.concatenate(parts, axis=1)
        return carry

    lax.fori_loop(0, chunks, build, 0)

    def split(value):
        high = value.astype(bf16)
        low = (value - high.astype(f32)).astype(bf16)
        return jnp.concatenate([high, low], axis=0)

    def gram(vector):
        stacked = split(vector)

        def body(chunk, total):
            if cached:
                block = products[chunk]
            else:
                block = jnp.concatenate(
                    [product(chunk * CHUNK + b)[1] for b in range(CHUNK)], axis=0
                )
            scores = dot_nt(stacked, block)
            scores = scores[:own_rows] + scores[own_rows:]
            weights = scores * masks[chunk].astype(f32)
            return total + dot_nn(split(weights), block)

        total = lax.fori_loop(0, chunks, body, jnp.zeros((2 * own_rows, rank), f32))
        return total[:own_rows] + total[own_rows:]

    scale = activity[...]
    first = scale * (rhs - gram(start[...])) - ridge * start[...]
    second = scale * gram(first) + ridge * first
    third = scale * gram(second) + ridge * second
    first_out[...] = first
    second_out[...] = second
    third_out[...] = third
    pairs = [(first, first), (first, second), (second, second), (first, third), (second, third)]
    for k, (a, b) in enumerate(pairs):
        dots_out[k : k + 1, :] = jnp.sum(a * b, axis=0, keepdims=True)
    dots_out[len(pairs) :, :] = jnp.zeros((8 - len(pairs), rank), f32)


def krylov(flags, word_index, start, activity, received, words):
    own_rows, rank = start.shape
    blocks = flags.shape[0]
    tile = words.shape[1]
    chunks = -(-blocks // CHUNK)
    cached = blocks * tile * rank * 2 <= 16 * 2**20
    whole = pl.BlockSpec(memory_space=pltpu.VMEM)
    scalars = pl.BlockSpec(memory_space=pltpu.SMEM)
    vector = jax.ShapeDtypeStruct((own_rows, rank), f32)
    scratch = [
        pltpu.SMEM((blocks + 1,), jnp.int32),
        pltpu.VMEM((2 * blocks, tile), f32),
        pltpu.VMEM((blocks, rank), f32),
        pltpu.VMEM((chunks, own_rows, CHUNK * tile), bf16),
    ]
    kernel = steps_kernel
    if cached:
        scratch.append(pltpu.VMEM((chunks, CHUNK * tile, rank), bf16))
    else:

        def kernel(*refs):
            steps_kernel(*refs, None)

    return pl.pallas_call(
        kernel,
        in_specs=[scalars, scalars, whole, whole, whole, whole],
        out_specs=[whole] * 4,
        out_shape=[vector, vector, vector, jax.ShapeDtypeStruct((8, rank), f32)],
        scratch_shapes=scratch,
        compiler_params=pltpu.CompilerParams(vmem_limit_bytes=48 * 2**20),
        name="krylov",
    )(flags, word_index, start, activity, received, words)


def on_device(
    factor_start,
    activity,
    word_factors,
    sub_factors,
    ratings,
    user_tile,
    word_tile,
    subreddit,
    counts,
    runs,
):
    own_rows, rank = factor_start.shape
    owners = lax.axis_size("own")
    _, _, groups, slots, tile, _ = ratings.shape
    word_tiles = word_factors.shape[1]
    tiles = own_rows * owners // tile
    devices = groups * owners

    words = lax.all_gather(word_factors[0], "loop", axis=0, tiled=True)

    sub_rows = sub_factors[subreddit[0, 0]]
    partial = rhs_partial(
        ratings[0, 0], runs[0, 0], sub_rows, word_factors[0], counts[0, 0],
        user_tile[0, 0], word_tile[0, 0], tiles,
    )
    live = jnp.arange(slots)[None, :] < counts[0, 0][:, None]
    owner_tile = (jnp.arange(owners) * own_rows) // tile
    wanted = live[:, None, :] & (user_tile[0, 0][:, None, :] == owner_tile[None, :, None])
    facts = jnp.concatenate(
        [wanted.astype(bf16), jnp.broadcast_to(word_tile[0, 0][:, None, :], wanted.shape).astype(bf16)],
        axis=-1,
    )
    facts = jnp.pad(facts[:, :, None, :], ((0, 0), (0, 0), (0, slots - 1), (0, rank - 2 * slots)))

    def to_owners(value):
        return jnp.broadcast_to(value[:, None], (groups, owners) + value.shape[1:])

    message = jnp.concatenate(
        [
            partial.reshape(groups, owners, own_rows, rank),
            to_owners(runs[0, 0].reshape(groups, 2 * slots, tile).astype(bf16)),
            to_owners(sub_rows),
            facts,
        ],
        axis=2,
    ).reshape(devices, own_rows + 4 * slots, rank)
    received = lax.all_to_all(message, AXES, 0, 0, tiled=True)

    got = received[:, own_rows + 3 * slots, : 2 * slots].astype(jnp.int32)
    flags = got[:, :slots].reshape(-1)
    shard = jnp.arange(devices, dtype=jnp.int32)[:, None] // owners
    word_index = (got[:, slots:] + word_tiles * shard).reshape(-1)

    first, second, third, dots = krylov(
        flags, word_index, factor_start, activity[:, None], received, words
    )
    everyone = lax.all_to_all(
        jnp.broadcast_to(dots[None], (devices,) + dots.shape), AXES, 0, 0, tiled=True
    )
    sums = jnp.sum(everyone, axis=(0, 2))
    rr, rq, qq, rz, qz = (sums[k] for k in range(5))
    step0 = rr / rq
    next_rr = rr - 2.0 * step0 * rq + step0 * step0 * qq
    grow = 1.0 + next_rr / rr
    slope = grow * (grow * rq - step0 * (rz + qq)) + step0 * step0 * qz
    step1 = next_rr / slope
    solution = factor_start + (step0 + step1 * grow) * first - (step1 * step0) * second
    residual = first - (step0 + step1 * grow) * second + (step1 * step0) * third
    return (solution, residual)


def solution(mesh):
    placed = (
        P(("loop", "own"), None),
        P(("loop", "own")),
        P("loop", None, None, None),
        P(),
        P("loop", "own", None, None, None, None),
        P("loop", "own", None, None),
        P("loop", "own", None, None),
        P("loop", "own", None, None),
        P("loop", "own", None),
        P("loop", "own", None, None, None, None),
    )
    return jax.shard_map(
        on_device,
        mesh=mesh,
        in_specs=placed,
        out_specs=(P(("loop", "own"), None), P(("loop", "own"), None)),
        check_vma=False,
    )
```

```python
import functools

import jax
import jax.numpy as jnp
from jax import lax
from jax.experimental import pallas as pl
from jax.experimental.pallas import tpu as pltpu
from jax.sharding import PartitionSpec as P

AXES = ("loop", "own")
CHUNK = 8
ridge = 0.05
f32 = jnp.float32
bf16 = jnp.bfloat16


def dot_nt(left, right):
    return lax.dot_general(left, right, (((1,), (1,)), ((), ())), preferred_element_type=f32)


def dot_nn(left, right):
    return jnp.dot(left, right, preferred_element_type=f32)


def mask_columns(first, length, tile):
    column = lax.broadcasted_iota(jnp.int32, (tile, first.shape[-1]), 0)
    inside = ((column - first) & (tile - 1)) < length
    return jnp.where(inside, 1.0, 0.0).astype(bf16)


def message_kernel(counts, user_tile, word_tile, subreddit, ratings, runs, words, subs, out, table):
    slots, tile = ratings.shape[1], ratings.shape[2]
    owners, rank = out.shape[1], out.shape[3]
    own_rows = out.shape[2] - 4 * slots
    tiles = owners * own_rows // tile
    group = pl.program_id(0)

    @pl.when(group == 0)
    def _():
        table[...] = subs[...].astype(f32)

    eye = (
        lax.broadcasted_iota(jnp.int32, (tile, tile), 0)
        == lax.broadcasted_iota(jnp.int32, (tile, tile), 1)
    ).astype(f32).astype(bf16)
    lane = lax.broadcasted_iota(jnp.int32, (1, rank), 1)
    products, weights, sub_rows, run_rows = [], [], [], []
    facts = [jnp.zeros((1, rank), f32) for _ in range(owners)]
    for s in range(slots):
        sub_row = table[pl.ds(subreddit[group, s], 1), :]
        sub_rows.append(sub_row)
        products.append((words[word_tile[group, s]].astype(f32) * sub_row).astype(bf16))
        pair = runs[0, s]
        run_rows.append(pair)
        seen = dot_nt(eye, mask_columns(pair[0:1], pair[1:2], tile))
        value = seen * ratings[0, s].astype(f32)
        live = s < counts[0, group]
        parts = []
        for u in range(tiles):
            mine = jnp.where(live & (user_tile[group, s] == u), 1.0, 0.0)
            parts.append((value * mine).astype(bf16))
        weights.append(jnp.concatenate(parts, axis=0))
        for o in range(owners):
            wanted = live & (user_tile[group, s] == (o * own_rows) // tile)
            facts[o] = facts[o] + jnp.where(lane == s, jnp.where(wanted, 1.0, 0.0), 0.0)
            facts[o] = facts[o] + jnp.where(
                lane == slots + s, word_tile[group, s].astype(f32), 0.0
            )
    total = dot_nn(jnp.concatenate(weights, axis=1), jnp.concatenate(products, axis=0))
    run_rows = jnp.concatenate(run_rows, axis=0).astype(f32).astype(out.dtype)
    for o in range(owners):
        out[0, o, :own_rows, :] = total[o * own_rows : (o + 1) * own_rows].astype(out.dtype)
        out[0, o, own_rows : own_rows + 2 * slots, :] = run_rows
        out[0, o, own_rows + 2 * slots :, :] = jnp.concatenate(
            sub_rows + [facts[o]] + [jnp.zeros((slots - 1, rank), f32)], axis=0
        ).astype(out.dtype)


def messages(counts, user_tile, word_tile, subreddit, ratings, runs, words, subs, owners, own_rows):
    groups, slots, tile, _ = ratings.shape
    rank = words.shape[-1]
    shape = (owners, own_rows + 4 * slots, rank)
    return pl.pallas_call(
        message_kernel,
        grid_spec=pltpu.PrefetchScalarGridSpec(
            num_scalar_prefetch=4,
            grid=(groups,),
            in_specs=[
                pl.BlockSpec((1, slots, tile, tile), lambda g, *_: (g, 0, 0, 0)),
                pl.BlockSpec((1, slots, 2, tile), lambda g, *_: (g, 0, 0, 0)),
                pl.BlockSpec(words.shape, lambda g, *_: (0, 0, 0)),
                pl.BlockSpec(subs.shape, lambda g, *_: (0, 0)),
            ],
            out_specs=pl.BlockSpec((1,) + shape, lambda g, *_: (g, 0, 0, 0)),
            scratch_shapes=[pltpu.VMEM(subs.shape, f32)],
        ),
        out_shape=jax.ShapeDtypeStruct((groups,) + shape, bf16),
        compiler_params=pltpu.CompilerParams(vmem_limit_bytes=32 * 2**20),
        cost_estimate=pl.CostEstimate(
            flops=2 * ratings.size * rank * 2, bytes_accessed=2 * ratings.size, transcendentals=0
        ),
        name="messages",
    )(counts, user_tile, word_tile, subreddit, ratings, runs, words, subs)


def steps_kernel(flags, word_index, start, activity, received, *refs, cached):
    own_rows, rank = start.shape
    sources, _, _ = received.shape
    blocks = flags.shape[0]
    slots = blocks // sources
    shards = len(refs) - 10 - int(cached)
    pieces = refs[:shards]
    first_out, second_out, third_out, dots_out = refs[shards : shards + 4]
    chosen, runs, subs, masks, words, arrived = refs[shards + 4 : shards + 10]
    products = refs[-1]
    word_tiles, tile, _ = pieces[0].shape

    copies = [
        pltpu.make_async_copy(
            piece, words.at[k * word_tiles : (k + 1) * word_tiles], arrived.at[k]
        )
        for k, piece in enumerate(pieces)
    ]
    for copy in copies:
        copy.start()

    def gather_one(src, total):
        runs[pl.ds(pl.multiple_of(src * 2 * slots, 2 * slots), 2 * slots), :] = received[
            src, own_rows : own_rows + 2 * slots, :
        ].astype(f32)
        subs[pl.ds(pl.multiple_of(src * slots, slots), slots), :] = received[
            src, own_rows + 2 * slots : own_rows + 4 * slots, :
        ].astype(f32)[:slots]
        return total + received[src, :own_rows, :].astype(f32)

    rhs = lax.fori_loop(0, sources, gather_one, jnp.zeros((own_rows, rank), f32))

    def choose(j, n):
        chosen[n] = j
        return n + flags[j]

    used = lax.fori_loop(0, blocks, choose, 0, unroll=8)
    chunks = lax.div(used + CHUNK - 1, CHUNK)

    offset = lax.rem(lax.axis_index("own") * own_rows, tile)
    pick = (
        lax.broadcasted_iota(jnp.int32, (own_rows, tile), 0) + offset
        == lax.broadcasted_iota(jnp.int32, (own_rows, tile), 1)
    ).astype(f32).astype(bf16)

    def block_at(i):
        return jnp.where(i < used, chosen[jnp.minimum(i, blocks - 1)], 0)

    def product(i):
        j = block_at(i)
        return (words[word_index[j]].astype(f32) * subs[pl.ds(j, 1), :]).astype(bf16)

    def build_masks(chunk, carry):
        parts = []
        for b in range(CHUNK):
            i = chunk * CHUNK + b
            j = block_at(i)
            first = runs[pl.ds(2 * j, 1), :].astype(jnp.int32)
            length = runs[pl.ds(2 * j + 1, 1), :].astype(jnp.int32)
            length = jnp.where(i < used, length, 0)
            parts.append(dot_nt(pick, mask_columns(first, length, tile)).astype(bf16))
        masks[chunk] = jnp.concatenate(parts, axis=1)
        return carry

    def build_products(chunk, carry):
        for b in range(CHUNK):
            products[chunk, b * tile : (b + 1) * tile, :] = product(chunk * CHUNK + b)
        return carry

    lax.fori_loop(0, chunks, build_masks, 0)
    for copy in copies:
        copy.wait()
    if cached:
        lax.fori_loop(0, chunks, build_products, 0)

    def gram(vector):
        rounded = vector.astype(bf16)

        def body(chunk, total):
            if cached:
                block = products[chunk]
            else:
                block = jnp.concatenate(
                    [product(chunk * CHUNK + b) for b in range(CHUNK)], axis=0
                )
            weights = dot_nt(rounded, block).astype(bf16) * masks[chunk]
            return total + dot_nn(weights, block)

        return lax.fori_loop(0, chunks, body, jnp.zeros((own_rows, rank), f32))

    def over_row(a, b):
        return jnp.sum(a * b, axis=1, keepdims=True)

    scale = activity[...]
    first = scale * (rhs - gram(start[...])) - ridge * start[...]
    second = scale * gram(first) + ridge * first
    norms, overlaps = over_row(first, first), over_row(first, second)
    share = jnp.where(norms > 0.0, overlaps / jnp.where(norms > 0.0, norms, 1.0), 0.0)
    rest = second - share * first
    third = scale * gram(rest) + ridge * rest + share * second
    first_out[...] = first
    second_out[...] = second
    third_out[...] = third
    rows = [norms, overlaps, over_row(second, second), over_row(first, third), over_row(second, third)]
    lane = lax.broadcasted_iota(jnp.int32, (1, rank), 1)
    line = jnp.zeros((1, rank), f32)
    for k, value in enumerate(rows):
        line = line + jnp.where(lane == k, jnp.sum(value, axis=0, keepdims=True), 0.0)
    dots_out[...] = jnp.broadcast_to(line[None], dots_out.shape)


def krylov(flags, word_index, start, activity, received, pieces):
    own_rows, rank = start.shape
    sources = received.shape[0]
    blocks = flags.shape[0]
    word_tiles, tile, _ = pieces[0].shape
    chunks = -(-blocks // CHUNK)
    cached = blocks * tile * rank * 2 <= 16 * 2**20
    whole = pl.BlockSpec(memory_space=pltpu.VMEM)
    scalars = pl.BlockSpec(memory_space=pltpu.SMEM)
    vector = jax.ShapeDtypeStruct((own_rows, rank), f32)
    scratch = [
        pltpu.SMEM((blocks + 1,), jnp.int32),
        pltpu.VMEM((2 * blocks, tile), f32),
        pltpu.VMEM((blocks, rank), f32),
        pltpu.VMEM((chunks, own_rows, CHUNK * tile), bf16),
        pltpu.VMEM((len(pieces) * word_tiles, tile, rank), bf16),
        pltpu.SemaphoreType.DMA((len(pieces),)),
    ]
    if cached:
        scratch.append(pltpu.VMEM((chunks, CHUNK * tile, rank), bf16))
    return pl.pallas_call(
        functools.partial(steps_kernel, cached=cached),
        in_specs=[scalars, scalars, whole, whole, whole]
        + [pl.BlockSpec(memory_space=pl.ANY)] * len(pieces),
        out_specs=[whole] * 4,
        out_shape=[vector, vector, vector, jax.ShapeDtypeStruct((sources, 1, rank), f32)],
        scratch_shapes=scratch,
        compiler_params=pltpu.CompilerParams(vmem_limit_bytes=48 * 2**20),
        name="krylov",
    )(flags, word_index, start, activity, received, *pieces)


def last_kernel(dots, start, first, second, third, solution_out, residual_out):
    line = dots[0]
    for k in range(1, dots.shape[0]):
        line = line + dots[k]
    rr, rq, qq, rz, qz = (line[:, k : k + 1] for k in range(5))
    step0 = rr / rq
    next_rr = rr - 2.0 * step0 * rq + step0 * step0 * qq
    grow = 1.0 + next_rr / rr
    slope = grow * (grow * rq - step0 * (rz + qq)) + step0 * step0 * qz
    step1 = next_rr / slope
    near, far = step0 + step1 * grow, step1 * step0
    solution_out[...] = start[...] + near * first[...] - far * second[...]
    residual_out[...] = first[...] - near * second[...] + far * third[...]


def last_step(dots, start, first, second, third):
    whole = pl.BlockSpec(memory_space=pltpu.VMEM)
    vector = jax.ShapeDtypeStruct(start.shape, f32)
    return pl.pallas_call(
        last_kernel,
        in_specs=[whole] * 5,
        out_specs=[whole] * 2,
        out_shape=[vector, vector],
        name="last_step",
    )(dots, start, first, second, third)


def ring_place(shard, chips):
    chip = shard // 2
    level, column = chip // 2, chip % 2
    return jnp.where(column == 0, level, chips - 1 - level)


def ring_gather(mine, shards):
    chips = shards // 2
    levels = chips // 2
    order = [2 * level for level in range(levels)] + [
        2 * level + 1 for level in reversed(range(levels))
    ]

    def shift(by):
        return [
            (2 * order[p] + core, 2 * order[(p + by) % chips] + core)
            for p in range(chips)
            for core in range(2)
        ]

    other = [(shard, shard ^ 1) for shard in range(shards)]
    up = down = mine
    held = {0: mine}
    for step in range(1, chips // 2 + 1):
        up = lax.ppermute(up, "loop", shift(1))
        held[chips - step] = up
        if step < chips - step:
            down = lax.ppermute(down, "loop", shift(-1))
            held[step] = down
    pieces = []
    for distance in range(chips):
        pieces += [held[distance], lax.ppermute(held[distance], "loop", other)]
    return pieces


def on_device(
    factor_start,
    activity,
    word_factors,
    sub_factors,
    ratings,
    user_tile,
    word_tile,
    subreddit,
    counts,
    runs,
):
    own_rows, rank = factor_start.shape
    owners, shards = lax.axis_size("own"), lax.axis_size("loop")
    _, _, groups, slots, tile, _ = ratings.shape
    word_tiles = word_factors.shape[1]
    devices = shards * owners

    pieces = ring_gather(word_factors[0], shards)
    message = messages(
        counts[0], user_tile[0, 0], word_tile[0, 0], subreddit[0, 0],
        ratings[0, 0], runs[0, 0], word_factors[0], sub_factors, owners, own_rows,
    ).reshape(devices, own_rows + 4 * slots, rank)
    received = lax.all_to_all(message, AXES, 0, 0, tiled=True)

    got = received[:, own_rows + 3 * slots, : 2 * slots].astype(jnp.int32)
    flags = got[:, :slots].reshape(-1)
    me = lax.axis_index("loop")
    chips = shards // 2
    shard = jnp.arange(devices, dtype=jnp.int32)[:, None] // owners
    distance = (ring_place(shard, chips) - ring_place(me, chips)) % chips
    piece = 2 * distance + (shard + me) % 2
    word_index = (got[:, slots:] + word_tiles * piece).reshape(-1)

    first, second, third, dots = krylov(
        flags, word_index, factor_start, activity[:, None], received, pieces
    )
    everyone = lax.all_to_all(dots, AXES, 0, 0, tiled=True)
    return tuple(last_step(everyone, factor_start, first, second, third))


def solution(mesh):
    placed = (
        P(("loop", "own"), None),
        P(("loop", "own")),
        P("loop", None, None, None),
        P(),
        P("loop", "own", None, None, None, None),
        P("loop", "own", None, None),
        P("loop", "own", None, None),
        P("loop", "own", None, None),
        P("loop", "own", None),
        P("loop", "own", None, None, None, None),
    )
    return jax.shard_map(
        on_device,
        mesh=mesh,
        in_specs=placed,
        out_specs=(P(("loop", "own"), None), P(("loop", "own"), None)),
        check_vma=False,
    )
```

```python
import functools

import jax
import jax.numpy as jnp
from jax import lax
from jax.experimental import pallas as pl
from jax.experimental.pallas import tpu as pltpu
from jax.sharding import PartitionSpec as P

AXES = ("loop", "own")
CHUNK = 8
ridge = 0.05
VMEM_LIMIT = 60 * 2**20
f32 = jnp.float32
bf16 = jnp.bfloat16


def dot_nt(left, right):
    return lax.dot_general(left, right, (((1,), (1,)), ((), ())), preferred_element_type=f32)


def dot_nn(left, right):
    return jnp.dot(left, right, preferred_element_type=f32)


def mask_columns(first, length, tile):
    column = lax.broadcasted_iota(jnp.int32, (tile, first.shape[-1]), 0)
    inside = ((column - first) & (tile - 1)) < length
    return jnp.where(inside, 1.0, 0.0).astype(bf16)


def facts_kernel(scalars, runs, subs, out, table):
    groups, slots = runs.shape[0], runs.shape[1]
    owners, rank = out.shape[1], out.shape[3]
    table[...] = subs[...].astype(f32)
    lane = lax.broadcasted_iota(jnp.int32, (1, rank), 1)

    def body(group, carry):
        sub_rows, run_rows = [], []
        marks = jnp.zeros((1, rank), jnp.int32)
        live = scalars[group, 3 * slots]
        for s in range(slots):
            sub_rows.append(table[pl.ds(scalars[group, 2 * slots + s], 1), :])
            run_rows.append(runs[group, s])
            marks = jnp.where(lane == s, jnp.where(s < live, scalars[group, s] + 1, 0), marks)
            marks = jnp.where(lane == slots + s, scalars[group, slots + s], marks)
        run_rows = jnp.concatenate(run_rows, axis=0).astype(f32).astype(out.dtype)
        rest = jnp.concatenate(
            sub_rows + [marks.astype(f32), jnp.zeros((slots - 1, rank), f32)], axis=0
        ).astype(out.dtype)
        for o in range(owners):
            out[group, o, : 2 * slots, :] = run_rows
            out[group, o, 2 * slots :, :] = rest
        return carry

    lax.fori_loop(0, groups, body, 0)


def facts(scalars, runs, subs, owners):
    groups, slots, _, _ = runs.shape
    rank = subs.shape[1]
    whole = pl.BlockSpec(memory_space=pltpu.VMEM)
    return pl.pallas_call(
        facts_kernel,
        in_specs=[pl.BlockSpec(memory_space=pltpu.SMEM), whole, whole],
        out_specs=whole,
        out_shape=jax.ShapeDtypeStruct((groups, owners, 4 * slots, rank), bf16),
        scratch_shapes=[pltpu.VMEM(subs.shape, f32)],
        compiler_params=pltpu.CompilerParams(vmem_limit_bytes=VMEM_LIMIT),
        name="facts",
    )(scalars, runs, subs)


def rhs_kernel(scalars, ratings, runs, words, subs, out, table, sums):
    slots, tile = ratings.shape[1], ratings.shape[2]
    owners, own_rows = out.shape[1], out.shape[4]
    tiles = owners * own_rows // tile
    step = pl.program_id(0)
    group = scalars[step, 3 * slots + 1]

    @pl.when(step == 0)
    def _():
        table[...] = subs[...].astype(f32)

    eye = (
        lax.broadcasted_iota(jnp.int32, (tile, tile), 0)
        == lax.broadcasted_iota(jnp.int32, (tile, tile), 1)
    ).astype(f32).astype(bf16)
    products, weights = [], []
    live = scalars[group, 3 * slots]
    for s in range(slots):
        sub_row = table[pl.ds(scalars[group, 2 * slots + s], 1), :]
        products.append(
            (words[scalars[group, slots + s]].astype(f32) * sub_row).astype(bf16)
        )
        pair = runs[0, s]
        seen = dot_nt(eye, mask_columns(pair[0:1], pair[1:2], tile)).astype(bf16)
        value = seen * ratings[0, s]
        user = jnp.where(s < live, scalars[group, s], -1)
        weights.append(
            jnp.concatenate(
                [value * jnp.where(user == u, 1.0, 0.0).astype(bf16) for u in range(tiles)], axis=0
            )
        )
    sums[...] = dot_nn(jnp.concatenate(weights, axis=1), jnp.concatenate(products, axis=0))
    me = lax.axis_index("own")
    for o in range(owners):
        owner = lax.rem(me + o, owners)
        rows = pl.ds(pl.multiple_of(owner * own_rows, own_rows), own_rows)
        out[0, o, 0, 0] = sums[rows, :].astype(out.dtype)


def rhs_sums(scalars, ratings, runs, words, subs, owners, own_rows):
    groups, slots, tile, _ = ratings.shape
    rank = words.shape[-1]
    levels = groups // 4

    def there(i, scalars):
        return scalars[i, 3 * slots + 1]

    return pl.pallas_call(
        rhs_kernel,
        grid_spec=pltpu.PrefetchScalarGridSpec(
            num_scalar_prefetch=1,
            grid=(groups,),
            in_specs=[
                pl.BlockSpec((1, slots, tile, tile), lambda i, s: (there(i, s), 0, 0, 0)),
                pl.BlockSpec((1, slots, 2, tile), lambda i, s: (there(i, s), 0, 0, 0)),
                pl.BlockSpec(words.shape, lambda i, s: (0, 0, 0)),
                pl.BlockSpec(subs.shape, lambda i, s: (0, 0)),
            ],
            out_specs=pl.BlockSpec(
                (1, owners, 1, 1, own_rows, rank),
                lambda i, s: (i // (2 * levels), 0, (i // levels) % 2, i % levels, 0, 0),
            ),
            scratch_shapes=[pltpu.VMEM(subs.shape, f32), pltpu.VMEM((owners * own_rows, rank), f32)],
        ),
        out_shape=jax.ShapeDtypeStruct((2, owners, 2, levels, own_rows, rank), bf16),
        compiler_params=pltpu.CompilerParams(vmem_limit_bytes=VMEM_LIMIT),
        cost_estimate=pl.CostEstimate(
            flops=16 * ratings.size * rank, bytes_accessed=2 * ratings.size, transcendentals=0
        ),
        name="rhs",
    )(scalars, ratings, runs, words, subs)


def add(left, right):
    return (left.astype(f32) + right.astype(f32)).astype(bf16)


def reduce_rhs(sums, shards, owners):
    levels = shards // 4
    core = [(shard, shard ^ 1) for shard in range(shards)]
    column = [(shard, shard ^ 2) for shard in range(shards)]
    sums = add(sums[0], lax.ppermute(sums[1], "loop", core))
    total = sums[0]
    for o in range(1, owners):
        total = add(total, lax.ppermute(sums[o], "own", [(k, (k + o) % owners) for k in range(owners)]))
    total = add(total[0], lax.ppermute(total[1], "loop", column))
    terms = [total[0]]
    for up in range(1, levels):
        shift = [(shard, (shard + 4 * up) % shards) for shard in range(shards)]
        terms.append(lax.ppermute(total[up], "loop", shift))
    return terms


def masks_kernel(marks, received, chosen, subs, masks_out, runs, masks, sent):
    sources = received.shape[0]
    own_rows = masks.shape[1]
    tile = received.shape[2]
    blocks = subs.shape[0]
    slots = blocks // sources

    def choose(j, n):
        chosen[n] = j
        return n + marks[j]

    used = lax.fori_loop(0, blocks, choose, 0, unroll=8)
    chosen[blocks] = used
    chunks = lax.div(used + CHUNK - 1, CHUNK)

    def unpack(src, carry):
        runs[pl.ds(pl.multiple_of(src * 2 * slots, 2 * slots), 2 * slots), :] = received[
            src, : 2 * slots, :
        ].astype(f32)
        subs[pl.ds(pl.multiple_of(src * slots, slots), slots), :] = received[
            src, 2 * slots :, :
        ].astype(f32)[:slots]
        return carry

    lax.fori_loop(0, sources, unpack, 0)

    offset = lax.rem(lax.axis_index("own") * own_rows, tile)
    pick = (
        lax.broadcasted_iota(jnp.int32, (own_rows, tile), 0) + offset
        == lax.broadcasted_iota(jnp.int32, (own_rows, tile), 1)
    ).astype(f32).astype(bf16)

    def send(chunk):
        return pltpu.make_async_copy(masks.at[chunk], masks_out.at[chunk], sent.at[chunk])

    def build(chunk, carry):
        parts = []
        for b in range(CHUNK):
            i = chunk * CHUNK + b
            j = jnp.where(i < used, chosen[jnp.minimum(i, blocks - 1)], 0)
            first = runs[pl.ds(2 * j, 1), :].astype(jnp.int32)
            length = runs[pl.ds(2 * j + 1, 1), :].astype(jnp.int32)
            length = jnp.where(i < used, length, 0)
            parts.append(dot_nt(pick, mask_columns(first, length, tile)).astype(bf16))
        masks[chunk] = jnp.concatenate(parts, axis=1)
        send(chunk).start()
        return carry

    def finish(chunk, carry):
        send(chunk).wait()
        return carry

    lax.fori_loop(0, chunks, build, 0)
    lax.fori_loop(0, chunks, finish, 0)


def build_masks(marks, received, own_rows):
    sources, rows, tile = received.shape
    blocks = marks.shape[0]
    rank = received.shape[2]
    chunks = -(-blocks // CHUNK)
    whole = pl.BlockSpec(memory_space=pltpu.VMEM)
    scalars = pl.BlockSpec(memory_space=pltpu.SMEM)
    return pl.pallas_call(
        masks_kernel,
        in_specs=[scalars, whole],
        out_specs=[scalars, whole, pl.BlockSpec(memory_space=pl.ANY)],
        out_shape=[
            jax.ShapeDtypeStruct((blocks + 1,), jnp.int32),
            jax.ShapeDtypeStruct((blocks, rank), f32),
            jax.ShapeDtypeStruct((chunks, own_rows, CHUNK * tile), bf16),
        ],
        scratch_shapes=[
            pltpu.VMEM((2 * blocks, tile), f32),
            pltpu.VMEM((chunks, own_rows, CHUNK * tile), bf16),
            pltpu.SemaphoreType.DMA((chunks,)),
        ],
        compiler_params=pltpu.CompilerParams(vmem_limit_bytes=VMEM_LIMIT),
        name="masks",
    )(marks, received)


def steps_kernel(chosen, word_index, start, activity, subs, masks_in, *refs, shards, levels, cached):
    own_rows, rank = start.shape
    blocks = subs.shape[0]
    pieces, refs = refs[:shards], refs[shards:]
    terms, refs = refs[:levels], refs[levels:]
    first_out, second_out, third_out, dots_out = refs[:4]
    masks, words, arrived, loaded = refs[4:8]
    products = refs[-1]
    word_tiles, tile, _ = pieces[0].shape
    used = chosen[blocks]
    chunks = lax.div(used + CHUNK - 1, CHUNK)

    copies = [
        pltpu.make_async_copy(
            piece, words.at[k * word_tiles : (k + 1) * word_tiles], arrived.at[k]
        )
        for k, piece in enumerate(pieces)
    ]
    for copy in copies:
        copy.start()

    def load(chunk):
        return pltpu.make_async_copy(masks_in.at[chunk], masks.at[chunk], loaded.at[chunk])

    def begin(chunk, carry):
        load(chunk).start()
        return carry

    lax.fori_loop(0, chunks, begin, 0)

    def product(i):
        j = jnp.where(i < used, chosen[jnp.minimum(i, blocks - 1)], 0)
        return (words[word_index[j]].astype(f32) * subs[pl.ds(j, 1), :]).astype(bf16)

    def build(chunk, carry):
        load(chunk).wait()
        if cached:
            for b in range(CHUNK):
                products[chunk, b * tile : (b + 1) * tile, :] = product(chunk * CHUNK + b)
        return carry

    for copy in copies:
        copy.wait()
    lax.fori_loop(0, chunks, build, 0)

    def gram(vector):
        rounded = vector.astype(bf16)

        def body(chunk, total):
            if cached:
                block = products[chunk]
            else:
                block = jnp.concatenate(
                    [product(chunk * CHUNK + b) for b in range(CHUNK)], axis=0
                )
            weights = dot_nt(rounded, block).astype(bf16) * masks[chunk]
            return total + dot_nn(weights, block)

        return lax.fori_loop(0, chunks, body, jnp.zeros((own_rows, rank), f32))

    def over_row(a, b):
        return jnp.sum(a * b, axis=1, keepdims=True)

    scale = activity[...]
    rhs = terms[0][...].astype(f32)
    for term in terms[1:]:
        rhs = rhs + term[...].astype(f32)
    first = scale * (rhs - gram(start[...])) - ridge * start[...]
    second = scale * gram(first) + ridge * first
    norms, overlaps = over_row(first, first), over_row(first, second)
    share = jnp.where(norms > 0.0, overlaps / jnp.where(norms > 0.0, norms, 1.0), 0.0)
    rest = second - share * first
    third = scale * gram(rest) + ridge * rest + share * second
    first_out[...] = first
    second_out[...] = second
    third_out[...] = third
    rows = [norms, overlaps, over_row(second, second), over_row(first, third), over_row(second, third)]
    lane = lax.broadcasted_iota(jnp.int32, (1, rank), 1)
    line = jnp.zeros((1, rank), f32)
    for k, value in enumerate(rows):
        line = line + jnp.where(lane == k, jnp.sum(value, axis=0, keepdims=True), 0.0)
    dots_out[...] = jnp.broadcast_to(line[None], dots_out.shape)


def krylov(chosen, word_index, start, activity, subs, masks, pieces, terms, devices):
    own_rows, rank = start.shape
    blocks = subs.shape[0]
    word_tiles, tile, _ = pieces[0].shape
    chunks = masks.shape[0]
    cached = blocks * tile * rank * 2 <= 16 * 2**20
    whole = pl.BlockSpec(memory_space=pltpu.VMEM)
    scalars = pl.BlockSpec(memory_space=pltpu.SMEM)
    anywhere = pl.BlockSpec(memory_space=pl.ANY)
    vector = jax.ShapeDtypeStruct((own_rows, rank), f32)
    scratch = [
        pltpu.VMEM(masks.shape, bf16),
        pltpu.VMEM((len(pieces) * word_tiles, tile, rank), bf16),
        pltpu.SemaphoreType.DMA((len(pieces),)),
        pltpu.SemaphoreType.DMA((chunks,)),
    ]
    if cached:
        scratch.append(pltpu.VMEM((chunks, CHUNK * tile, rank), bf16))
    return pl.pallas_call(
        functools.partial(
            steps_kernel, shards=len(pieces), levels=len(terms), cached=cached
        ),
        in_specs=[scalars, scalars, whole, whole, whole, anywhere]
        + [anywhere] * len(pieces)
        + [whole] * len(terms),
        out_specs=[whole] * 4,
        out_shape=[vector, vector, vector, jax.ShapeDtypeStruct((devices, 1, rank), f32)],
        scratch_shapes=scratch,
        compiler_params=pltpu.CompilerParams(vmem_limit_bytes=VMEM_LIMIT),
        name="krylov",
    )(chosen, word_index, start, activity, subs, masks, *pieces, *terms)


def last_kernel(dots, start, first, second, third, solution_out, residual_out):
    line = dots[0]
    for k in range(1, dots.shape[0]):
        line = line + dots[k]
    rr, rq, qq, rz, qz = (line[:, k : k + 1] for k in range(5))
    step0 = rr / rq
    next_rr = rr - 2.0 * step0 * rq + step0 * step0 * qq
    grow = 1.0 + next_rr / rr
    slope = grow * (grow * rq - step0 * (rz + qq)) + step0 * step0 * qz
    step1 = next_rr / slope
    near, far = step0 + step1 * grow, step1 * step0
    solution_out[...] = start[...] + near * first[...] - far * second[...]
    residual_out[...] = first[...] - near * second[...] + far * third[...]


def last_step(dots, start, first, second, third):
    whole = pl.BlockSpec(memory_space=pltpu.VMEM)
    vector = jax.ShapeDtypeStruct(start.shape, f32)
    return pl.pallas_call(
        last_kernel,
        in_specs=[whole] * 5,
        out_specs=[whole] * 2,
        out_shape=[vector, vector],
        compiler_params=pltpu.CompilerParams(vmem_limit_bytes=VMEM_LIMIT),
        name="last_step",
    )(dots, start, first, second, third)


def ring_place(shard, chips):
    chip = shard // 2
    level, column = chip // 2, chip % 2
    return jnp.where(column == 0, level, chips - 1 - level)


def ring_gather(mine, shards):
    chips = shards // 2
    levels = chips // 2
    order = [2 * level for level in range(levels)] + [
        2 * level + 1 for level in reversed(range(levels))
    ]

    def shift(by):
        return [
            (2 * order[p] + core, 2 * order[(p + by) % chips] + core)
            for p in range(chips)
            for core in range(2)
        ]

    other = [(shard, shard ^ 1) for shard in range(shards)]
    up = down = mine
    held = {0: mine}
    for step in range(1, chips // 2 + 1):
        up = lax.ppermute(up, "loop", shift(1))
        held[chips - step] = up
        if step < chips - step:
            down = lax.ppermute(down, "loop", shift(-1))
            held[step] = down
    pieces = []
    for distance in range(chips):
        pieces += [held[distance], lax.ppermute(held[distance], "loop", other)]
    return pieces


def on_device(
    factor_start,
    activity,
    word_factors,
    sub_factors,
    ratings,
    user_tile,
    word_tile,
    subreddit,
    counts,
    runs,
):
    own_rows, rank = factor_start.shape
    owners, shards = lax.axis_size("own"), lax.axis_size("loop")
    _, _, groups, slots, tile, _ = ratings.shape
    word_tiles = word_factors.shape[1]
    devices = shards * owners
    chips, levels = shards // 2, shards // 4
    me, owner = lax.axis_index("loop"), lax.axis_index("own")

    step = jnp.arange(groups, dtype=jnp.int32)
    level = (me // 4 + step % levels) % levels
    order = 4 * level + (me % 4) ^ (2 * ((step // levels) % 2) + step // (2 * levels))
    scalars = jnp.concatenate(
        [user_tile[0, 0], word_tile[0, 0], subreddit[0, 0], counts[0, 0][:, None], order[:, None]],
        axis=1,
    )

    pieces = ring_gather(word_factors[0], shards)
    message = facts(scalars, runs[0, 0], sub_factors, owners).reshape(devices, 4 * slots, rank)
    received = lax.all_to_all(message, AXES, 0, 0, tiled=True)
    sums = rhs_sums(
        scalars, ratings[0, 0], runs[0, 0], word_factors[0], sub_factors, owners, own_rows
    )
    terms = reduce_rhs(sums, shards, owners)

    got = received[:, 3 * slots, : 2 * slots].astype(jnp.int32)
    marks = (got[:, :slots] == owner * own_rows // tile + 1).astype(jnp.int32).reshape(-1)
    shard = jnp.arange(devices, dtype=jnp.int32)[:, None] // owners
    distance = (ring_place(shard, chips) - ring_place(me, chips)) % chips
    piece = 2 * distance + (shard + me) % 2
    word_index = (got[:, slots:] + word_tiles * piece).reshape(-1)

    chosen, subs, masks = build_masks(marks, received, own_rows)
    first, second, third, dots = krylov(
        chosen, word_index, factor_start, activity[:, None], subs, masks, pieces, terms, devices
    )
    everyone = lax.all_to_all(dots, AXES, 0, 0, tiled=True)
    return tuple(last_step(everyone, factor_start, first, second, third))


def solution(mesh):
    placed = (
        P(("loop", "own"), None),
        P(("loop", "own")),
        P("loop", None, None, None),
        P(),
        P("loop", "own", None, None, None, None),
        P("loop", "own", None, None),
        P("loop", "own", None, None),
        P("loop", "own", None, None),
        P("loop", "own", None),
        P("loop", "own", None, None, None, None),
    )
    return jax.shard_map(
        on_device,
        mesh=mesh,
        in_specs=placed,
        out_specs=(P(("loop", "own"), None), P(("loop", "own"), None)),
        check_vma=False,
    )
```

```python
import functools

import jax
import jax.numpy as jnp
from jax import lax
from jax.experimental import pallas as pl
from jax.experimental.pallas import tpu as pltpu
from jax.sharding import PartitionSpec as P

AXES = ("loop", "own")
CHUNK = 8
ridge = 0.05
VMEM_LIMIT = 60 * 2**20
f32 = jnp.float32
bf16 = jnp.bfloat16


def dot_nt(left, right):
    return lax.dot_general(left, right, (((1,), (1,)), ((), ())), preferred_element_type=f32)


def dot_nn(left, right):
    return jnp.dot(left, right, preferred_element_type=f32)


def mask_columns(first, length, tile):
    column = lax.broadcasted_iota(jnp.int32, (tile, first.shape[-1]), 0)
    inside = ((column - first) & (tile - 1)) < length
    return jnp.where(inside, 1.0, 0.0).astype(bf16)


def facts_kernel(scalars, runs, subs, out, table):
    groups, slots = runs.shape[0], runs.shape[1]
    owners, rank = out.shape[1], out.shape[3]
    table[...] = subs[...].astype(f32)
    lane = lax.broadcasted_iota(jnp.int32, (1, rank), 1)

    def body(group, carry):
        sub_rows, run_rows = [], []
        marks = jnp.zeros((1, rank), jnp.int32)
        live = scalars[group, 3 * slots]
        for s in range(slots):
            sub_rows.append(table[pl.ds(scalars[group, 2 * slots + s], 1), :])
            run_rows.append(runs[group, s])
            marks = jnp.where(lane == s, jnp.where(s < live, scalars[group, s] + 1, 0), marks)
            marks = jnp.where(lane == slots + s, scalars[group, slots + s], marks)
        run_rows = jnp.concatenate(run_rows, axis=0).astype(f32).astype(out.dtype)
        rest = jnp.concatenate(
            sub_rows + [marks.astype(f32), jnp.zeros((slots - 1, rank), f32)], axis=0
        ).astype(out.dtype)
        for o in range(owners):
            out[group, o, : 2 * slots, :] = run_rows
            out[group, o, 2 * slots :, :] = rest
        return carry

    lax.fori_loop(0, groups, body, 0)


def facts(scalars, runs, subs, owners):
    groups, slots, _, _ = runs.shape
    rank = subs.shape[1]
    whole = pl.BlockSpec(memory_space=pltpu.VMEM)
    return pl.pallas_call(
        facts_kernel,
        in_specs=[pl.BlockSpec(memory_space=pltpu.SMEM), whole, whole],
        out_specs=whole,
        out_shape=jax.ShapeDtypeStruct((groups, owners, 4 * slots, rank), bf16),
        scratch_shapes=[pltpu.VMEM(subs.shape, f32)],
        compiler_params=pltpu.CompilerParams(vmem_limit_bytes=VMEM_LIMIT),
        name="facts",
    )(scalars, runs, subs)


def rhs_kernel(scalars, ratings_in, runs_in, words_in, subs_in, *refs, half, owners, own_rows):
    given, refs = (refs[0], refs[1:]) if half == 0 else (None, refs)
    outs, (ratings, runs, words, subs, table, sums, arrived, loaded) = refs[:-8], refs[-8:]
    steps, slots, tile = ratings.shape[0], ratings.shape[1], ratings.shape[2]
    levels = steps // 2

    def load(step):
        group = scalars[half * steps + step, 3 * slots + 1]
        return pltpu.make_async_copy(ratings_in.at[group], ratings.at[step], arrived.at[step])

    tables = [
        pltpu.make_async_copy(source, target, loaded.at[k])
        for k, (source, target) in enumerate(
            [(subs_in, subs), (runs_in, runs), (words_in, words)]
        )
    ]
    for copy in tables:
        copy.start()
    for step in range(steps):
        load(step).start()
    tables[0].wait()
    table[...] = subs[...].astype(f32)
    tables[1].wait()
    tables[2].wait()

    eye = (
        lax.broadcasted_iota(jnp.int32, (tile, tile), 0)
        == lax.broadcasted_iota(jnp.int32, (tile, tile), 1)
    ).astype(f32).astype(bf16)
    me = lax.axis_index("own")
    for step in range(steps):
        group = scalars[half * steps + step, 3 * slots + 1]
        live = scalars[group, 3 * slots]
        columns = []
        for s in range(slots):
            pair = runs[group, s]
            columns.append(
                mask_columns(pair[0:1], jnp.where(s < live, pair[1:2], 0), tile)
            )
        seen = dot_nt(eye, jnp.concatenate(columns, axis=0)).astype(bf16)
        load(step).wait()
        sums[step % 2] = jnp.zeros(sums.shape[1:], f32)
        for s in range(slots):
            sub_row = table[pl.ds(scalars[group, 2 * slots + s], 1), :]
            product = (words[scalars[group, slots + s]].astype(f32) * sub_row).astype(bf16)
            weights = seen[:, s * tile : (s + 1) * tile] * ratings[step, s]
            rows = pl.ds(pl.multiple_of(scalars[group, s] * tile, tile), tile)
            sums[step % 2, rows, :] += dot_nn(weights, product)
        for o in range(owners):
            owner = lax.rem(me + o, owners)
            rows = pl.ds(pl.multiple_of(owner * own_rows, own_rows), own_rows)
            value = sums[step % 2, rows, :]
            if half == 0:
                value = value + given[o, step // levels, step % levels].astype(f32)
                outs[2 * o + step // levels][step % levels] = value.astype(bf16)
            else:
                outs[0][o, step // levels, step % levels] = value.astype(bf16)


def rhs_sums(scalars, ratings, runs, words, subs, half, given, owners, own_rows):
    groups, slots, tile, _ = ratings.shape
    rank = words.shape[-1]
    steps, levels = groups // 2, groups // 4
    anywhere = pl.BlockSpec(memory_space=pl.ANY)
    whole = pl.BlockSpec(memory_space=pltpu.VMEM)
    part = (levels, own_rows, rank)
    shapes = [part] * (2 * owners) if half == 0 else [(owners, 2) + part]
    return pl.pallas_call(
        functools.partial(rhs_kernel, half=half, owners=owners, own_rows=own_rows),
        in_specs=[pl.BlockSpec(memory_space=pltpu.SMEM)] + [anywhere] * 4 + [whole] * (1 - half),
        out_specs=[whole] * len(shapes),
        out_shape=[jax.ShapeDtypeStruct(shape, bf16) for shape in shapes],
        scratch_shapes=[
            pltpu.VMEM((steps,) + ratings.shape[1:], bf16),
            pltpu.VMEM(runs.shape, jnp.int32),
            pltpu.VMEM(words.shape, bf16),
            pltpu.VMEM(subs.shape, bf16),
            pltpu.VMEM(subs.shape, f32),
            pltpu.VMEM((2, owners * own_rows, rank), f32),
            pltpu.SemaphoreType.DMA((steps,)),
            pltpu.SemaphoreType.DMA((3,)),
        ],
        compiler_params=pltpu.CompilerParams(vmem_limit_bytes=VMEM_LIMIT),
        cost_estimate=pl.CostEstimate(
            flops=8 * ratings.size * rank, bytes_accessed=8 * ratings.size, transcendentals=0
        ),
        name="rhs",
    )(scalars, ratings, runs, words, subs, *([given] if half == 0 else []))


def reduce_chip(parts, shards, owners):
    total = [part.astype(f32) for part in parts[:1]]
    for o in range(owners):
        for column in range(2):
            if o or column:
                pairs = [
                    (shard * owners + k, (shard ^ 2 * column) * owners + (k + o) % owners)
                    for shard in range(shards)
                    for k in range(owners)
                ]
                total.append(lax.ppermute(parts[2 * o + column], AXES, pairs).astype(f32))
    return sum(total[1:], total[0]).astype(bf16)


def reduce_levels(total, shards):
    levels = shards // 4
    terms = [total[0]]
    for up in range(1, levels):
        shift = [(shard, (shard + 4 * up) % shards) for shard in range(shards)]
        terms.append(lax.ppermute(total[up], "loop", shift))
    return terms


def masks_kernel(marks, received, chosen, subs, masks_out, runs, masks, sent):
    sources = received.shape[0]
    own_rows = masks.shape[1]
    tile = received.shape[2]
    blocks = subs.shape[0]
    slots = blocks // sources

    def choose(j, n):
        chosen[n] = j
        return n + marks[j]

    used = lax.fori_loop(0, blocks, choose, 0, unroll=8)
    chosen[blocks] = used
    chunks = lax.div(used + CHUNK - 1, CHUNK)

    def unpack(src, carry):
        runs[pl.ds(pl.multiple_of(src * 2 * slots, 2 * slots), 2 * slots), :] = received[
            src, : 2 * slots, :
        ].astype(f32)
        subs[pl.ds(pl.multiple_of(src * slots, slots), slots), :] = received[
            src, 2 * slots :, :
        ].astype(f32)[:slots]
        return carry

    lax.fori_loop(0, sources, unpack, 0)

    offset = lax.rem(lax.axis_index("own") * own_rows, tile)
    pick = (
        lax.broadcasted_iota(jnp.int32, (own_rows, tile), 0) + offset
        == lax.broadcasted_iota(jnp.int32, (own_rows, tile), 1)
    ).astype(f32).astype(bf16)

    def send(chunk):
        return pltpu.make_async_copy(masks.at[chunk], masks_out.at[chunk], sent.at[chunk])

    def build(chunk, carry):
        parts = []
        for b in range(CHUNK):
            i = chunk * CHUNK + b
            j = jnp.where(i < used, chosen[jnp.minimum(i, blocks - 1)], 0)
            first = runs[pl.ds(2 * j, 1), :].astype(jnp.int32)
            length = runs[pl.ds(2 * j + 1, 1), :].astype(jnp.int32)
            length = jnp.where(i < used, length, 0)
            parts.append(dot_nt(pick, mask_columns(first, length, tile)).astype(bf16))
        masks[chunk] = jnp.concatenate(parts, axis=1)
        send(chunk).start()
        return carry

    def finish(chunk, carry):
        send(chunk).wait()
        return carry

    lax.fori_loop(0, chunks, build, 0)
    lax.fori_loop(0, chunks, finish, 0)


def build_masks(marks, received, own_rows):
    sources, rows, tile = received.shape
    blocks = marks.shape[0]
    rank = received.shape[2]
    chunks = -(-blocks // CHUNK)
    whole = pl.BlockSpec(memory_space=pltpu.VMEM)
    scalars = pl.BlockSpec(memory_space=pltpu.SMEM)
    return pl.pallas_call(
        masks_kernel,
        in_specs=[scalars, whole],
        out_specs=[scalars, whole, pl.BlockSpec(memory_space=pl.ANY)],
        out_shape=[
            jax.ShapeDtypeStruct((blocks + 1,), jnp.int32),
            jax.ShapeDtypeStruct((blocks, rank), f32),
            jax.ShapeDtypeStruct((chunks, own_rows, CHUNK * tile), bf16),
        ],
        scratch_shapes=[
            pltpu.VMEM((2 * blocks, tile), f32),
            pltpu.VMEM((chunks, own_rows, CHUNK * tile), bf16),
            pltpu.SemaphoreType.DMA((chunks,)),
        ],
        compiler_params=pltpu.CompilerParams(vmem_limit_bytes=VMEM_LIMIT),
        name="masks",
    )(marks, received)


def steps_kernel(chosen, word_index, start, activity, subs, masks_in, *refs, shards, levels, cached):
    own_rows, rank = start.shape
    blocks = subs.shape[0]
    pieces, refs = refs[:shards], refs[shards:]
    terms, refs = refs[:levels], refs[levels:]
    first_out, second_out, third_out, dots_out = refs[:4]
    masks, words, arrived, loaded = refs[4:8]
    products = refs[-1]
    word_tiles, tile, _ = pieces[0].shape
    used = chosen[blocks]
    chunks = lax.div(used + CHUNK - 1, CHUNK)

    copies = [
        pltpu.make_async_copy(
            piece, words.at[k * word_tiles : (k + 1) * word_tiles], arrived.at[k]
        )
        for k, piece in enumerate(pieces)
    ]
    for copy in copies:
        copy.start()

    def load(chunk):
        return pltpu.make_async_copy(masks_in.at[chunk], masks.at[chunk], loaded.at[chunk])

    def begin(chunk, carry):
        load(chunk).start()
        return carry

    lax.fori_loop(0, chunks, begin, 0)

    def product(i):
        j = jnp.where(i < used, chosen[jnp.minimum(i, blocks - 1)], 0)
        return (words[word_index[j]].astype(f32) * subs[pl.ds(j, 1), :]).astype(bf16)

    def build(chunk, carry):
        load(chunk).wait()
        if cached:
            for b in range(CHUNK):
                products[chunk, b * tile : (b + 1) * tile, :] = product(chunk * CHUNK + b)
        return carry

    for copy in copies:
        copy.wait()
    lax.fori_loop(0, chunks, build, 0)

    def gram(vector):
        rounded = vector.astype(bf16)

        def body(chunk, total):
            if cached:
                block = products[chunk]
            else:
                block = jnp.concatenate(
                    [product(chunk * CHUNK + b) for b in range(CHUNK)], axis=0
                )
            weights = dot_nt(rounded, block).astype(bf16) * masks[chunk]
            return total + dot_nn(weights, block)

        return lax.fori_loop(0, chunks, body, jnp.zeros((own_rows, rank), f32))

    def over_row(a, b):
        return jnp.sum(a * b, axis=1, keepdims=True)

    scale = activity[...]
    rhs = terms[0][...].astype(f32)
    for term in terms[1:]:
        rhs = rhs + term[...].astype(f32)
    first = scale * (rhs - gram(start[...])) - ridge * start[...]
    second = scale * gram(first) + ridge * first
    norms, overlaps = over_row(first, first), over_row(first, second)
    share = jnp.where(norms > 0.0, overlaps / jnp.where(norms > 0.0, norms, 1.0), 0.0)
    rest = second - share * first
    third = scale * gram(rest) + ridge * rest + share * second
    first_out[...] = first
    second_out[...] = second
    third_out[...] = third
    rows = [norms, overlaps, over_row(second, second), over_row(first, third), over_row(second, third)]
    lane = lax.broadcasted_iota(jnp.int32, (1, rank), 1)
    line = jnp.zeros((1, rank), f32)
    for k, value in enumerate(rows):
        line = line + jnp.where(lane == k, jnp.sum(value, axis=0, keepdims=True), 0.0)
    dots_out[...] = jnp.broadcast_to(line[None], dots_out.shape)


def krylov(chosen, word_index, start, activity, subs, masks, pieces, terms, devices):
    own_rows, rank = start.shape
    blocks = subs.shape[0]
    word_tiles, tile, _ = pieces[0].shape
    chunks = masks.shape[0]
    cached = blocks * tile * rank * 2 <= 16 * 2**20
    whole = pl.BlockSpec(memory_space=pltpu.VMEM)
    scalars = pl.BlockSpec(memory_space=pltpu.SMEM)
    anywhere = pl.BlockSpec(memory_space=pl.ANY)
    vector = jax.ShapeDtypeStruct((own_rows, rank), f32)
    scratch = [
        pltpu.VMEM(masks.shape, bf16),
        pltpu.VMEM((len(pieces) * word_tiles, tile, rank), bf16),
        pltpu.SemaphoreType.DMA((len(pieces),)),
        pltpu.SemaphoreType.DMA((chunks,)),
    ]
    if cached:
        scratch.append(pltpu.VMEM((chunks, CHUNK * tile, rank), bf16))
    return pl.pallas_call(
        functools.partial(
            steps_kernel, shards=len(pieces), levels=len(terms), cached=cached
        ),
        in_specs=[scalars, scalars, whole, whole, whole, anywhere]
        + [anywhere] * len(pieces)
        + [whole] * len(terms),
        out_specs=[whole] * 4,
        out_shape=[vector, vector, vector, jax.ShapeDtypeStruct((devices, 1, rank), f32)],
        scratch_shapes=scratch,
        compiler_params=pltpu.CompilerParams(vmem_limit_bytes=VMEM_LIMIT),
        name="krylov",
    )(chosen, word_index, start, activity, subs, masks, *pieces, *terms)


def last_kernel(dots, start, first, second, third, solution_out, residual_out):
    line = dots[0]
    for k in range(1, dots.shape[0]):
        line = line + dots[k]
    rr, rq, qq, rz, qz = (line[:, k : k + 1] for k in range(5))
    step0 = rr / rq
    next_rr = rr - 2.0 * step0 * rq + step0 * step0 * qq
    grow = 1.0 + next_rr / rr
    slope = grow * (grow * rq - step0 * (rz + qq)) + step0 * step0 * qz
    step1 = next_rr / slope
    near, far = step0 + step1 * grow, step1 * step0
    solution_out[...] = start[...] + near * first[...] - far * second[...]
    residual_out[...] = first[...] - near * second[...] + far * third[...]


def last_step(dots, start, first, second, third):
    whole = pl.BlockSpec(memory_space=pltpu.VMEM)
    vector = jax.ShapeDtypeStruct(start.shape, f32)
    return pl.pallas_call(
        last_kernel,
        in_specs=[whole] * 5,
        out_specs=[whole] * 2,
        out_shape=[vector, vector],
        compiler_params=pltpu.CompilerParams(vmem_limit_bytes=VMEM_LIMIT),
        name="last_step",
    )(dots, start, first, second, third)


def ring_place(shard, chips):
    chip = shard // 2
    level, column = chip // 2, chip % 2
    return jnp.where(column == 0, level, chips - 1 - level)


def ring_round(up, down, held, step, shards):
    chips = shards // 2
    levels = chips // 2
    order = [2 * level for level in range(levels)] + [
        2 * level + 1 for level in reversed(range(levels))
    ]

    def shift(by):
        return [
            (2 * order[p] + core, 2 * order[(p + by) % chips] + core)
            for p in range(chips)
            for core in range(2)
        ]

    up = lax.ppermute(up, "loop", shift(1))
    held[chips - step] = up
    if step < chips - step:
        down = lax.ppermute(down, "loop", shift(-1))
        held[step] = down
    return up, down


def other_core(value, shards):
    return lax.ppermute(value, "loop", [(shard, shard ^ 1) for shard in range(shards)])


def on_device(
    factor_start,
    activity,
    word_factors,
    sub_factors,
    ratings,
    user_tile,
    word_tile,
    subreddit,
    counts,
    runs,
):
    own_rows, rank = factor_start.shape
    owners, shards = lax.axis_size("own"), lax.axis_size("loop")
    _, _, groups, slots, tile, _ = ratings.shape
    word_tiles = word_factors.shape[1]
    devices = shards * owners
    chips, levels = shards // 2, shards // 4
    me, owner = lax.axis_index("loop"), lax.axis_index("own")
    together = lax.optimization_barrier

    step = jnp.arange(groups, dtype=jnp.int32)
    level = (me // 4 + step % levels) % levels
    order = 4 * level + (me % 4) ^ (2 * ((step // levels) % 2) + step // (2 * levels))
    scalars = jnp.concatenate(
        [user_tile[0, 0], word_tile[0, 0], subreddit[0, 0], counts[0, 0][:, None], order[:, None]],
        axis=1,
    )

    mine = word_factors[0]
    inputs = (scalars, ratings[0, 0], runs[0, 0], mine, sub_factors)
    held = {0: mine}
    up, down = ring_round(mine, mine, held, 1, shards)
    (away,) = rhs_sums(*inputs, 1, None, owners, own_rows)
    up, down, away, scalars = together((up, down, away, scalars))

    up, down = ring_round(up, down, held, 2, shards)
    message = facts(scalars, runs[0, 0], sub_factors, owners).reshape(devices, 4 * slots, rank)
    received = lax.all_to_all(message, AXES, 0, 0, tiled=True)
    parts = rhs_sums(*inputs, 0, other_core(away, shards), owners, own_rows)
    up, down, parts = together((up, down, parts))

    up, down = ring_round(up, down, held, 3, shards)
    total = reduce_chip(parts, shards, owners)
    up, down, total = together((up, down, total))

    for step in range(4, chips // 2 + 1):
        up, down = ring_round(up, down, held, step, shards)
    terms = reduce_levels(total, shards)
    pieces = []
    for distance in range(chips):
        pieces += [held[distance], other_core(held[distance], shards)]

    got = received[:, 3 * slots, : 2 * slots].astype(jnp.int32)
    marks = (got[:, :slots] == owner * own_rows // tile + 1).astype(jnp.int32).reshape(-1)
    shard = jnp.arange(devices, dtype=jnp.int32)[:, None] // owners
    distance = (ring_place(shard, chips) - ring_place(me, chips)) % chips
    piece = 2 * distance + (shard + me) % 2
    word_index = (got[:, slots:] + word_tiles * piece).reshape(-1)

    chosen, subs, masks = build_masks(marks, received, own_rows)
    first, second, third, dots = krylov(
        chosen, word_index, factor_start, activity[:, None], subs, masks, pieces, terms, devices
    )
    everyone = lax.all_to_all(dots, AXES, 0, 0, tiled=True)
    return tuple(last_step(everyone, factor_start, first, second, third))


def solution(mesh):
    placed = (
        P(("loop", "own"), None),
        P(("loop", "own")),
        P("loop", None, None, None),
        P(),
        P("loop", "own", None, None, None, None),
        P("loop", "own", None, None),
        P("loop", "own", None, None),
        P("loop", "own", None, None),
        P("loop", "own", None),
        P("loop", "own", None, None, None, None),
    )
    return jax.shard_map(
        on_device,
        mesh=mesh,
        in_specs=placed,
        out_specs=(P(("loop", "own"), None), P(("loop", "own"), None)),
        check_vma=False,
    )
```

```python
import functools

import jax
import jax.numpy as jnp
from jax import lax
from jax.experimental import pallas as pl
from jax.experimental.pallas import tpu as pltpu
from jax.sharding import PartitionSpec as P

AXES = ("loop", "own")
CHUNK = 8
ridge = 0.05
VMEM_LIMIT = 60 * 2**20
f32 = jnp.float32
bf16 = jnp.bfloat16


def dot_nt(left, right):
    return lax.dot_general(left, right, (((1,), (1,)), ((), ())), preferred_element_type=f32)


def dot_nn(left, right):
    return jnp.dot(left, right, preferred_element_type=f32)


def mask_columns(first, length, tile):
    column = lax.broadcasted_iota(jnp.int32, (tile, first.shape[-1]), 0)
    inside = ((column - first) & (tile - 1)) < length
    return jnp.where(inside, 1.0, 0.0).astype(bf16)


def facts_kernel(user_tile, word_tile, subreddit, counts, runs, subs, out, table):
    groups, slots = runs.shape[0], runs.shape[1]
    owners, rank = out.shape[1], out.shape[3]
    table[...] = subs[...].astype(f32)
    lane = lax.broadcasted_iota(jnp.int32, (1, rank), 1)

    def body(group, carry):
        sub_rows, run_rows = [], []
        marks = jnp.zeros((1, rank), jnp.int32)
        live = counts[0, group]
        for s in range(slots):
            sub_rows.append(table[pl.ds(subreddit[s, group], 1), :])
            run_rows.append(runs[group, s])
            marks = jnp.where(lane == s, jnp.where(s < live, user_tile[s, group] + 1, 0), marks)
            marks = jnp.where(lane == slots + s, word_tile[s, group], marks)
        run_rows = jnp.concatenate(run_rows, axis=0).astype(f32).astype(out.dtype)
        rest = jnp.concatenate(
            sub_rows + [marks.astype(f32), jnp.zeros((slots - 1, rank), f32)], axis=0
        ).astype(out.dtype)
        for o in range(owners):
            out[group, o, : 2 * slots, :] = run_rows
            out[group, o, 2 * slots :, :] = rest
        return carry

    lax.fori_loop(0, groups, body, 0)


def facts(scalars, runs, subs, owners):
    groups, slots, _, _ = runs.shape
    rank = subs.shape[1]
    whole = pl.BlockSpec(memory_space=pltpu.VMEM)
    return pl.pallas_call(
        facts_kernel,
        in_specs=[pl.BlockSpec(memory_space=pltpu.SMEM)] * 4 + [whole, whole],
        out_specs=whole,
        out_shape=jax.ShapeDtypeStruct((groups, owners, 4 * slots, rank), bf16),
        scratch_shapes=[pltpu.VMEM(subs.shape, f32)],
        compiler_params=pltpu.CompilerParams(vmem_limit_bytes=VMEM_LIMIT),
        name="facts",
    )(*scalars, runs, subs)


def rhs_kernel(
    user_tile, word_tile, subreddit, counts, ratings_in, runs_in, words_in, subs_in, *refs,
    half, owners, own_rows,
):
    given, refs = (refs[0], refs[1:]) if half == 0 else (None, refs)
    outs, (ratings, runs, words, subs, table, sums, arrived, loaded) = refs[:-8], refs[-8:]
    steps, slots, tile = ratings.shape[0], ratings.shape[1], ratings.shape[2]
    levels = steps // 2

    place = lax.axis_index("loop")
    level, seat = lax.div(place, 4), lax.rem(place, 4)

    def group_at(step):
        there = lax.rem(seat + 2 * (step // levels), 4)
        if half:
            there = there + 1 - 2 * lax.rem(there, 2)
        return 4 * lax.rem(level + step % levels, levels) + there

    def load(step):
        group = group_at(step)
        return pltpu.make_async_copy(ratings_in.at[group], ratings.at[step], arrived.at[step])

    tables = [
        pltpu.make_async_copy(source, target, loaded.at[k])
        for k, (source, target) in enumerate(
            [(subs_in, subs), (runs_in, runs), (words_in, words)]
        )
    ]
    for copy in tables:
        copy.start()
    for step in range(steps):
        load(step).start()
    tables[0].wait()
    table[...] = subs[...].astype(f32)
    tables[1].wait()
    tables[2].wait()

    eye = (
        lax.broadcasted_iota(jnp.int32, (tile, tile), 0)
        == lax.broadcasted_iota(jnp.int32, (tile, tile), 1)
    ).astype(f32).astype(bf16)
    me = lax.axis_index("own")
    for step in range(steps):
        group = group_at(step)
        live = counts[0, group]
        columns = []
        for s in range(slots):
            pair = runs[group, s]
            columns.append(
                mask_columns(pair[0:1], jnp.where(s < live, pair[1:2], 0), tile)
            )
        seen = dot_nt(eye, jnp.concatenate(columns, axis=0)).astype(bf16)
        load(step).wait()
        sums[step % 2] = jnp.zeros(sums.shape[1:], f32)
        for s in range(slots):
            sub_row = table[pl.ds(subreddit[s, group], 1), :]
            product = (words[word_tile[s, group]].astype(f32) * sub_row).astype(bf16)
            weights = seen[:, s * tile : (s + 1) * tile] * ratings[step, s]
            rows = pl.ds(pl.multiple_of(user_tile[s, group] * tile, tile), tile)
            sums[step % 2, rows, :] += dot_nn(weights, product)
        for o in range(owners):
            owner = lax.rem(me + o, owners)
            rows = pl.ds(pl.multiple_of(owner * own_rows, own_rows), own_rows)
            value = sums[step % 2, rows, :]
            if half == 0:
                value = value + given[o, step // levels, step % levels].astype(f32)
                outs[2 * o + step // levels][step % levels] = value.astype(bf16)
            else:
                outs[0][o, step // levels, step % levels] = value.astype(bf16)


def rhs_sums(scalars, ratings, runs, words, subs, half, given, owners, own_rows):
    groups, slots, tile, _ = ratings.shape
    rank = words.shape[-1]
    steps, levels = groups // 2, groups // 4
    anywhere = pl.BlockSpec(memory_space=pl.ANY)
    whole = pl.BlockSpec(memory_space=pltpu.VMEM)
    part = (levels, own_rows, rank)
    shapes = [part] * (2 * owners) if half == 0 else [(owners, 2) + part]
    return pl.pallas_call(
        functools.partial(rhs_kernel, half=half, owners=owners, own_rows=own_rows),
        in_specs=[pl.BlockSpec(memory_space=pltpu.SMEM)] * 4
        + [anywhere] * 4
        + [whole] * (1 - half),
        out_specs=[whole] * len(shapes),
        out_shape=[jax.ShapeDtypeStruct(shape, bf16) for shape in shapes],
        scratch_shapes=[
            pltpu.VMEM((steps,) + ratings.shape[1:], bf16),
            pltpu.VMEM(runs.shape, jnp.int32),
            pltpu.VMEM(words.shape, bf16),
            pltpu.VMEM(subs.shape, bf16),
            pltpu.VMEM(subs.shape, f32),
            pltpu.VMEM((2, owners * own_rows, rank), f32),
            pltpu.SemaphoreType.DMA((steps,)),
            pltpu.SemaphoreType.DMA((3,)),
        ],
        compiler_params=pltpu.CompilerParams(vmem_limit_bytes=VMEM_LIMIT),
        cost_estimate=pl.CostEstimate(
            flops=8 * ratings.size * rank, bytes_accessed=8 * ratings.size, transcendentals=0
        ),
        name="rhs",
    )(*scalars, ratings, runs, words, subs, *([given] if half == 0 else []))


def reduce_chip(parts, shards, owners):
    total = [part.astype(f32) for part in parts[:1]]
    for o in range(owners):
        for column in range(2):
            if o or column:
                pairs = [
                    (shard * owners + k, (shard ^ 2 * column) * owners + (k + o) % owners)
                    for shard in range(shards)
                    for k in range(owners)
                ]
                total.append(lax.ppermute(parts[2 * o + column], AXES, pairs).astype(f32))
    return sum(total[1:], total[0]).astype(bf16)


def reduce_levels(total, shards):
    levels = shards // 4
    terms = [total[0]]
    for up in range(1, levels):
        shift = [(shard, (shard + 4 * up) % shards) for shard in range(shards)]
        terms.append(lax.ppermute(total[up], "loop", shift))
    return terms


def masks_kernel(
    received, chosen, places, subs, masks_out, runs, masks, lines, facts, sent, moved, *, word_tiles
):
    sources = received.shape[0]
    own_rows = masks.shape[1]
    tile = received.shape[2]
    blocks = subs.shape[0]
    slots = blocks // sources
    owners = lax.axis_size("own")
    chips = lax.axis_size("loop") // 2

    def unpack(src, carry):
        runs[pl.ds(pl.multiple_of(src * 2 * slots, 2 * slots), 2 * slots), :] = received[
            src, : 2 * slots, :
        ].astype(f32)
        rest = received[src, 2 * slots :, :].astype(f32)
        subs[pl.ds(pl.multiple_of(src * slots, slots), slots), :] = rest[:slots]
        lines[pl.ds(src, 1), :] = rest[slots : slots + 1].astype(jnp.int32)
        return carry

    lax.fori_loop(0, sources, unpack, 0, unroll=4)
    move = pltpu.make_async_copy(lines, facts, moved.at[0])
    move.start()
    move.wait()

    me = lax.axis_index("loop")
    wanted = lax.div(lax.axis_index("own") * own_rows, tile) + 1

    def ring_at(shard):
        level, column = lax.div(shard, 4), lax.rem(lax.div(shard, 2), 2)
        return jnp.where(column == 0, level, chips - 1 - level)

    def choose(src, n):
        shard = lax.div(src, owners)
        distance = lax.rem(ring_at(shard) - ring_at(me) + chips, chips)
        first = word_tiles * (2 * distance + lax.rem(shard + me, 2))
        for s in range(slots):
            chosen[n] = src * slots + s
            places[n] = first + facts[src, slots + s]
            n = n + jnp.where(facts[src, s] == wanted, 1, 0)
        return n

    used = lax.fori_loop(0, sources, choose, 0)
    chosen[blocks] = used
    chunks = lax.div(used + CHUNK - 1, CHUNK)

    offset = lax.rem(lax.axis_index("own") * own_rows, tile)
    pick = (
        lax.broadcasted_iota(jnp.int32, (own_rows, tile), 0) + offset
        == lax.broadcasted_iota(jnp.int32, (own_rows, tile), 1)
    ).astype(f32).astype(bf16)

    def send(chunk):
        return pltpu.make_async_copy(masks.at[chunk], masks_out.at[chunk], sent.at[chunk])

    def build(chunk, carry):
        parts = []
        for b in range(CHUNK):
            i = chunk * CHUNK + b
            j = jnp.where(i < used, chosen[jnp.minimum(i, blocks - 1)], 0)
            first = runs[pl.ds(2 * j, 1), :].astype(jnp.int32)
            length = runs[pl.ds(2 * j + 1, 1), :].astype(jnp.int32)
            length = jnp.where(i < used, length, 0)
            parts.append(mask_columns(first, length, tile))
        masks[chunk] = dot_nt(pick, jnp.concatenate(parts, axis=0)).astype(bf16)
        send(chunk).start()
        return carry

    def finish(chunk, carry):
        send(chunk).wait()
        return carry

    lax.fori_loop(0, chunks, build, 0)
    lax.fori_loop(0, chunks, finish, 0)


def build_masks(received, slots, word_tiles, own_rows):
    sources, _, tile = received.shape
    blocks = sources * slots
    rank = tile
    chunks = -(-blocks // CHUNK)
    whole = pl.BlockSpec(memory_space=pltpu.VMEM)
    scalars = pl.BlockSpec(memory_space=pltpu.SMEM)
    return pl.pallas_call(
        functools.partial(masks_kernel, word_tiles=word_tiles),
        in_specs=[whole],
        out_specs=[scalars, scalars, whole, pl.BlockSpec(memory_space=pl.ANY)],
        out_shape=[
            jax.ShapeDtypeStruct((blocks + 1,), jnp.int32),
            jax.ShapeDtypeStruct((blocks,), jnp.int32),
            jax.ShapeDtypeStruct((blocks, rank), f32),
            jax.ShapeDtypeStruct((chunks, own_rows, CHUNK * tile), bf16),
        ],
        scratch_shapes=[
            pltpu.VMEM((2 * blocks, tile), f32),
            pltpu.VMEM((chunks, own_rows, CHUNK * tile), bf16),
            pltpu.VMEM((sources, tile), jnp.int32),
            pltpu.SMEM((sources, tile), jnp.int32),
            pltpu.SemaphoreType.DMA((chunks,)),
            pltpu.SemaphoreType.DMA((1,)),
        ],
        compiler_params=pltpu.CompilerParams(vmem_limit_bytes=VMEM_LIMIT),
        cost_estimate=pl.CostEstimate(
            flops=40 * received.size * tile, bytes_accessed=40 * received.size, transcendentals=0
        ),
        name="masks",
    )(received)


def steps_kernel(chosen, places, start, activity, subs, masks_in, *refs, shards, levels, cached):
    own_rows, rank = start.shape
    blocks = subs.shape[0]
    pieces, refs = refs[:shards], refs[shards:]
    terms, refs = refs[:levels], refs[levels:]
    first_out, second_out, third_out, dots_out = refs[:4]
    masks, words, arrived, loaded = refs[4:8]
    products = refs[-1]
    word_tiles, tile, _ = pieces[0].shape
    used = chosen[blocks]
    chunks = lax.div(used + CHUNK - 1, CHUNK)

    copies = [
        pltpu.make_async_copy(
            piece, words.at[k * word_tiles : (k + 1) * word_tiles], arrived.at[k]
        )
        for k, piece in enumerate(pieces)
    ]
    for copy in copies:
        copy.start()

    def load(chunk):
        return pltpu.make_async_copy(masks_in.at[chunk], masks.at[chunk], loaded.at[chunk])

    def begin(chunk, carry):
        load(chunk).start()
        return carry

    lax.fori_loop(0, chunks, begin, 0)

    def product(i):
        i = jnp.minimum(i, used - 1)
        return (words[places[i]].astype(f32) * subs[pl.ds(chosen[i], 1), :]).astype(bf16)

    def build(chunk, carry):
        load(chunk).wait()
        if cached:
            for b in range(CHUNK):
                products[chunk, b * tile : (b + 1) * tile, :] = product(chunk * CHUNK + b)
        return carry

    for copy in copies:
        copy.wait()
    lax.fori_loop(0, chunks, build, 0)

    def gram(vector):
        rounded = vector.astype(bf16)

        def body(chunk, total):
            if cached:
                block = products[chunk]
            else:
                block = jnp.concatenate(
                    [product(chunk * CHUNK + b) for b in range(CHUNK)], axis=0
                )
            weights = dot_nt(rounded, block).astype(bf16) * masks[chunk]
            return total + dot_nn(weights, block)

        return lax.fori_loop(0, chunks, body, jnp.zeros((own_rows, rank), f32))

    def over_row(a, b):
        return jnp.sum(a * b, axis=1, keepdims=True)

    scale = jnp.broadcast_to(activity[...], (rank, own_rows)).T
    rhs = terms[0][...].astype(f32)
    for term in terms[1:]:
        rhs = rhs + term[...].astype(f32)
    first = scale * (rhs - gram(start[...])) - ridge * start[...]
    second = scale * gram(first) + ridge * first
    norms, overlaps = over_row(first, first), over_row(first, second)
    share = jnp.where(norms > 0.0, overlaps / jnp.where(norms > 0.0, norms, 1.0), 0.0)
    rest = second - share * first
    third = scale * gram(rest) + ridge * rest + share * second
    first_out[...] = first
    second_out[...] = second
    third_out[...] = third
    rows = [norms, overlaps, over_row(second, second), over_row(first, third), over_row(second, third)]
    lane = lax.broadcasted_iota(jnp.int32, (1, rank), 1)
    line = jnp.zeros((1, rank), f32)
    for k, value in enumerate(rows):
        line = line + jnp.where(lane == k, jnp.sum(value, axis=0, keepdims=True), 0.0)
    dots_out[...] = jnp.broadcast_to(line[None], dots_out.shape)


def krylov(chosen, places, start, activity, subs, masks, pieces, terms, devices):
    own_rows, rank = start.shape
    blocks = subs.shape[0]
    word_tiles, tile, _ = pieces[0].shape
    chunks = masks.shape[0]
    cached = blocks * tile * rank * 2 <= 16 * 2**20
    whole = pl.BlockSpec(memory_space=pltpu.VMEM)
    scalars = pl.BlockSpec(memory_space=pltpu.SMEM)
    anywhere = pl.BlockSpec(memory_space=pl.ANY)
    vector = jax.ShapeDtypeStruct((own_rows, rank), f32)
    scratch = [
        pltpu.VMEM(masks.shape, bf16),
        pltpu.VMEM((len(pieces) * word_tiles, tile, rank), bf16),
        pltpu.SemaphoreType.DMA((len(pieces),)),
        pltpu.SemaphoreType.DMA((chunks,)),
    ]
    if cached:
        scratch.append(pltpu.VMEM((chunks, CHUNK * tile, rank), bf16))
    return pl.pallas_call(
        functools.partial(
            steps_kernel, shards=len(pieces), levels=len(terms), cached=cached
        ),
        in_specs=[scalars, scalars, whole, whole, whole, anywhere]
        + [anywhere] * len(pieces)
        + [whole] * len(terms),
        out_specs=[whole] * 4,
        out_shape=[vector, vector, vector, jax.ShapeDtypeStruct((devices, 1, rank), f32)],
        scratch_shapes=scratch,
        compiler_params=pltpu.CompilerParams(vmem_limit_bytes=VMEM_LIMIT),
        name="krylov",
    )(chosen, places, start, activity, subs, masks, *pieces, *terms)


def last_kernel(dots, start, first, second, third, solution_out, residual_out):
    line = dots[0]
    for k in range(1, dots.shape[0]):
        line = line + dots[k]
    rr, rq, qq, rz, qz = (line[:, k : k + 1] for k in range(5))
    step0 = rr / rq
    next_rr = rr - 2.0 * step0 * rq + step0 * step0 * qq
    grow = 1.0 + next_rr / rr
    slope = grow * (grow * rq - step0 * (rz + qq)) + step0 * step0 * qz
    step1 = next_rr / slope
    near, far = step0 + step1 * grow, step1 * step0
    solution_out[...] = start[...] + near * first[...] - far * second[...]
    residual_out[...] = first[...] - near * second[...] + far * third[...]


def last_step(dots, start, first, second, third):
    whole = pl.BlockSpec(memory_space=pltpu.VMEM)
    vector = jax.ShapeDtypeStruct(start.shape, f32)
    return pl.pallas_call(
        last_kernel,
        in_specs=[whole] * 5,
        out_specs=[whole] * 2,
        out_shape=[vector, vector],
        compiler_params=pltpu.CompilerParams(vmem_limit_bytes=VMEM_LIMIT),
        name="last_step",
    )(dots, start, first, second, third)


def ring_round(up, down, held, step, shards):
    chips = shards // 2
    levels = chips // 2
    order = [2 * level for level in range(levels)] + [
        2 * level + 1 for level in reversed(range(levels))
    ]

    def shift(by):
        return [
            (2 * order[p] + core, 2 * order[(p + by) % chips] + core)
            for p in range(chips)
            for core in range(2)
        ]

    up = lax.ppermute(up, "loop", shift(1))
    held[chips - step] = up
    if step < chips - step:
        down = lax.ppermute(down, "loop", shift(-1))
        held[step] = down
    return up, down


def other_core(value, shards):
    return lax.ppermute(value, "loop", [(shard, shard ^ 1) for shard in range(shards)])


def on_device(
    factor_start,
    activity,
    word_factors,
    sub_factors,
    ratings,
    user_tile,
    word_tile,
    subreddit,
    counts,
    runs,
):
    own_rows, rank = factor_start.shape
    owners, shards = lax.axis_size("own"), lax.axis_size("loop")
    slots = ratings.shape[3]
    word_tiles = word_factors.shape[1]
    devices = shards * owners
    chips = shards // 2
    together = lax.optimization_barrier

    scalars = (user_tile[0, 0].T, word_tile[0, 0].T, subreddit[0, 0].T, counts[0])
    mine = word_factors[0]
    held = {0: mine}

    message = facts(scalars, runs[0, 0], sub_factors, owners).reshape(devices, 4 * slots, rank)
    received = lax.all_to_all(message, AXES, 0, 0, tiled=True)
    up, down = ring_round(mine, mine, held, 1, shards)
    up, down, _, *inputs = together(
        (up, down, message, ratings[0, 0], runs[0, 0], mine, sub_factors)
    )

    up, down = ring_round(up, down, held, 2, shards)
    (away,) = rhs_sums(scalars, *inputs, 1, None, owners, own_rows)
    up, down, away, received = together((up, down, away, received))

    up, down = ring_round(up, down, held, 3, shards)
    parts = rhs_sums(scalars, *inputs, 0, other_core(away, shards), owners, own_rows)
    up, down, parts = together((up, down, parts))

    for step in range(4, chips // 2 + 1):
        up, down = ring_round(up, down, held, step, shards)
    total = reduce_chip(parts, shards, owners)
    held[chips // 2], total, received = together((held[chips // 2], total, received))

    terms = reduce_levels(total, shards)
    pieces = []
    for distance in range(chips):
        pieces += [held[distance], other_core(held[distance], shards)]
    chosen, places, subs, masks = build_masks(received, slots, word_tiles, own_rows)
    first, second, third, dots = krylov(
        chosen, places, factor_start, activity[None], subs, masks, pieces, terms, devices
    )
    everyone = lax.all_to_all(dots, AXES, 0, 0, tiled=True)
    return tuple(last_step(everyone, factor_start, first, second, third))


def solution(mesh):
    placed = (
        P(("loop", "own"), None),
        P(("loop", "own")),
        P("loop", None, None, None),
        P(),
        P("loop", "own", None, None, None, None),
        P("loop", "own", None, None),
        P("loop", "own", None, None),
        P("loop", "own", None, None),
        P("loop", "own", None),
        P("loop", "own", None, None, None, None),
    )
    return jax.shard_map(
        on_device,
        mesh=mesh,
        in_specs=placed,
        out_specs=(P(("loop", "own"), None), P(("loop", "own"), None)),
        check_vma=False,
    )
```

```python
import functools

import jax
import jax.numpy as jnp
from jax import lax
from jax.experimental import pallas as pl
from jax.experimental.pallas import tpu as pltpu
from jax.sharding import PartitionSpec as P

AXES = ("loop", "own")
CHUNK = 16
ridge = 0.05
VMEM_LIMIT = 60 * 2**20
f32 = jnp.float32
bf16 = jnp.bfloat16


def dot_nt(left, right):
    return lax.dot_general(left, right, (((1,), (1,)), ((), ())), preferred_element_type=f32)


def dot_nn(left, right):
    return jnp.dot(left, right, preferred_element_type=f32)


def mask_columns(first, length, tile):
    column = lax.broadcasted_iota(jnp.int32, (tile, first.shape[-1]), 0)
    inside = ((column - first) & (tile - 1)) < length
    return jnp.where(inside, 1.0, 0.0).astype(bf16)


def facts_kernel(user_tile, word_tile, subreddit, counts, runs, subs, out, table):
    groups, slots = runs.shape[0], runs.shape[1]
    owners, rank = out.shape[1], out.shape[3]
    table[...] = subs[...].astype(f32)
    lane = lax.broadcasted_iota(jnp.int32, (1, rank), 1)

    def body(group, carry):
        sub_rows, run_rows = [], []
        marks = jnp.zeros((1, rank), jnp.int32)
        live = counts[0, group]
        for s in range(slots):
            sub_rows.append(table[pl.ds(subreddit[s, group], 1), :])
            run_rows.append(runs[group, s])
            marks = jnp.where(lane == s, jnp.where(s < live, user_tile[s, group] + 1, 0), marks)
            marks = jnp.where(lane == slots + s, word_tile[s, group], marks)
        run_rows = jnp.concatenate(run_rows, axis=0).astype(f32).astype(out.dtype)
        rest = jnp.concatenate(
            sub_rows + [marks.astype(f32), jnp.zeros((slots - 1, rank), f32)], axis=0
        ).astype(out.dtype)
        for o in range(owners):
            out[group, o, : 2 * slots, :] = run_rows
            out[group, o, 2 * slots :, :] = rest
        return carry

    lax.fori_loop(0, groups, body, 0)


def facts(scalars, runs, subs, owners):
    groups, slots, _, _ = runs.shape
    rank = subs.shape[1]
    whole = pl.BlockSpec(memory_space=pltpu.VMEM)
    return pl.pallas_call(
        facts_kernel,
        in_specs=[pl.BlockSpec(memory_space=pltpu.SMEM)] * 4 + [whole, whole],
        out_specs=whole,
        out_shape=jax.ShapeDtypeStruct((groups, owners, 4 * slots, rank), bf16),
        scratch_shapes=[pltpu.VMEM(subs.shape, f32)],
        compiler_params=pltpu.CompilerParams(vmem_limit_bytes=VMEM_LIMIT),
        name="facts",
    )(*scalars, runs, subs)


def rhs_kernel(
    user_tile, word_tile, subreddit, counts, ratings_in, runs_in, words_in, subs_in, *refs,
    half, owners, own_rows,
):
    given, refs = (refs[0], refs[1:]) if half == 0 else (None, refs)
    outs, (ratings, runs, words, subs, table, sums, arrived, loaded) = refs[:-8], refs[-8:]
    steps, slots, tile = ratings.shape[0], ratings.shape[1], ratings.shape[2]
    levels = steps // 2

    place = lax.axis_index("loop")
    level, seat = lax.div(place, 4), lax.rem(place, 4)

    def group_at(step):
        there = lax.rem(seat + 2 * (step // levels), 4)
        if half:
            there = there + 1 - 2 * lax.rem(there, 2)
        return 4 * lax.rem(level + step % levels, levels) + there

    def load(step):
        group = group_at(step)
        return pltpu.make_async_copy(ratings_in.at[group], ratings.at[step], arrived.at[step])

    tables = [
        pltpu.make_async_copy(source, target, loaded.at[k])
        for k, (source, target) in enumerate(
            [(subs_in, subs), (runs_in, runs), (words_in, words)]
        )
    ]
    for copy in tables:
        copy.start()
    for step in range(steps):
        load(step).start()
    tables[0].wait()
    table[...] = subs[...].astype(f32)
    tables[1].wait()
    tables[2].wait()

    eye = (
        lax.broadcasted_iota(jnp.int32, (tile, tile), 0)
        == lax.broadcasted_iota(jnp.int32, (tile, tile), 1)
    ).astype(f32).astype(bf16)
    me = lax.axis_index("own")
    for step in range(steps):
        group = group_at(step)
        live = counts[0, group]
        columns = []
        for s in range(slots):
            pair = runs[group, s]
            columns.append(
                mask_columns(pair[0:1], jnp.where(s < live, pair[1:2], 0), tile)
            )
        seen = dot_nt(eye, jnp.concatenate(columns, axis=0)).astype(bf16)
        load(step).wait()
        sums[step % 2] = jnp.zeros(sums.shape[1:], f32)
        for s in range(slots):
            sub_row = table[pl.ds(subreddit[s, group], 1), :]
            product = (words[word_tile[s, group]].astype(f32) * sub_row).astype(bf16)
            weights = seen[:, s * tile : (s + 1) * tile] * ratings[step, s]
            rows = pl.ds(pl.multiple_of(user_tile[s, group] * tile, tile), tile)
            sums[step % 2, rows, :] += dot_nn(weights, product)
        for o in range(owners):
            owner = lax.rem(me + o, owners)
            rows = pl.ds(pl.multiple_of(owner * own_rows, own_rows), own_rows)
            value = sums[step % 2, rows, :]
            if half == 0:
                value = value + given[o, step // levels, step % levels].astype(f32)
                outs[2 * o + step // levels][step % levels] = value.astype(bf16)
            else:
                outs[0][o, step // levels, step % levels] = value.astype(bf16)


def rhs_sums(scalars, ratings, runs, words, subs, half, given, owners, own_rows):
    groups, slots, tile, _ = ratings.shape
    rank = words.shape[-1]
    steps, levels = groups // 2, groups // 4
    anywhere = pl.BlockSpec(memory_space=pl.ANY)
    whole = pl.BlockSpec(memory_space=pltpu.VMEM)
    part = (levels, own_rows, rank)
    shapes = [part] * (2 * owners) if half == 0 else [(owners, 2) + part]
    return pl.pallas_call(
        functools.partial(rhs_kernel, half=half, owners=owners, own_rows=own_rows),
        in_specs=[pl.BlockSpec(memory_space=pltpu.SMEM)] * 4
        + [anywhere] * 4
        + [whole] * (1 - half),
        out_specs=[whole] * len(shapes),
        out_shape=[jax.ShapeDtypeStruct(shape, bf16) for shape in shapes],
        scratch_shapes=[
            pltpu.VMEM((steps,) + ratings.shape[1:], bf16),
            pltpu.VMEM(runs.shape, jnp.int32),
            pltpu.VMEM(words.shape, bf16),
            pltpu.VMEM(subs.shape, bf16),
            pltpu.VMEM(subs.shape, f32),
            pltpu.VMEM((2, owners * own_rows, rank), f32),
            pltpu.SemaphoreType.DMA((steps,)),
            pltpu.SemaphoreType.DMA((3,)),
        ],
        compiler_params=pltpu.CompilerParams(vmem_limit_bytes=VMEM_LIMIT),
        cost_estimate=pl.CostEstimate(
            flops=8 * ratings.size * rank, bytes_accessed=8 * ratings.size, transcendentals=0
        ),
        name="rhs",
    )(*scalars, ratings, runs, words, subs, *([given] if half == 0 else []))


def reduce_chip(parts, shards, owners):
    total = [part.astype(f32) for part in parts[:1]]
    for o in range(owners):
        for column in range(2):
            if o or column:
                pairs = [
                    (shard * owners + k, (shard ^ 2 * column) * owners + (k + o) % owners)
                    for shard in range(shards)
                    for k in range(owners)
                ]
                total.append(lax.ppermute(parts[2 * o + column], AXES, pairs).astype(f32))
    return sum(total[1:], total[0]).astype(bf16)


def reduce_levels(total, shards):
    levels = shards // 4
    terms = [total[0]]
    for up in range(1, levels):
        shift = [(shard, (shard + 4 * up) % shards) for shard in range(shards)]
        terms.append(lax.ppermute(total[up], "loop", shift))
    return terms


def masks_kernel(
    received, chosen, places, subs, masks_out, runs, masks, lines, facts, sent, moved, *, word_tiles
):
    sources = received.shape[0]
    own_rows = masks.shape[1]
    tile = received.shape[2]
    blocks = subs.shape[0]
    slots = blocks // sources
    owners = lax.axis_size("own")
    chips = lax.axis_size("loop") // 2

    def unpack(src, carry):
        runs[pl.ds(pl.multiple_of(src * 2 * slots, 2 * slots), 2 * slots), :] = received[
            src, : 2 * slots, :
        ].astype(f32)
        rest = received[src, 2 * slots :, :].astype(f32)
        subs[pl.ds(pl.multiple_of(src * slots, slots), slots), :] = rest[:slots]
        lines[pl.ds(src, 1), :] = rest[slots : slots + 1].astype(jnp.int32)
        return carry

    lax.fori_loop(0, sources, unpack, 0, unroll=4)
    move = pltpu.make_async_copy(lines, facts, moved.at[0])
    move.start()
    move.wait()

    me = lax.axis_index("loop")
    wanted = lax.div(lax.axis_index("own") * own_rows, tile) + 1

    def ring_at(shard):
        level, column = lax.div(shard, 4), lax.rem(lax.div(shard, 2), 2)
        return jnp.where(column == 0, level, chips - 1 - level)

    def choose(src, n):
        shard = lax.div(src, owners)
        distance = lax.rem(ring_at(shard) - ring_at(me) + chips, chips)
        first = word_tiles * (2 * distance + lax.rem(shard + me, 2))
        for s in range(slots):
            chosen[n] = src * slots + s
            places[n] = first + facts[src, slots + s]
            n = n + jnp.where(facts[src, s] == wanted, 1, 0)
        return n

    used = lax.fori_loop(0, sources, choose, 0)
    chosen[blocks] = used
    chunks = lax.div(used + CHUNK - 1, CHUNK)

    offset = lax.rem(lax.axis_index("own") * own_rows, tile)
    pick = (
        lax.broadcasted_iota(jnp.int32, (own_rows, tile), 0) + offset
        == lax.broadcasted_iota(jnp.int32, (own_rows, tile), 1)
    ).astype(f32).astype(bf16)

    def send(chunk):
        return pltpu.make_async_copy(masks.at[chunk], masks_out.at[chunk], sent.at[chunk])

    def build(chunk, carry):
        parts = []
        for b in range(CHUNK):
            i = chunk * CHUNK + b
            j = jnp.where(i < used, chosen[jnp.minimum(i, blocks - 1)], 0)
            first = runs[pl.ds(2 * j, 1), :].astype(jnp.int32)
            length = runs[pl.ds(2 * j + 1, 1), :].astype(jnp.int32)
            length = jnp.where(i < used, length, 0)
            parts.append(mask_columns(first, length, tile))
        masks[chunk] = dot_nt(pick, jnp.concatenate(parts, axis=0)).astype(bf16)
        send(chunk).start()
        return carry

    def finish(chunk, carry):
        send(chunk).wait()
        return carry

    lax.fori_loop(0, chunks, build, 0)
    lax.fori_loop(0, chunks, finish, 0)


def build_masks(received, slots, word_tiles, own_rows):
    sources, _, tile = received.shape
    blocks = sources * slots
    rank = tile
    chunks = -(-blocks // CHUNK)
    whole = pl.BlockSpec(memory_space=pltpu.VMEM)
    scalars = pl.BlockSpec(memory_space=pltpu.SMEM)
    return pl.pallas_call(
        functools.partial(masks_kernel, word_tiles=word_tiles),
        in_specs=[whole],
        out_specs=[scalars, scalars, whole, pl.BlockSpec(memory_space=pl.ANY)],
        out_shape=[
            jax.ShapeDtypeStruct((blocks + 1,), jnp.int32),
            jax.ShapeDtypeStruct((blocks,), jnp.int32),
            jax.ShapeDtypeStruct((blocks, rank), f32),
            jax.ShapeDtypeStruct((chunks, own_rows, CHUNK * tile), bf16),
        ],
        scratch_shapes=[
            pltpu.VMEM((2 * blocks, tile), f32),
            pltpu.VMEM((chunks, own_rows, CHUNK * tile), bf16),
            pltpu.VMEM((sources, tile), jnp.int32),
            pltpu.SMEM((sources, tile), jnp.int32),
            pltpu.SemaphoreType.DMA((chunks,)),
            pltpu.SemaphoreType.DMA((1,)),
        ],
        compiler_params=pltpu.CompilerParams(vmem_limit_bytes=VMEM_LIMIT),
        cost_estimate=pl.CostEstimate(
            flops=40 * received.size * tile, bytes_accessed=40 * received.size, transcendentals=0
        ),
        name="masks",
    )(received)


def steps_kernel(chosen, places, start, activity, subs, masks_in, *refs, shards, levels, cached):
    own_rows, rank = start.shape
    blocks = subs.shape[0]
    pieces, refs = refs[:shards], refs[shards:]
    terms, refs = refs[:levels], refs[levels:]
    first_out, second_out, third_out, dots_out = refs[:4]
    masks, words, arrived, loaded = refs[4:8]
    products = refs[-1]
    word_tiles, tile, _ = pieces[0].shape
    used = chosen[blocks]
    chunks = lax.div(used + CHUNK - 1, CHUNK)

    copies = [
        pltpu.make_async_copy(
            piece, words.at[k * word_tiles : (k + 1) * word_tiles], arrived.at[k]
        )
        for k, piece in enumerate(pieces)
    ]
    for copy in copies:
        copy.start()

    def load(chunk):
        return pltpu.make_async_copy(masks_in.at[chunk], masks.at[chunk], loaded.at[chunk])

    def begin(chunk, carry):
        load(chunk).start()
        return carry

    lax.fori_loop(0, chunks, begin, 0)

    def product(i):
        i = jnp.minimum(i, used - 1)
        return (words[places[i]].astype(f32) * subs[pl.ds(chosen[i], 1), :]).astype(bf16)

    for copy in copies:
        copy.wait()

    def gram(vector, build=False):
        rounded = vector.astype(bf16)

        def body(chunk, total):
            if build:
                load(chunk).wait()
            if cached and not build:
                block = products[chunk]
            else:
                block = jnp.concatenate(
                    [product(chunk * CHUNK + b) for b in range(CHUNK)], axis=0
                )
                if cached:
                    products[chunk] = block
            weights = dot_nt(rounded, block).astype(bf16) * masks[chunk]
            return total + dot_nn(weights, block)

        return lax.fori_loop(0, chunks, body, jnp.zeros((own_rows, rank), f32))

    def over_row(a, b):
        return jnp.sum(a * b, axis=1, keepdims=True)

    scale = jnp.broadcast_to(activity[...], (rank, own_rows)).T
    rhs = terms[0][...].astype(f32)
    for term in terms[1:]:
        rhs = rhs + term[...].astype(f32)
    first = scale * (rhs - gram(start[...], build=True)) - ridge * start[...]
    second = scale * gram(first) + ridge * first
    norms, overlaps = over_row(first, first), over_row(first, second)
    share = jnp.where(norms > 0.0, overlaps / jnp.where(norms > 0.0, norms, 1.0), 0.0)
    rest = second - share * first
    third = scale * gram(rest) + ridge * rest + share * second
    first_out[...] = first
    second_out[...] = second
    third_out[...] = third
    rows = [norms, overlaps, over_row(second, second), over_row(first, third), over_row(second, third)]
    lane = lax.broadcasted_iota(jnp.int32, (1, rank), 1)
    line = jnp.zeros((1, rank), f32)
    for k, value in enumerate(rows):
        line = line + jnp.where(lane == k, jnp.sum(value, axis=0, keepdims=True), 0.0)
    dots_out[...] = jnp.broadcast_to(line[None], dots_out.shape)


def krylov(chosen, places, start, activity, subs, masks, pieces, terms, devices):
    own_rows, rank = start.shape
    blocks = subs.shape[0]
    word_tiles, tile, _ = pieces[0].shape
    chunks = masks.shape[0]
    cached = blocks * tile * rank * 2 <= 16 * 2**20
    whole = pl.BlockSpec(memory_space=pltpu.VMEM)
    scalars = pl.BlockSpec(memory_space=pltpu.SMEM)
    anywhere = pl.BlockSpec(memory_space=pl.ANY)
    vector = jax.ShapeDtypeStruct((own_rows, rank), f32)
    scratch = [
        pltpu.VMEM(masks.shape, bf16),
        pltpu.VMEM((len(pieces) * word_tiles, tile, rank), bf16),
        pltpu.SemaphoreType.DMA((len(pieces),)),
        pltpu.SemaphoreType.DMA((chunks,)),
    ]
    if cached:
        scratch.append(pltpu.VMEM((chunks, CHUNK * tile, rank), bf16))
    return pl.pallas_call(
        functools.partial(
            steps_kernel, shards=len(pieces), levels=len(terms), cached=cached
        ),
        in_specs=[scalars, scalars, whole, whole, whole, anywhere]
        + [anywhere] * len(pieces)
        + [whole] * len(terms),
        out_specs=[whole] * 4,
        out_shape=[vector, vector, vector, jax.ShapeDtypeStruct((devices, 1, rank), f32)],
        scratch_shapes=scratch,
        compiler_params=pltpu.CompilerParams(vmem_limit_bytes=VMEM_LIMIT),
        name="krylov",
    )(chosen, places, start, activity, subs, masks, *pieces, *terms)


def last_kernel(dots, start, first, second, third, solution_out, residual_out):
    line = dots[0]
    for k in range(1, dots.shape[0]):
        line = line + dots[k]
    rr, rq, qq, rz, qz = (line[:, k : k + 1] for k in range(5))
    step0 = rr / rq
    next_rr = rr - 2.0 * step0 * rq + step0 * step0 * qq
    grow = 1.0 + next_rr / rr
    slope = grow * (grow * rq - step0 * (rz + qq)) + step0 * step0 * qz
    step1 = next_rr / slope
    near, far = step0 + step1 * grow, step1 * step0
    solution_out[...] = start[...] + near * first[...] - far * second[...]
    residual_out[...] = first[...] - near * second[...] + far * third[...]


def last_step(dots, start, first, second, third):
    whole = pl.BlockSpec(memory_space=pltpu.VMEM)
    vector = jax.ShapeDtypeStruct(start.shape, f32)
    return pl.pallas_call(
        last_kernel,
        in_specs=[whole] * 5,
        out_specs=[whole] * 2,
        out_shape=[vector, vector],
        compiler_params=pltpu.CompilerParams(vmem_limit_bytes=VMEM_LIMIT),
        name="last_step",
    )(dots, start, first, second, third)


def ring_round(up, down, held, step, shards):
    chips = shards // 2
    levels = chips // 2
    order = [2 * level for level in range(levels)] + [
        2 * level + 1 for level in reversed(range(levels))
    ]

    def shift(by):
        return [
            (2 * order[p] + core, 2 * order[(p + by) % chips] + core)
            for p in range(chips)
            for core in range(2)
        ]

    up = lax.ppermute(up, "loop", shift(1))
    held[chips - step] = up
    if step < chips - step:
        down = lax.ppermute(down, "loop", shift(-1))
        held[step] = down
    return up, down


def other_core(value, shards):
    return lax.ppermute(value, "loop", [(shard, shard ^ 1) for shard in range(shards)])


def on_device(
    factor_start,
    activity,
    word_factors,
    sub_factors,
    ratings,
    user_tile,
    word_tile,
    subreddit,
    counts,
    runs,
):
    own_rows, rank = factor_start.shape
    owners, shards = lax.axis_size("own"), lax.axis_size("loop")
    slots = ratings.shape[3]
    word_tiles = word_factors.shape[1]
    devices = shards * owners
    chips = shards // 2
    together = lax.optimization_barrier

    scalars = (user_tile[0, 0].T, word_tile[0, 0].T, subreddit[0, 0].T, counts[0])
    mine = word_factors[0]
    held = {0: mine}

    message = facts(scalars, runs[0, 0], sub_factors, owners).reshape(devices, 4 * slots, rank)
    received = lax.all_to_all(message, AXES, 0, 0, tiled=True)
    up, down = ring_round(mine, mine, held, 1, shards)
    up, down, _, *inputs = together(
        (up, down, message, ratings[0, 0], runs[0, 0], mine, sub_factors)
    )

    up, down = ring_round(up, down, held, 2, shards)
    (away,) = rhs_sums(scalars, *inputs, 1, None, owners, own_rows)
    up, down, away, received = together((up, down, away, received))

    up, down = ring_round(up, down, held, 3, shards)
    parts = rhs_sums(scalars, *inputs, 0, other_core(away, shards), owners, own_rows)
    up, down, parts = together((up, down, parts))

    for step in range(4, chips // 2 + 1):
        up, down = ring_round(up, down, held, step, shards)
    total = reduce_chip(parts, shards, owners)
    lists = build_masks(received, slots, word_tiles, own_rows)
    held[chips // 2], total, *lists = together((held[chips // 2], total, *lists))
    chosen, places, subs, masks = lists

    terms = reduce_levels(total, shards)
    pieces = []
    for distance in range(chips):
        pieces += [held[distance], other_core(held[distance], shards)]
    first, second, third, dots = krylov(
        chosen, places, factor_start, activity[None], subs, masks, pieces, terms, devices
    )
    everyone = lax.all_to_all(dots, AXES, 0, 0, tiled=True)
    return tuple(last_step(everyone, factor_start, first, second, third))


def solution(mesh):
    placed = (
        P(("loop", "own"), None),
        P(("loop", "own")),
        P("loop", None, None, None),
        P(),
        P("loop", "own", None, None, None, None),
        P("loop", "own", None, None),
        P("loop", "own", None, None),
        P("loop", "own", None, None),
        P("loop", "own", None),
        P("loop", "own", None, None, None, None),
    )
    return jax.shard_map(
        on_device,
        mesh=mesh,
        in_specs=placed,
        out_specs=(P(("loop", "own"), None), P(("loop", "own"), None)),
        check_vma=False,
    )
```

```python
import functools

import jax
import jax.numpy as jnp
from jax import lax
from jax.experimental import pallas as pl
from jax.experimental.pallas import tpu as pltpu
from jax.sharding import PartitionSpec as P

AXES = ("loop", "own")
CHUNK = 16
FACT_ROWS = 16
ridge = 0.05
VMEM_LIMIT = 60 * 2**20
f32 = jnp.float32
bf16 = jnp.bfloat16


def dot_nt(left, right):
    return lax.dot_general(left, right, (((1,), (1,)), ((), ())), preferred_element_type=f32)


def dot_nn(left, right):
    return jnp.dot(left, right, preferred_element_type=f32)


def mask_columns(first, length, tile):
    column = lax.broadcasted_iota(jnp.int32, (tile, first.shape[-1]), 0)
    inside = ((column - first) & (tile - 1)) < length
    return jnp.where(inside, 1.0, 0.0).astype(bf16)


def fact_line(user_tile, word_tile, subreddit, live, group, slots, rank):
    lane = lax.broadcasted_iota(jnp.int32, (1, rank), 1)
    line = jnp.zeros((1, rank), jnp.int32)
    for s in range(slots):
        sub = subreddit[s, group]
        user = jnp.where(s < live, user_tile[s, group] + 1, 0)
        values = (user, word_tile[s, group], lax.div(sub, 128), lax.rem(sub, 128))
        for k, value in enumerate(values):
            line = jnp.where(lane == k * slots + s, value, line)
    return line.astype(f32)


def rhs_kernel(
    user_tile, word_tile, subreddit, counts, ratings_in, runs_in, words_in, subs_in, *refs,
    half, owners, own_rows,
):
    if half == 0:
        given_in, refs, given = refs[0], refs[1:-1], refs[-1]
    outs, (ratings, runs, words, subs, table, sums, arrived, loaded) = refs[:-8], refs[-8:]
    steps, slots, tile = ratings.shape[0], ratings.shape[1], ratings.shape[2]
    rank = words.shape[-1]
    levels = steps // 2

    place = lax.axis_index("loop")
    level, seat = lax.div(place, 4), lax.rem(place, 4)

    def group_at(step):
        there = lax.rem(seat + 2 * (step // levels), 4)
        if half:
            there = there + 1 - 2 * lax.rem(there, 2)
        return 4 * lax.rem(level + step % levels, levels) + there

    def load(step):
        group = group_at(step)
        return pltpu.make_async_copy(ratings_in.at[group], ratings.at[step], arrived.at[step])

    tables = [
        pltpu.make_async_copy(source, target, loaded.at[k])
        for k, (source, target) in enumerate(
            [(subs_in, subs), (runs_in, runs), (words_in, words)]
        )
    ]
    for copy in tables:
        copy.start()
    for step in range(steps):
        load(step).start()
    if half == 0:
        gift = pltpu.make_async_copy(given_in, given, loaded.at[3])
        gift.start()
    tables[0].wait()
    table[...] = subs[...].astype(f32)
    tables[1].wait()
    tables[2].wait()

    if half == 0:
        gift.wait()
    eye = (
        lax.broadcasted_iota(jnp.int32, (tile, tile), 0)
        == lax.broadcasted_iota(jnp.int32, (tile, tile), 1)
    ).astype(f32).astype(bf16)
    me = lax.axis_index("own")
    for step in range(steps):
        group = group_at(step)
        live = counts[0, group]
        columns = []
        for s in range(slots):
            pair = runs[group, s]
            columns.append(
                mask_columns(pair[0:1], jnp.where(s < live, pair[1:2], 0), tile)
            )
        seen = dot_nt(eye, jnp.concatenate(columns, axis=0)).astype(bf16)
        load(step).wait()
        sums[step % 2] = jnp.zeros(sums.shape[1:], f32)
        for s in range(slots):
            sub_row = table[pl.ds(subreddit[s, group], 1), :]
            product = (words[word_tile[s, group]].astype(f32) * sub_row).astype(bf16)
            weights = seen[:, s * tile : (s + 1) * tile] * ratings[step, s]
            rows = pl.ds(pl.multiple_of(user_tile[s, group] * tile, tile), tile)
            sums[step % 2, rows, :] += dot_nn(weights, product)
        line = fact_line(user_tile, word_tile, subreddit, live, group, slots, rank)
        spans = jnp.concatenate([runs[group, s] for s in range(slots)], axis=0).astype(f32)
        end = own_rows + 2 * slots
        for o in range(owners):
            owner = lax.rem(me + o, owners)
            rows = pl.ds(pl.multiple_of(owner * own_rows, own_rows), own_rows)
            value = sums[step % 2, rows, :]
            column, up = step // levels, step % levels
            if half == 0:
                other = given[o, column, up].astype(f32)
                value = jnp.concatenate(
                    [
                        value + other[:own_rows],
                        spans,
                        other[own_rows:end],
                        line,
                        other[end : end + 1],
                        jnp.zeros((FACT_ROWS - 2, rank), f32),
                    ],
                    axis=0,
                )
                outs[2 * o + column][up] = value.astype(bf16)
            else:
                value = jnp.concatenate(
                    [value, spans, line, jnp.zeros((FACT_ROWS - 1, rank), f32)], axis=0
                )
                outs[0][o, column, up] = value.astype(bf16)


def rhs_sums(scalars, ratings, runs, words, subs, half, given, owners, own_rows):
    groups, slots, tile, _ = ratings.shape
    rank = words.shape[-1]
    steps, levels = groups // 2, groups // 4
    anywhere = pl.BlockSpec(memory_space=pl.ANY)
    whole = pl.BlockSpec(memory_space=pltpu.VMEM)
    part = (levels, own_rows + 2 * slots * (2 - half) + FACT_ROWS, rank)
    shapes = [part] * (2 * owners) if half == 0 else [(owners, 2) + part]
    return pl.pallas_call(
        functools.partial(rhs_kernel, half=half, owners=owners, own_rows=own_rows),
        in_specs=[pl.BlockSpec(memory_space=pltpu.SMEM)] * 4
        + [anywhere] * (5 - half),
        out_specs=[whole] * len(shapes),
        out_shape=[jax.ShapeDtypeStruct(shape, bf16) for shape in shapes],
        scratch_shapes=[
            pltpu.VMEM((steps,) + ratings.shape[1:], bf16),
            pltpu.VMEM(runs.shape, jnp.int32),
            pltpu.VMEM(words.shape, bf16),
            pltpu.VMEM(subs.shape, bf16),
            pltpu.VMEM(subs.shape, f32),
            pltpu.VMEM((2, owners * own_rows, rank), f32),
            pltpu.SemaphoreType.DMA((steps,)),
            pltpu.SemaphoreType.DMA((4,)),
        ]
        + ([pltpu.VMEM(given.shape, bf16)] if half == 0 else []),
        compiler_params=pltpu.CompilerParams(vmem_limit_bytes=VMEM_LIMIT),
        cost_estimate=pl.CostEstimate(
            flops=8 * ratings.size * rank, bytes_accessed=8 * ratings.size, transcendentals=0
        ),
        name="rhs",
    )(*scalars, ratings, runs, words, subs, *([given] if half == 0 else []))


def chip_kernel(*refs, own_rows, spans):
    levels, _, rank = refs[0].shape
    parts, outs = refs[:-levels], refs[-levels:]
    lines = outs[0].shape[0] - own_rows - spans * len(parts)
    for up in range(levels):
        total = parts[0][up, :own_rows, :].astype(f32)
        for part in parts[1:]:
            total = total + part[up, :own_rows, :].astype(f32)
        outs[up][:own_rows, :] = total.astype(bf16)
        facts = []
        for k, part in enumerate(parts):
            at = own_rows + spans * k
            outs[up][at : at + spans, :] = part[up, own_rows : own_rows + spans, :]
            facts.append(part[up, own_rows + spans :, :].astype(f32)[:2])
        facts.append(jnp.zeros((lines - 2 * len(parts), rank), f32))
        outs[up][own_rows + spans * len(parts) :, :] = jnp.concatenate(
            facts[: len(facts) - (lines == 2 * len(parts))], axis=0
        ).astype(bf16)


def reduce_chip(parts, shards, owners, own_rows):
    given = []
    for o in range(owners):
        for column in range(2):
            pairs = [
                (shard * owners + k, (shard ^ 2 * column) * owners + (k + o) % owners)
                for shard in range(shards)
                for k in range(owners)
            ]
            part = parts[2 * o + column]
            given.append(lax.ppermute(part, AXES, pairs) if o or column else part)
    levels, rows, rank = parts[0].shape
    spans = rows - own_rows - FACT_ROWS
    lines = -(-2 * len(parts) // FACT_ROWS) * FACT_ROWS
    whole = pl.BlockSpec(memory_space=pltpu.VMEM)
    shape = jax.ShapeDtypeStruct((own_rows + spans * len(parts) + lines, rank), bf16)
    return pl.pallas_call(
        functools.partial(chip_kernel, own_rows=own_rows, spans=spans),
        in_specs=[whole] * len(parts),
        out_specs=[whole] * levels,
        out_shape=[shape] * levels,
        compiler_params=pltpu.CompilerParams(vmem_limit_bytes=VMEM_LIMIT),
        name="chip",
    )(*given)


def reduce_levels(total, shards):
    levels = shards // 4
    terms = [total[0]]
    for up in range(1, levels):
        shift = [(shard, (shard + 4 * up) % shards) for shard in range(shards)]
        terms.append(lax.ppermute(total[up], "loop", shift))
    return terms


def steps_kernel(start, activity, subs_in, *refs, shards, levels, slots, cached):
    own_rows, rank = start.shape
    pieces, refs = refs[:shards], refs[shards:]
    terms, refs = refs[:levels], refs[levels:]
    first_out, second_out, third_out, dots_out = refs[:4]
    masks, words, subs, table, runs, lines, facts, chosen, places, arrived, moved = refs[4:15]
    products = refs[-1]
    word_tiles, tile, _ = pieces[0].shape
    sources = lines.shape[0] // levels
    spans = 2 * slots * sources

    copies = [
        pltpu.make_async_copy(
            piece, words.at[k * word_tiles : (k + 1) * word_tiles], arrived.at[k]
        )
        for k, piece in enumerate(pieces)
    ]
    look = pltpu.make_async_copy(subs_in, subs, moved.at[1])
    look.start()
    for copy in copies:
        copy.start()

    for up, term in enumerate(terms):
        rest = term[own_rows + spans :, :].astype(f32)
        lines[up * sources : (up + 1) * sources, :] = rest[:sources].astype(jnp.int32)
    move = pltpu.make_async_copy(lines, facts, moved.at[0])
    move.start()
    rhs = jnp.zeros((own_rows, rank), f32)
    for up, term in enumerate(terms):
        rhs = rhs + term[:own_rows, :].astype(f32)
        runs[up * spans : (up + 1) * spans, :] = term[own_rows : own_rows + spans, :].astype(f32)
    look.wait()
    table[...] = subs[...].astype(f32)
    move.wait()

    place = lax.axis_index("loop")
    level, seat = lax.div(place, 4), lax.rem(place, 4)
    wanted = lax.div(lax.axis_index("own") * own_rows, tile) + 1
    chips = shards // 2

    def ring_at(level, column):
        return jnp.where(column == 0, level, chips - 1 - level)

    used = 0
    column = lax.div(seat, 2)
    for up in range(levels):
        there = lax.rem(level - up + levels, levels)
        ahead = [
            lax.rem(ring_at(there, side) - ring_at(level, column) + chips, chips)
            for side in (column, 1 - column)
        ]

        def choose(k, n, up=up, ahead=ahead):
            src = up * sources + k
            side = lax.rem(lax.div(k, 2), 2)
            distance = jnp.where(side == 0, ahead[0], ahead[1])
            piece = 2 * distance + lax.rem(k, 2)
            for s in range(slots):
                chosen[n] = src * slots + s
                places[0, n] = word_tiles * piece + facts[src, slots + s]
                places[1, n] = 128 * facts[src, 2 * slots + s] + facts[src, 3 * slots + s]
                n = n + jnp.where(facts[src, s] == wanted, 1, 0)
            return n

        used = lax.fori_loop(0, sources, choose, used)
    chunks = lax.div(used + CHUNK - 1, CHUNK)

    offset = lax.rem(lax.axis_index("own") * own_rows, tile)
    pick = (
        lax.broadcasted_iota(jnp.int32, (own_rows, tile), 0) + offset
        == lax.broadcasted_iota(jnp.int32, (own_rows, tile), 1)
    ).astype(f32).astype(bf16)

    def mask(chunk):
        parts = []
        for b in range(CHUNK):
            i = chunk * CHUNK + b
            j = chosen[jnp.minimum(i, used - 1)]
            first = runs[pl.ds(2 * j, 1), :].astype(jnp.int32)
            length = runs[pl.ds(2 * j + 1, 1), :].astype(jnp.int32)
            length = jnp.where(i < used, length, 0)
            parts.append(mask_columns(first, length, tile))
        return dot_nt(pick, jnp.concatenate(parts, axis=0)).astype(bf16)

    def product(i):
        i = jnp.minimum(i, used - 1)
        return (words[places[0, i]].astype(f32) * table[pl.ds(places[1, i], 1), :]).astype(bf16)

    for copy in copies:
        copy.wait()

    def gram(vector, build=False):
        rounded = vector.astype(bf16)

        def body(chunk, total):
            if build:
                masks[chunk] = mask(chunk)
            if cached and not build:
                block = products[chunk]
            else:
                block = jnp.concatenate(
                    [product(chunk * CHUNK + b) for b in range(CHUNK)], axis=0
                )
                if cached:
                    products[chunk] = block
            weights = dot_nt(rounded, block).astype(bf16) * masks[chunk]
            return total + dot_nn(weights, block)

        return lax.fori_loop(0, chunks, body, jnp.zeros((own_rows, rank), f32))

    def over_row(a, b):
        return jnp.sum(a * b, axis=1, keepdims=True)

    scale = jnp.broadcast_to(activity[...], (rank, own_rows)).T
    first = scale * (rhs - gram(start[...], build=True)) - ridge * start[...]
    second = scale * gram(first) + ridge * first
    norms, overlaps = over_row(first, first), over_row(first, second)
    share = jnp.where(norms > 0.0, overlaps / jnp.where(norms > 0.0, norms, 1.0), 0.0)
    rest = second - share * first
    third = scale * gram(rest) + ridge * rest + share * second
    first_out[...] = first
    second_out[...] = second
    third_out[...] = third
    rows = [norms, overlaps, over_row(second, second), over_row(first, third), over_row(second, third)]
    lane = lax.broadcasted_iota(jnp.int32, (1, rank), 1)
    line = jnp.zeros((1, rank), f32)
    for k, value in enumerate(rows):
        line = line + jnp.where(lane == k, jnp.sum(value, axis=0, keepdims=True), 0.0)
    dots_out[...] = jnp.broadcast_to(line[None], dots_out.shape)


def krylov(start, activity, subs, pieces, terms, slots, devices):
    own_rows, rank = start.shape
    blocks = devices * slots
    word_tiles, tile, _ = pieces[0].shape
    chunks = -(-blocks // CHUNK)
    cached = blocks * tile * rank * 2 <= 16 * 2**20
    whole = pl.BlockSpec(memory_space=pltpu.VMEM)
    anywhere = pl.BlockSpec(memory_space=pl.ANY)
    vector = jax.ShapeDtypeStruct((own_rows, rank), f32)
    scratch = [
        pltpu.VMEM((chunks, own_rows, CHUNK * tile), bf16),
        pltpu.VMEM((len(pieces) * word_tiles, tile, rank), bf16),
        pltpu.VMEM(subs.shape, bf16),
        pltpu.VMEM(subs.shape, f32),
        pltpu.VMEM((2 * blocks, tile), f32),
        pltpu.VMEM((devices, rank), jnp.int32),
        pltpu.SMEM((devices, rank), jnp.int32),
        pltpu.SMEM((blocks,), jnp.int32),
        pltpu.SMEM((2, blocks), jnp.int32),
        pltpu.SemaphoreType.DMA((len(pieces),)),
        pltpu.SemaphoreType.DMA((2,)),
    ]
    if cached:
        scratch.append(pltpu.VMEM((chunks, CHUNK * tile, rank), bf16))
    return pl.pallas_call(
        functools.partial(
            steps_kernel, shards=len(pieces), levels=len(terms), slots=slots, cached=cached
        ),
        in_specs=[whole, whole, anywhere] + [anywhere] * len(pieces) + [whole] * len(terms),
        out_specs=[whole] * 4,
        out_shape=[vector, vector, vector, jax.ShapeDtypeStruct((devices, 1, rank), f32)],
        scratch_shapes=scratch,
        compiler_params=pltpu.CompilerParams(vmem_limit_bytes=VMEM_LIMIT),
        name="krylov",
    )(start, activity, subs, *pieces, *terms)


def last_kernel(dots, start, first, second, third, solution_out, residual_out):
    line = dots[0]
    for k in range(1, dots.shape[0]):
        line = line + dots[k]
    rr, rq, qq, rz, qz = (line[:, k : k + 1] for k in range(5))
    step0 = rr / rq
    next_rr = rr - 2.0 * step0 * rq + step0 * step0 * qq
    grow = 1.0 + next_rr / rr
    slope = grow * (grow * rq - step0 * (rz + qq)) + step0 * step0 * qz
    step1 = next_rr / slope
    near, far = step0 + step1 * grow, step1 * step0
    solution_out[...] = start[...] + near * first[...] - far * second[...]
    residual_out[...] = first[...] - near * second[...] + far * third[...]


def last_step(dots, start, first, second, third):
    whole = pl.BlockSpec(memory_space=pltpu.VMEM)
    vector = jax.ShapeDtypeStruct(start.shape, f32)
    return pl.pallas_call(
        last_kernel,
        in_specs=[whole] * 5,
        out_specs=[whole] * 2,
        out_shape=[vector, vector],
        compiler_params=pltpu.CompilerParams(vmem_limit_bytes=VMEM_LIMIT),
        name="last_step",
    )(dots, start, first, second, third)


def ring_round(up, down, held, step, shards):
    chips = shards // 2
    levels = chips // 2
    order = [2 * level for level in range(levels)] + [
        2 * level + 1 for level in reversed(range(levels))
    ]

    def shift(by):
        return [
            (2 * order[p] + core, 2 * order[(p + by) % chips] + core)
            for p in range(chips)
            for core in range(2)
        ]

    up = lax.ppermute(up, "loop", shift(1))
    held[chips - step] = up
    if step < chips - step:
        down = lax.ppermute(down, "loop", shift(-1))
        held[step] = down
    return up, down


def other_core(value, shards):
    return lax.ppermute(value, "loop", [(shard, shard ^ 1) for shard in range(shards)])


def on_device(
    factor_start,
    activity,
    word_factors,
    sub_factors,
    ratings,
    user_tile,
    word_tile,
    subreddit,
    counts,
    runs,
):
    own_rows, rank = factor_start.shape
    owners, shards = lax.axis_size("own"), lax.axis_size("loop")
    slots = ratings.shape[3]
    devices = shards * owners
    chips = shards // 2
    together = lax.optimization_barrier

    scalars = (user_tile[0, 0].T, word_tile[0, 0].T, subreddit[0, 0].T, counts[0])
    mine = word_factors[0]
    held = {0: mine}

    inputs = (scalars, ratings[0, 0], runs[0, 0], mine, sub_factors)
    up, down = ring_round(mine, mine, held, 1, shards)
    (away,) = rhs_sums(*inputs, 1, None, owners, own_rows)
    up, down, away = together((up, down, away))

    up, down = ring_round(up, down, held, 2, shards)
    parts = rhs_sums(*inputs, 0, other_core(away, shards), owners, own_rows)
    up, down, parts = together((up, down, parts))

    up, down = ring_round(up, down, held, 3, shards)
    total = reduce_chip(parts, shards, owners, own_rows)
    up, down, total = together((up, down, total))

    for step in range(4, chips // 2 + 1):
        up, down = ring_round(up, down, held, step, shards)
    terms = reduce_levels(total, shards)
    pieces = []
    for distance in range(chips):
        pieces += [held[distance], other_core(held[distance], shards)]
    first, second, third, dots = krylov(
        factor_start, activity[None], sub_factors, pieces, terms, slots, devices
    )
    everyone = lax.all_to_all(dots, AXES, 0, 0, tiled=True)
    return tuple(last_step(everyone, factor_start, first, second, third))


def solution(mesh):
    placed = (
        P(("loop", "own"), None),
        P(("loop", "own")),
        P("loop", None, None, None),
        P(),
        P("loop", "own", None, None, None, None),
        P("loop", "own", None, None),
        P("loop", "own", None, None),
        P("loop", "own", None, None),
        P("loop", "own", None),
        P("loop", "own", None, None, None, None),
    )
    return jax.shard_map(
        on_device,
        mesh=mesh,
        in_specs=placed,
        out_specs=(P(("loop", "own"), None), P(("loop", "own"), None)),
        check_vma=False,
    )
```

```python
import functools

import jax
import jax.numpy as jnp
from jax import lax
from jax.experimental import pallas as pl
from jax.experimental.pallas import tpu as pltpu
from jax.sharding import PartitionSpec as P

AXES = ("loop", "own")
CHUNK = 16
FACT_ROWS = 16
ridge = 0.05
VMEM_LIMIT = 60 * 2**20
f32 = jnp.float32
bf16 = jnp.bfloat16


def dot_nt(left, right):
    return lax.dot_general(left, right, (((1,), (1,)), ((), ())), preferred_element_type=f32)


def dot_nn(left, right):
    return jnp.dot(left, right, preferred_element_type=f32)


def mask_columns(first, length, tile):
    column = lax.broadcasted_iota(jnp.int32, (tile, first.shape[-1]), 0)
    inside = ((column - first) & (tile - 1)) < length
    return jnp.where(inside, 1.0, 0.0).astype(bf16)


def fact_line(user_tile, word_tile, subreddit, live, group, slots, rank):
    lane = lax.broadcasted_iota(jnp.int32, (1, rank), 1)
    line = jnp.zeros((1, rank), jnp.int32)
    for s in range(slots):
        sub = subreddit[s, group]
        user = jnp.where(s < live, user_tile[s, group] + 1, 0)
        values = (user, word_tile[s, group], lax.div(sub, 128), lax.rem(sub, 128))
        for k, value in enumerate(values):
            line = jnp.where(lane == k * slots + s, value, line)
    return line.astype(f32)


def rhs_kernel(
    user_tile, word_tile, subreddit, counts, ratings_in, runs_in, words_in, subs_in, *refs,
    half, owners, own_rows,
):
    if half == 0:
        given_in, refs, given = refs[0], refs[1:-1], refs[-1]
    outs, (ratings, runs, words, subs, table, sums, arrived, loaded) = refs[:-8], refs[-8:]
    steps, slots, tile = ratings.shape[0], ratings.shape[1], ratings.shape[2]
    rank = words.shape[-1]
    levels = steps // 2

    place = lax.axis_index("loop")
    level, seat = lax.div(place, 4), lax.rem(place, 4)

    def group_at(step):
        there = lax.rem(seat + 2 * (step // levels), 4)
        if half:
            there = there + 1 - 2 * lax.rem(there, 2)
        return 4 * lax.rem(level + step % levels, levels) + there

    def load(step):
        group = group_at(step)
        return pltpu.make_async_copy(ratings_in.at[group], ratings.at[step], arrived.at[step])

    tables = [
        pltpu.make_async_copy(source, target, loaded.at[k])
        for k, (source, target) in enumerate(
            [(subs_in, subs), (runs_in, runs), (words_in, words)]
        )
    ]
    for copy in tables:
        copy.start()
    for step in range(steps):
        load(step).start()
    if half == 0:
        gift = pltpu.make_async_copy(given_in, given, loaded.at[3])
        gift.start()
    tables[0].wait()
    table[...] = subs[...].astype(f32)
    tables[1].wait()
    tables[2].wait()

    if half == 0:
        gift.wait()
    eye = (
        lax.broadcasted_iota(jnp.int32, (tile, tile), 0)
        == lax.broadcasted_iota(jnp.int32, (tile, tile), 1)
    ).astype(f32).astype(bf16)
    me = lax.axis_index("own")
    for step in range(steps):
        group = group_at(step)
        live = counts[0, group]
        columns = []
        for s in range(slots):
            pair = runs[group, s]
            columns.append(
                mask_columns(pair[0:1], jnp.where(s < live, pair[1:2], 0), tile)
            )
        seen = dot_nt(eye, jnp.concatenate(columns, axis=0)).astype(bf16)
        load(step).wait()
        sums[step % 2] = jnp.zeros(sums.shape[1:], f32)
        for s in range(slots):
            sub_row = table[pl.ds(subreddit[s, group], 1), :]
            product = (words[word_tile[s, group]].astype(f32) * sub_row).astype(bf16)
            weights = seen[:, s * tile : (s + 1) * tile] * ratings[step, s]
            rows = pl.ds(pl.multiple_of(user_tile[s, group] * tile, tile), tile)
            sums[step % 2, rows, :] += dot_nn(weights, product)
        line = fact_line(user_tile, word_tile, subreddit, live, group, slots, rank)
        spans = jnp.concatenate([runs[group, s] for s in range(slots)], axis=0).astype(f32)
        end = own_rows + 2 * slots
        for o in range(owners):
            owner = lax.rem(me + o, owners)
            rows = pl.ds(pl.multiple_of(owner * own_rows, own_rows), own_rows)
            value = sums[step % 2, rows, :]
            column, up = step // levels, step % levels
            if half == 0:
                other = given[o, column, up].astype(f32)
                value = jnp.concatenate(
                    [
                        value + other[:own_rows],
                        spans,
                        other[own_rows:end],
                        line,
                        other[end : end + 1],
                        jnp.zeros((FACT_ROWS - 2, rank), f32),
                    ],
                    axis=0,
                )
                outs[2 * o + column][up] = value.astype(bf16)
            else:
                value = jnp.concatenate(
                    [value, spans, line, jnp.zeros((FACT_ROWS - 1, rank), f32)], axis=0
                )
                outs[0][o, column, up] = value.astype(bf16)


def rhs_sums(scalars, ratings, runs, words, subs, half, given, owners, own_rows):
    groups, slots, tile, _ = ratings.shape
    rank = words.shape[-1]
    steps, levels = groups // 2, groups // 4
    anywhere = pl.BlockSpec(memory_space=pl.ANY)
    whole = pl.BlockSpec(memory_space=pltpu.VMEM)
    part = (levels, own_rows + 2 * slots * (2 - half) + FACT_ROWS, rank)
    shapes = [part] * (2 * owners) if half == 0 else [(owners, 2) + part]
    return pl.pallas_call(
        functools.partial(rhs_kernel, half=half, owners=owners, own_rows=own_rows),
        in_specs=[pl.BlockSpec(memory_space=pltpu.SMEM)] * 4
        + [anywhere] * (5 - half),
        out_specs=[whole] * len(shapes),
        out_shape=[jax.ShapeDtypeStruct(shape, bf16) for shape in shapes],
        scratch_shapes=[
            pltpu.VMEM((steps,) + ratings.shape[1:], bf16),
            pltpu.VMEM(runs.shape, jnp.int32),
            pltpu.VMEM(words.shape, bf16),
            pltpu.VMEM(subs.shape, bf16),
            pltpu.VMEM(subs.shape, f32),
            pltpu.VMEM((2, owners * own_rows, rank), f32),
            pltpu.SemaphoreType.DMA((steps,)),
            pltpu.SemaphoreType.DMA((4,)),
        ]
        + ([pltpu.VMEM(given.shape, bf16)] if half == 0 else []),
        compiler_params=pltpu.CompilerParams(vmem_limit_bytes=VMEM_LIMIT),
        cost_estimate=pl.CostEstimate(
            flops=8 * ratings.size * rank, bytes_accessed=8 * ratings.size, transcendentals=0
        ),
        name="rhs",
    )(*scalars, ratings, runs, words, subs, *([given] if half == 0 else []))


def chip_kernel(*refs, own_rows, spans):
    levels, _, rank = refs[0].shape
    parts, outs = refs[:-levels], refs[-levels:]
    lines = outs[0].shape[0] - own_rows - spans * len(parts)
    for up in range(levels):
        total = parts[0][up, :own_rows, :].astype(f32)
        for part in parts[1:]:
            total = total + part[up, :own_rows, :].astype(f32)
        outs[up][:own_rows, :] = total.astype(bf16)
        facts = []
        for k, part in enumerate(parts):
            at = own_rows + spans * k
            outs[up][at : at + spans, :] = part[up, own_rows : own_rows + spans, :]
            facts.append(part[up, own_rows + spans :, :].astype(f32)[:2])
        facts.append(jnp.zeros((lines - 2 * len(parts), rank), f32))
        outs[up][own_rows + spans * len(parts) :, :] = jnp.concatenate(
            facts[: len(facts) - (lines == 2 * len(parts))], axis=0
        ).astype(bf16)


def reduce_chip(parts, shards, owners, own_rows):
    given = []
    for o in range(owners):
        for column in range(2):
            pairs = [
                (shard * owners + k, (shard ^ 2 * column) * owners + (k + o) % owners)
                for shard in range(shards)
                for k in range(owners)
            ]
            part = parts[2 * o + column]
            given.append(lax.ppermute(part, AXES, pairs) if o or column else part)
    levels, rows, rank = parts[0].shape
    spans = rows - own_rows - FACT_ROWS
    lines = -(-2 * len(parts) // FACT_ROWS) * FACT_ROWS
    whole = pl.BlockSpec(memory_space=pltpu.VMEM)
    shape = jax.ShapeDtypeStruct((own_rows + spans * len(parts) + lines, rank), bf16)
    return pl.pallas_call(
        functools.partial(chip_kernel, own_rows=own_rows, spans=spans),
        in_specs=[whole] * len(parts),
        out_specs=[whole] * levels,
        out_shape=[shape] * levels,
        compiler_params=pltpu.CompilerParams(vmem_limit_bytes=VMEM_LIMIT),
        name="chip",
    )(*given)


def reduce_levels(total, shards):
    levels = shards // 4
    terms = [total[0]]
    for up in range(1, levels):
        shift = [(shard, (shard + 4 * up) % shards) for shard in range(shards)]
        terms.append(lax.ppermute(total[up], "loop", shift))
    return terms


def steps_kernel(start, activity, subs_in, *refs, shards, levels, slots, cached):
    own_rows, rank = start.shape
    pieces, refs = refs[:shards], refs[shards:]
    terms, refs = refs[:levels], refs[levels:]
    first_out, second_out, third_out, dots_out = refs[:4]
    masks, words, subs, table, runs, lines, facts, chosen, places, arrived, moved = refs[4:15]
    products = refs[-1]
    word_tiles, tile, _ = pieces[0].shape
    sources = lines.shape[0] // levels
    spans = 2 * slots * sources

    copies = [
        pltpu.make_async_copy(
            piece, words.at[k * word_tiles : (k + 1) * word_tiles], arrived.at[k]
        )
        for k, piece in enumerate(pieces)
    ]
    look = pltpu.make_async_copy(subs_in, subs, moved.at[1])
    look.start()
    for copy in copies:
        copy.start()

    for up, term in enumerate(terms):
        rest = term[own_rows + spans :, :].astype(f32)
        lines[up * sources : (up + 1) * sources, :] = rest[:sources].astype(jnp.int32)
    move = pltpu.make_async_copy(lines, facts, moved.at[0])
    move.start()
    rhs = jnp.zeros((own_rows, rank), f32)
    for up, term in enumerate(terms):
        rhs = rhs + term[:own_rows, :].astype(f32)
        runs[up * spans : (up + 1) * spans, :] = term[own_rows : own_rows + spans, :].astype(f32)
    look.wait()
    table[...] = subs[...].astype(f32)
    move.wait()

    place = lax.axis_index("loop")
    level, seat = lax.div(place, 4), lax.rem(place, 4)
    wanted = lax.div(lax.axis_index("own") * own_rows, tile) + 1
    chips = shards // 2

    def ring_at(level, column):
        return jnp.where(column == 0, level, chips - 1 - level)

    used = 0
    column = lax.div(seat, 2)
    for up in range(levels):
        there = lax.rem(level - up + levels, levels)
        ahead = [
            lax.rem(ring_at(there, side) - ring_at(level, column) + chips, chips)
            for side in (column, 1 - column)
        ]

        def choose(k, n, up=up, ahead=ahead):
            src = up * sources + k
            side = lax.rem(lax.div(k, 2), 2)
            distance = jnp.where(side == 0, ahead[0], ahead[1])
            piece = 2 * distance + lax.rem(k, 2)
            for s in range(slots):
                chosen[n] = src * slots + s
                places[0, n] = word_tiles * piece + facts[src, slots + s]
                places[1, n] = 128 * facts[src, 2 * slots + s] + facts[src, 3 * slots + s]
                n = n + jnp.where(facts[src, s] == wanted, 1, 0)
            return n

        used = lax.fori_loop(0, sources, choose, used)
    chunks = lax.div(used + CHUNK - 1, CHUNK)

    offset = lax.rem(lax.axis_index("own") * own_rows, tile)
    pick = (
        lax.broadcasted_iota(jnp.int32, (own_rows, tile), 0) + offset
        == lax.broadcasted_iota(jnp.int32, (own_rows, tile), 1)
    ).astype(f32).astype(bf16)

    def mask(chunk):
        parts = []
        for b in range(CHUNK):
            i = chunk * CHUNK + b
            j = chosen[jnp.minimum(i, used - 1)]
            first = runs[pl.ds(2 * j, 1), :].astype(jnp.int32)
            length = runs[pl.ds(2 * j + 1, 1), :].astype(jnp.int32)
            length = jnp.where(i < used, length, 0)
            parts.append(mask_columns(first, length, tile))
        return dot_nt(pick, jnp.concatenate(parts, axis=0)).astype(bf16)

    def product(i):
        i = jnp.minimum(i, used - 1)
        return (words[places[0, i]].astype(f32) * table[pl.ds(places[1, i], 1), :]).astype(bf16)

    for copy in copies:
        copy.wait()

    def gram(vector, build=False):
        rounded = vector.astype(bf16)

        def body(chunk, total):
            if build:
                masks[chunk] = mask(chunk)
            if cached and not build:
                block = products[chunk]
            else:
                block = jnp.concatenate(
                    [product(chunk * CHUNK + b) for b in range(CHUNK)], axis=0
                )
                if cached:
                    products[chunk] = block
            weights = dot_nt(rounded, block).astype(bf16) * masks[chunk]
            return total + dot_nn(weights, block)

        return lax.fori_loop(0, chunks, body, jnp.zeros((own_rows, rank), f32))

    def over_row(a, b):
        return jnp.sum(a * b, axis=1, keepdims=True)

    scale = jnp.broadcast_to(activity[...], (rank, own_rows)).T
    first = scale * (rhs - gram(start[...], build=True)) - ridge * start[...]
    second = scale * gram(first) + ridge * first
    norms, overlaps = over_row(first, first), over_row(first, second)
    share = jnp.where(norms > 0.0, overlaps / jnp.where(norms > 0.0, norms, 1.0), 0.0)
    rest = second - share * first
    third = scale * gram(rest) + ridge * rest + share * second
    first_out[...] = first
    second_out[...] = second
    third_out[...] = third
    rows = [norms, overlaps, over_row(second, second), over_row(first, third), over_row(second, third)]
    lane = lax.broadcasted_iota(jnp.int32, (1, rank), 1)
    line = jnp.zeros((1, rank), f32)
    for k, value in enumerate(rows):
        line = line + jnp.where(lane == k, jnp.sum(value, axis=0, keepdims=True), 0.0)
    dots_out[...] = jnp.broadcast_to(line[None], dots_out.shape)


def krylov(start, activity, subs, pieces, terms, slots, devices):
    own_rows, rank = start.shape
    blocks = devices * slots
    word_tiles, tile, _ = pieces[0].shape
    chunks = -(-blocks // CHUNK)
    cached = blocks * tile * rank * 2 <= 16 * 2**20
    whole = pl.BlockSpec(memory_space=pltpu.VMEM)
    anywhere = pl.BlockSpec(memory_space=pl.ANY)
    vector = jax.ShapeDtypeStruct((own_rows, rank), f32)
    scratch = [
        pltpu.VMEM((chunks, own_rows, CHUNK * tile), bf16),
        pltpu.VMEM((len(pieces) * word_tiles, tile, rank), bf16),
        pltpu.VMEM(subs.shape, bf16),
        pltpu.VMEM(subs.shape, f32),
        pltpu.VMEM((2 * blocks, tile), f32),
        pltpu.VMEM((devices, rank), jnp.int32),
        pltpu.SMEM((devices, rank), jnp.int32),
        pltpu.SMEM((blocks,), jnp.int32),
        pltpu.SMEM((2, blocks), jnp.int32),
        pltpu.SemaphoreType.DMA((len(pieces),)),
        pltpu.SemaphoreType.DMA((2,)),
    ]
    if cached:
        scratch.append(pltpu.VMEM((chunks, CHUNK * tile, rank), bf16))
    return pl.pallas_call(
        functools.partial(
            steps_kernel, shards=len(pieces), levels=len(terms), slots=slots, cached=cached
        ),
        in_specs=[whole, whole, anywhere] + [anywhere] * len(pieces) + [whole] * len(terms),
        out_specs=[whole] * 4,
        out_shape=[vector, vector, vector, jax.ShapeDtypeStruct((devices, 1, rank), f32)],
        scratch_shapes=scratch,
        compiler_params=pltpu.CompilerParams(vmem_limit_bytes=VMEM_LIMIT),
        name="krylov",
    )(start, activity, subs, *pieces, *terms)


def last_kernel(dots, start, first, second, third, solution_out, residual_out):
    line = dots[0]
    for k in range(1, dots.shape[0]):
        line = line + dots[k]
    rr, rq, qq, rz, qz = (line[:, k : k + 1] for k in range(5))
    step0 = rr / rq
    next_rr = rr - 2.0 * step0 * rq + step0 * step0 * qq
    grow = 1.0 + next_rr / rr
    slope = grow * (grow * rq - step0 * (rz + qq)) + step0 * step0 * qz
    step1 = next_rr / slope
    near, far = step0 + step1 * grow, step1 * step0
    solution_out[...] = start[...] + near * first[...] - far * second[...]
    residual_out[...] = first[...] - near * second[...] + far * third[...]


def last_step(dots, start, first, second, third):
    whole = pl.BlockSpec(memory_space=pltpu.VMEM)
    vector = jax.ShapeDtypeStruct(start.shape, f32)
    return pl.pallas_call(
        last_kernel,
        in_specs=[whole] * 5,
        out_specs=[whole] * 2,
        out_shape=[vector, vector],
        compiler_params=pltpu.CompilerParams(vmem_limit_bytes=VMEM_LIMIT),
        name="last_step",
    )(dots, start, first, second, third)


def ring_round(up, down, held, step, shards):
    chips = shards // 2
    levels = chips // 2
    order = [2 * level for level in range(levels)] + [
        2 * level + 1 for level in reversed(range(levels))
    ]

    def shift(by):
        return [
            (2 * order[p] + core, 2 * order[(p + by) % chips] + core)
            for p in range(chips)
            for core in range(2)
        ]

    up = lax.ppermute(up, "loop", shift(1))
    held[chips - step] = up
    if step < chips - step:
        down = lax.ppermute(down, "loop", shift(-1))
        held[step] = down
    return up, down


def other_core(value, shards):
    return lax.ppermute(value, "loop", [(shard, shard ^ 1) for shard in range(shards)])


def on_device(
    factor_start,
    activity,
    word_factors,
    sub_factors,
    ratings,
    user_tile,
    word_tile,
    subreddit,
    counts,
    runs,
):
    own_rows, rank = factor_start.shape
    owners, shards = lax.axis_size("own"), lax.axis_size("loop")
    slots = ratings.shape[3]
    devices = shards * owners
    chips = shards // 2
    together = lax.optimization_barrier

    scalars = (user_tile[0, 0].T, word_tile[0, 0].T, subreddit[0, 0].T, counts[0])
    mine = word_factors[0]
    held = {0: mine}

    inputs = (scalars, ratings[0, 0], runs[0, 0], mine, sub_factors)
    up, down = ring_round(mine, mine, held, 1, shards)
    (away,) = rhs_sums(*inputs, 1, None, owners, own_rows)
    crossed = {0: other_core(mine, shards)}
    up, down, away, crossed = together((up, down, away, crossed))

    def cross(step):
        for distance in {step, chips - step}:
            crossed[distance] = other_core(held[distance], shards)

    cross(1)
    up, down = ring_round(up, down, held, 2, shards)
    parts = rhs_sums(*inputs, 0, other_core(away, shards), owners, own_rows)
    up, down, parts, crossed = together((up, down, parts, crossed))

    up, down = ring_round(up, down, held, 3, shards)
    total = reduce_chip(parts, shards, owners, own_rows)
    up, down, total = together((up, down, total))

    for step in range(4, chips // 2 + 1):
        up, down = ring_round(up, down, held, step, shards)
    terms = reduce_levels(total, shards)
    held[chips // 2], terms, crossed = together((held[chips // 2], terms, crossed))

    for step in range(2, chips // 2 + 1):
        cross(step)
    pieces = []
    for distance in range(chips):
        pieces += [held[distance], crossed[distance]]
    first, second, third, dots = krylov(
        factor_start, activity[None], sub_factors, pieces, terms, slots, devices
    )
    everyone = lax.all_to_all(dots, AXES, 0, 0, tiled=True)
    return tuple(last_step(everyone, factor_start, first, second, third))


def solution(mesh):
    placed = (
        P(("loop", "own"), None),
        P(("loop", "own")),
        P("loop", None, None, None),
        P(),
        P("loop", "own", None, None, None, None),
        P("loop", "own", None, None),
        P("loop", "own", None, None),
        P("loop", "own", None, None),
        P("loop", "own", None),
        P("loop", "own", None, None, None, None),
    )
    return jax.shard_map(
        on_device,
        mesh=mesh,
        in_specs=placed,
        out_specs=(P(("loop", "own"), None), P(("loop", "own"), None)),
        check_vma=False,
    )
```

```python
import functools

import jax
import jax.numpy as jnp
from jax import lax
from jax.experimental import pallas as pl
from jax.experimental.pallas import tpu as pltpu
from jax.sharding import PartitionSpec as P

AXES = ("loop", "own")
CHUNK = 48
FACT_ROWS = 16
ridge = 0.05
VMEM_LIMIT = 60 * 2**20
f32 = jnp.float32
bf16 = jnp.bfloat16


def dot_nt(left, right):
    return lax.dot_general(left, right, (((1,), (1,)), ((), ())), preferred_element_type=f32)


def dot_nn(left, right):
    return jnp.dot(left, right, preferred_element_type=f32)


def mask_columns(first, length, tile):
    column = lax.broadcasted_iota(jnp.int32, (tile, first.shape[-1]), 0)
    inside = ((column - first) & (tile - 1)) < length
    return jnp.where(inside, 1.0, 0.0).astype(bf16)


def fact_line(user_tile, word_tile, subreddit, live, group, slots, rank):
    lane = lax.broadcasted_iota(jnp.int32, (1, rank), 1)
    line = jnp.zeros((1, rank), jnp.int32)
    for s in range(slots):
        sub = subreddit[s, group]
        user = jnp.where(s < live, user_tile[s, group] + 1, 0)
        values = (user, word_tile[s, group], lax.div(sub, 128), lax.rem(sub, 128))
        for k, value in enumerate(values):
            line = jnp.where(lane == k * slots + s, value, line)
    return line.astype(f32)


def rhs_kernel(
    user_tile, word_tile, subreddit, counts, ratings_in, runs_in, words_in, subs_in, *refs,
    half, owners, own_rows,
):
    if half == 0:
        given_in, refs, given = refs[0], refs[1:-1], refs[-1]
    outs, (ratings, runs, words, subs, table, sums, arrived, loaded) = refs[:-8], refs[-8:]
    steps, slots, tile = ratings.shape[0], ratings.shape[1], ratings.shape[2]
    rank = words.shape[-1]
    levels = steps // 2

    place = lax.axis_index("loop")
    level, seat = lax.div(place, 4), lax.rem(place, 4)

    def group_at(step):
        there = lax.rem(seat + 2 * (step // levels), 4)
        if half:
            there = there + 1 - 2 * lax.rem(there, 2)
        return 4 * lax.rem(level + step % levels, levels) + there

    def load(step):
        group = group_at(step)
        return pltpu.make_async_copy(ratings_in.at[group], ratings.at[step], arrived.at[step])

    tables = [
        pltpu.make_async_copy(source, target, loaded.at[k])
        for k, (source, target) in enumerate(
            [(subs_in, subs), (runs_in, runs), (words_in, words)]
        )
    ]
    for copy in tables:
        copy.start()
    for step in range(steps):
        load(step).start()
    if half == 0:
        gift = pltpu.make_async_copy(given_in, given, loaded.at[3])
        gift.start()
    tables[0].wait()
    table[...] = subs[...].astype(f32)
    tables[1].wait()
    tables[2].wait()

    if half == 0:
        gift.wait()
    eye = (
        lax.broadcasted_iota(jnp.int32, (tile, tile), 0)
        == lax.broadcasted_iota(jnp.int32, (tile, tile), 1)
    ).astype(f32).astype(bf16)
    me = lax.axis_index("own")
    for step in range(steps):
        group = group_at(step)
        live = counts[0, group]
        columns = []
        for s in range(slots):
            pair = runs[group, s]
            columns.append(
                mask_columns(pair[0:1], jnp.where(s < live, pair[1:2], 0), tile)
            )
        seen = dot_nt(eye, jnp.concatenate(columns, axis=0)).astype(bf16)
        load(step).wait()
        sums[step % 2] = jnp.zeros(sums.shape[1:], f32)
        for s in range(slots):
            sub_row = table[pl.ds(subreddit[s, group], 1), :]
            product = (words[word_tile[s, group]].astype(f32) * sub_row).astype(bf16)
            weights = seen[:, s * tile : (s + 1) * tile] * ratings[step, s]
            rows = pl.ds(pl.multiple_of(user_tile[s, group] * tile, tile), tile)
            sums[step % 2, rows, :] += dot_nn(weights, product)
        line = fact_line(user_tile, word_tile, subreddit, live, group, slots, rank)
        spans = jnp.concatenate([runs[group, s] for s in range(slots)], axis=0).astype(f32)
        end = own_rows + 2 * slots
        for o in range(owners):
            owner = lax.rem(me + o, owners)
            rows = pl.ds(pl.multiple_of(owner * own_rows, own_rows), own_rows)
            value = sums[step % 2, rows, :]
            column, up = step // levels, step % levels
            if half == 0:
                other = given[o, column, up].astype(f32)
                value = jnp.concatenate(
                    [
                        value + other[:own_rows],
                        spans,
                        other[own_rows:end],
                        line,
                        other[end : end + 1],
                        jnp.zeros((FACT_ROWS - 2, rank), f32),
                    ],
                    axis=0,
                )
                outs[2 * o + column][up] = value.astype(bf16)
            else:
                value = jnp.concatenate(
                    [value, spans, line, jnp.zeros((FACT_ROWS - 1, rank), f32)], axis=0
                )
                outs[0][o, column, up] = value.astype(bf16)


def rhs_sums(scalars, ratings, runs, words, subs, half, given, owners, own_rows):
    groups, slots, tile, _ = ratings.shape
    rank = words.shape[-1]
    steps, levels = groups // 2, groups // 4
    anywhere = pl.BlockSpec(memory_space=pl.ANY)
    whole = pl.BlockSpec(memory_space=pltpu.VMEM)
    part = (levels, own_rows + 2 * slots * (2 - half) + FACT_ROWS, rank)
    shapes = [part] * (2 * owners) if half == 0 else [(owners, 2) + part]
    return pl.pallas_call(
        functools.partial(rhs_kernel, half=half, owners=owners, own_rows=own_rows),
        in_specs=[pl.BlockSpec(memory_space=pltpu.SMEM)] * 4
        + [anywhere] * (5 - half),
        out_specs=[whole] * len(shapes),
        out_shape=[jax.ShapeDtypeStruct(shape, bf16) for shape in shapes],
        scratch_shapes=[
            pltpu.VMEM((steps,) + ratings.shape[1:], bf16),
            pltpu.VMEM(runs.shape, jnp.int32),
            pltpu.VMEM(words.shape, bf16),
            pltpu.VMEM(subs.shape, bf16),
            pltpu.VMEM(subs.shape, f32),
            pltpu.VMEM((2, owners * own_rows, rank), f32),
            pltpu.SemaphoreType.DMA((steps,)),
            pltpu.SemaphoreType.DMA((4,)),
        ]
        + ([pltpu.VMEM(given.shape, bf16)] if half == 0 else []),
        compiler_params=pltpu.CompilerParams(vmem_limit_bytes=VMEM_LIMIT),
        cost_estimate=pl.CostEstimate(
            flops=8 * ratings.size * rank, bytes_accessed=8 * ratings.size, transcendentals=0
        ),
        name="rhs",
    )(*scalars, ratings, runs, words, subs, *([given] if half == 0 else []))


def chip_kernel(*refs, own_rows, spans):
    levels, _, rank = refs[0].shape
    parts, outs = refs[:-levels], refs[-levels:]
    lines = outs[0].shape[0] - own_rows - spans * len(parts)
    for up in range(levels):
        total = parts[0][up, :own_rows, :].astype(f32)
        for part in parts[1:]:
            total = total + part[up, :own_rows, :].astype(f32)
        outs[up][:own_rows, :] = total.astype(bf16)
        facts = []
        for k, part in enumerate(parts):
            at = own_rows + spans * k
            outs[up][at : at + spans, :] = part[up, own_rows : own_rows + spans, :]
            facts.append(part[up, own_rows + spans :, :].astype(f32)[:2])
        facts.append(jnp.zeros((lines - 2 * len(parts), rank), f32))
        outs[up][own_rows + spans * len(parts) :, :] = jnp.concatenate(
            facts[: len(facts) - (lines == 2 * len(parts))], axis=0
        ).astype(bf16)


def reduce_chip(parts, shards, owners, own_rows):
    given = []
    for o in range(owners):
        for column in range(2):
            pairs = [
                (shard * owners + k, (shard ^ 2 * column) * owners + (k + o) % owners)
                for shard in range(shards)
                for k in range(owners)
            ]
            part = parts[2 * o + column]
            given.append(lax.ppermute(part, AXES, pairs) if o or column else part)
    levels, rows, rank = parts[0].shape
    spans = rows - own_rows - FACT_ROWS
    lines = -(-2 * len(parts) // FACT_ROWS) * FACT_ROWS
    whole = pl.BlockSpec(memory_space=pltpu.VMEM)
    shape = jax.ShapeDtypeStruct((own_rows + spans * len(parts) + lines, rank), bf16)
    return pl.pallas_call(
        functools.partial(chip_kernel, own_rows=own_rows, spans=spans),
        in_specs=[whole] * len(parts),
        out_specs=[whole] * levels,
        out_shape=[shape] * levels,
        compiler_params=pltpu.CompilerParams(vmem_limit_bytes=VMEM_LIMIT),
        name="chip",
    )(*given)


def reduce_levels(total, shards):
    levels = shards // 4
    terms = [total[0]]
    for up in range(1, levels):
        shift = [(shard, (shard + 4 * up) % shards) for shard in range(shards)]
        terms.append(lax.ppermute(total[up], "loop", shift))
    return terms


def steps_kernel(activity, start_in, subs_in, *refs, shards, levels, slots, cached):
    pieces, refs = refs[:shards], refs[shards:]
    terms_in, refs = refs[:levels], refs[levels:]
    first_out, second_out, third_out, dots_out = refs[:4]
    masks, words, start, terms, subs, table, runs, lines = refs[4:12]
    facts, chosen, places, arrived, moved, given = refs[12:18]
    products = refs[-1]
    own_rows, rank = start.shape
    word_tiles, tile, _ = pieces[0].shape
    sources = lines.shape[0] // levels
    spans = 2 * slots * sources

    gifts = [
        pltpu.make_async_copy(term, terms.at[up], given.at[up]) for up, term in enumerate(terms_in)
    ]
    for copy in gifts:
        copy.start()
    copies = [
        pltpu.make_async_copy(
            piece, words.at[k * word_tiles : (k + 1) * word_tiles], arrived.at[k]
        )
        for k, piece in enumerate(pieces)
    ]
    look = pltpu.make_async_copy(subs_in, subs, moved.at[1])
    look.start()
    begin = pltpu.make_async_copy(start_in, start, moved.at[2])
    begin.start()
    for copy in copies:
        copy.start()
    for copy in gifts:
        copy.wait()

    for up in range(levels):
        rest = terms[up, own_rows + spans :, :].astype(f32)
        lines[up * sources : (up + 1) * sources, :] = rest[:sources].astype(jnp.int32)
    move = pltpu.make_async_copy(lines, facts, moved.at[0])
    move.start()
    rhs = jnp.zeros((own_rows, rank), f32)
    for up in range(levels):
        rhs = rhs + terms[up, :own_rows, :].astype(f32)
        runs[up * spans : (up + 1) * spans, :] = terms[
            up, own_rows : own_rows + spans, :
        ].astype(f32)
    begin.wait()
    look.wait()
    table[...] = subs[...].astype(f32)
    move.wait()

    place = lax.axis_index("loop")
    level, seat = lax.div(place, 4), lax.rem(place, 4)
    wanted = lax.div(lax.axis_index("own") * own_rows, tile) + 1
    chips = shards // 2

    def ring_at(level, column):
        return jnp.where(column == 0, level, chips - 1 - level)

    used = 0
    column = lax.div(seat, 2)
    for up in range(levels):
        there = lax.rem(level - up + levels, levels)
        ahead = [
            lax.rem(ring_at(there, side) - ring_at(level, column) + chips, chips)
            for side in (column, 1 - column)
        ]

        def choose(k, n, up=up, ahead=ahead):
            src = up * sources + k
            side = lax.rem(lax.div(k, 2), 2)
            distance = jnp.where(side == 0, ahead[0], ahead[1])
            places[src] = word_tiles * (2 * distance + lax.rem(k, 2))
            for s in range(slots):
                chosen[n] = src * slots + s
                n = n + jnp.where(facts[src, s] == wanted, 1, 0)
            return n

        used = lax.fori_loop(0, sources, choose, used)
    chunks = lax.div(used + CHUNK - 1, CHUNK)

    offset = lax.rem(lax.axis_index("own") * own_rows, tile)
    pick = (
        lax.broadcasted_iota(jnp.int32, (own_rows, tile), 0) + offset
        == lax.broadcasted_iota(jnp.int32, (own_rows, tile), 1)
    ).astype(f32).astype(bf16)

    def mask(chunk):
        parts = []
        for b in range(CHUNK):
            i = chunk * CHUNK + b
            j = chosen[jnp.minimum(i, used - 1)]
            first = runs[pl.ds(2 * j, 1), :].astype(jnp.int32)
            length = runs[pl.ds(2 * j + 1, 1), :].astype(jnp.int32)
            length = jnp.where(i < used, length, 0)
            parts.append(mask_columns(first, length, tile))
        return dot_nt(pick, jnp.concatenate(parts, axis=0)).astype(bf16)

    def product(i):
        j = chosen[jnp.minimum(i, used - 1)]
        src, s = lax.div(j, slots), lax.rem(j, slots)
        sub = 128 * facts[src, 2 * slots + s] + facts[src, 3 * slots + s]
        rows = words[places[src] + facts[src, slots + s]].astype(f32)
        return (rows * table[pl.ds(sub, 1), :]).astype(bf16)

    for copy in copies:
        copy.wait()

    def gram(vector, build=False):
        rounded = vector.astype(bf16)

        def body(chunk, total):
            if build:
                masks[chunk] = mask(chunk)
            if cached and not build:
                block = products[chunk]
            else:
                block = jnp.concatenate(
                    [product(chunk * CHUNK + b) for b in range(CHUNK)], axis=0
                )
                if cached:
                    products[chunk] = block
            weights = dot_nt(rounded, block).astype(bf16) * masks[chunk]
            return total + dot_nn(weights, block)

        return lax.fori_loop(0, chunks, body, jnp.zeros((own_rows, rank), f32))

    def over_row(a, b):
        return jnp.sum(a * b, axis=1, keepdims=True)

    scale = jnp.broadcast_to(activity[...], (rank, own_rows)).T
    first = scale * (rhs - gram(start[...], build=True)) - ridge * start[...]
    second = scale * gram(first) + ridge * first
    norms, overlaps = over_row(first, first), over_row(first, second)
    share = jnp.where(norms > 0.0, overlaps / jnp.where(norms > 0.0, norms, 1.0), 0.0)
    rest = second - share * first
    third = scale * gram(rest) + ridge * rest + share * second
    first_out[...] = first
    second_out[...] = second
    third_out[...] = third
    rows = [norms, overlaps, over_row(second, second), over_row(first, third), over_row(second, third)]
    lane = lax.broadcasted_iota(jnp.int32, (1, rank), 1)
    line = jnp.zeros((1, rank), f32)
    for k, value in enumerate(rows):
        line = line + jnp.where(lane == k, jnp.sum(value, axis=0, keepdims=True), 0.0)
    dots_out[...] = jnp.broadcast_to(line[None], dots_out.shape)


def krylov(start, activity, subs, pieces, terms, slots, devices):
    own_rows, rank = start.shape
    blocks = devices * slots
    word_tiles, tile, _ = pieces[0].shape
    chunks = -(-blocks // CHUNK)
    cached = blocks * tile * rank * 2 <= 16 * 2**20
    whole = pl.BlockSpec(memory_space=pltpu.VMEM)
    anywhere = pl.BlockSpec(memory_space=pl.ANY)
    vector = jax.ShapeDtypeStruct((own_rows, rank), f32)
    scratch = [
        pltpu.VMEM((chunks, own_rows, CHUNK * tile), bf16),
        pltpu.VMEM((len(pieces) * word_tiles, tile, rank), bf16),
        pltpu.VMEM(start.shape, f32),
        pltpu.VMEM((len(terms),) + terms[0].shape, bf16),
        pltpu.VMEM(subs.shape, bf16),
        pltpu.VMEM(subs.shape, f32),
        pltpu.VMEM((2 * blocks, tile), f32),
        pltpu.VMEM((devices, rank), jnp.int32),
        pltpu.SMEM((devices, rank), jnp.int32),
        pltpu.SMEM((blocks,), jnp.int32),
        pltpu.SMEM((devices,), jnp.int32),
        pltpu.SemaphoreType.DMA((len(pieces),)),
        pltpu.SemaphoreType.DMA((3,)),
        pltpu.SemaphoreType.DMA((len(terms),)),
    ]
    if cached:
        scratch.append(pltpu.VMEM((chunks, CHUNK * tile, rank), bf16))
    return pl.pallas_call(
        functools.partial(
            steps_kernel, shards=len(pieces), levels=len(terms), slots=slots, cached=cached
        ),
        in_specs=[whole] + [anywhere] * (2 + len(pieces) + len(terms)),
        out_specs=[whole] * 4,
        out_shape=[vector, vector, vector, jax.ShapeDtypeStruct((devices, 1, rank), f32)],
        scratch_shapes=scratch,
        compiler_params=pltpu.CompilerParams(vmem_limit_bytes=VMEM_LIMIT),
        name="krylov",
    )(activity, start, subs, *pieces, *terms)


def last_kernel(dots, start, first, second, third, solution_out, residual_out):
    line = dots[0]
    for k in range(1, dots.shape[0]):
        line = line + dots[k]
    rr, rq, qq, rz, qz = (line[:, k : k + 1] for k in range(5))
    step0 = rr / rq
    next_rr = rr - 2.0 * step0 * rq + step0 * step0 * qq
    grow = 1.0 + next_rr / rr
    slope = grow * (grow * rq - step0 * (rz + qq)) + step0 * step0 * qz
    step1 = next_rr / slope
    near, far = step0 + step1 * grow, step1 * step0
    solution_out[...] = start[...] + near * first[...] - far * second[...]
    residual_out[...] = first[...] - near * second[...] + far * third[...]


def last_step(dots, start, first, second, third):
    whole = pl.BlockSpec(memory_space=pltpu.VMEM)
    vector = jax.ShapeDtypeStruct(start.shape, f32)
    return pl.pallas_call(
        last_kernel,
        in_specs=[whole] * 5,
        out_specs=[whole] * 2,
        out_shape=[vector, vector],
        compiler_params=pltpu.CompilerParams(vmem_limit_bytes=VMEM_LIMIT),
        name="last_step",
    )(dots, start, first, second, third)


def ring_round(up, down, held, step, shards):
    chips = shards // 2
    levels = chips // 2
    order = [2 * level for level in range(levels)] + [
        2 * level + 1 for level in reversed(range(levels))
    ]

    def shift(by):
        return [
            (2 * order[p] + core, 2 * order[(p + by) % chips] + core)
            for p in range(chips)
            for core in range(2)
        ]

    up = lax.ppermute(up, "loop", shift(1))
    held[chips - step] = up
    if step < chips - step:
        down = lax.ppermute(down, "loop", shift(-1))
        held[step] = down
    return up, down


def other_core(value, shards):
    return lax.ppermute(value, "loop", [(shard, shard ^ 1) for shard in range(shards)])


def on_device(
    factor_start,
    activity,
    word_factors,
    sub_factors,
    ratings,
    user_tile,
    word_tile,
    subreddit,
    counts,
    runs,
):
    own_rows, rank = factor_start.shape
    owners, shards = lax.axis_size("own"), lax.axis_size("loop")
    slots = ratings.shape[3]
    devices = shards * owners
    chips = shards // 2
    together = lax.optimization_barrier

    scalars = (user_tile[0, 0].T, word_tile[0, 0].T, subreddit[0, 0].T, counts[0])
    mine = word_factors[0]
    held = {0: mine}

    inputs = (scalars, ratings[0, 0], runs[0, 0], mine, sub_factors)
    up, down = ring_round(mine, mine, held, 1, shards)
    (away,) = rhs_sums(*inputs, 1, None, owners, own_rows)
    crossed = {0: other_core(mine, shards)}
    up, down, away, crossed = together((up, down, away, crossed))

    def cross(step):
        for distance in {step, chips - step}:
            crossed[distance] = other_core(held[distance], shards)

    cross(1)
    up, down = ring_round(up, down, held, 2, shards)
    parts = rhs_sums(*inputs, 0, other_core(away, shards), owners, own_rows)
    up, down, parts, crossed = together((up, down, parts, crossed))

    up, down = ring_round(up, down, held, 3, shards)
    total = reduce_chip(parts, shards, owners, own_rows)
    up, down, total = together((up, down, total))

    for step in range(4, chips // 2 + 1):
        up, down = ring_round(up, down, held, step, shards)
    terms = reduce_levels(total, shards)
    held[chips // 2], terms, crossed = together((held[chips // 2], terms, crossed))

    for step in range(2, chips // 2 + 1):
        cross(step)
    pieces = []
    for distance in range(chips):
        pieces += [held[distance], crossed[distance]]
    first, second, third, dots = krylov(
        factor_start, activity[None], sub_factors, pieces, terms, slots, devices
    )
    everyone = lax.all_to_all(dots, AXES, 0, 0, tiled=True)
    return tuple(last_step(everyone, factor_start, first, second, third))


def solution(mesh):
    placed = (
        P(("loop", "own"), None),
        P(("loop", "own")),
        P("loop", None, None, None),
        P(),
        P("loop", "own", None, None, None, None),
        P("loop", "own", None, None),
        P("loop", "own", None, None),
        P("loop", "own", None, None),
        P("loop", "own", None),
        P("loop", "own", None, None, None, None),
    )
    return jax.shard_map(
        on_device,
        mesh=mesh,
        in_specs=placed,
        out_specs=(P(("loop", "own"), None), P(("loop", "own"), None)),
        check_vma=False,
    )
```

```python
import functools

import jax
import jax.numpy as jnp
from jax import lax
from jax.experimental import pallas as pl
from jax.experimental.pallas import tpu as pltpu
from jax.sharding import PartitionSpec as P

AXES = ("loop", "own")
CHUNK = 48
FACT_ROWS = 16
ridge = 0.05
MIB = 2**20
VMEM_LIMIT = 60 * MIB
f32 = jnp.float32
bf16 = jnp.bfloat16


def dot_nt(left, right):
    return lax.dot_general(left, right, (((1,), (1,)), ((), ())), preferred_element_type=f32)


def dot_nn(left, right):
    return jnp.dot(left, right, preferred_element_type=f32)


def mask_columns(first, length, tile):
    column = lax.broadcasted_iota(jnp.int32, (tile, first.shape[-1]), 0)
    inside = ((column - first) & (tile - 1)) < length
    return jnp.where(inside, 1.0, 0.0).astype(bf16)


def fact_line(user_tile, word_tile, subreddit, live, group, slots, rank):
    lane = lax.broadcasted_iota(jnp.int32, (1, rank), 1)
    line = jnp.zeros((1, rank), jnp.int32)
    for s in range(slots):
        sub = subreddit[s, group]
        user = jnp.where(s < live, user_tile[s, group] + 1, 0)
        values = (user, word_tile[s, group], lax.div(sub, 128), lax.rem(sub, 128))
        for k, value in enumerate(values):
            line = jnp.where(lane == k * slots + s, value, line)
    return line.astype(f32)


def rhs_kernel(
    user_tile, word_tile, subreddit, counts, ratings_in, runs_in, words_in, subs_in, *refs,
    half, owners, own_rows,
):
    if half == 0:
        given, refs = refs[0], refs[1:]
    outs, (ratings, runs, words, subs, table, sums, arrived, loaded) = refs[:-8], refs[-8:]
    steps, slots, tile = ratings.shape[0], ratings.shape[1], ratings.shape[2]
    rank = words.shape[-1]
    levels = steps // 2

    place = lax.axis_index("loop")
    level, seat = lax.div(place, 4), lax.rem(place, 4)

    def group_at(step):
        there = lax.rem(seat + 2 * (step // levels), 4)
        if half:
            there = there + 1 - 2 * lax.rem(there, 2)
        return 4 * lax.rem(level + step % levels, levels) + there

    def load(step):
        group = group_at(step)
        return pltpu.make_async_copy(ratings_in.at[group], ratings.at[step], arrived.at[step])

    tables = [
        pltpu.make_async_copy(source, target, loaded.at[k])
        for k, (source, target) in enumerate(
            [(subs_in, subs), (runs_in, runs), (words_in, words)]
        )
    ]
    for copy in tables:
        copy.start()
    for step in range(steps):
        load(step).start()
    tables[0].wait()
    table[...] = subs[...].astype(f32)
    tables[1].wait()
    tables[2].wait()

    eye = (
        lax.broadcasted_iota(jnp.int32, (tile, tile), 0)
        == lax.broadcasted_iota(jnp.int32, (tile, tile), 1)
    ).astype(f32).astype(bf16)
    me = lax.axis_index("own")
    for step in range(steps):
        group = group_at(step)
        live = counts[0, group]
        columns = []
        for s in range(slots):
            pair = runs[group, s]
            columns.append(
                mask_columns(pair[0:1], jnp.where(s < live, pair[1:2], 0), tile)
            )
        seen = dot_nt(eye, jnp.concatenate(columns, axis=0)).astype(bf16)
        load(step).wait()
        sums[step % 2] = jnp.zeros(sums.shape[1:], f32)
        for s in range(slots):
            sub_row = table[pl.ds(subreddit[s, group], 1), :]
            product = (words[word_tile[s, group]].astype(f32) * sub_row).astype(bf16)
            weights = seen[:, s * tile : (s + 1) * tile] * ratings[step, s]
            rows = pl.ds(pl.multiple_of(user_tile[s, group] * tile, tile), tile)
            sums[step % 2, rows, :] += dot_nn(weights, product)
        line = fact_line(user_tile, word_tile, subreddit, live, group, slots, rank)
        spans = jnp.concatenate([runs[group, s] for s in range(slots)], axis=0).astype(f32)
        end = own_rows + 2 * slots
        for o in range(owners):
            owner = lax.rem(me + o, owners)
            rows = pl.ds(pl.multiple_of(owner * own_rows, own_rows), own_rows)
            value = sums[step % 2, rows, :]
            column, up = step // levels, step % levels
            if half == 0:
                other = given[o, column, up].astype(f32)
                value = jnp.concatenate(
                    [
                        value + other[:own_rows],
                        spans,
                        other[own_rows:end],
                        line,
                        other[end : end + 1],
                        jnp.zeros((FACT_ROWS - 2, rank), f32),
                    ],
                    axis=0,
                )
                outs[2 * o + column][up] = value.astype(bf16)
            else:
                value = jnp.concatenate(
                    [value, spans, line, jnp.zeros((FACT_ROWS - 1, rank), f32)], axis=0
                )
                outs[0][o, column, up] = value.astype(bf16)


def rhs_sums(scalars, ratings, runs, words, subs, half, given, owners, own_rows):
    groups, slots, tile, _ = ratings.shape
    rank = words.shape[-1]
    steps, levels = groups // 2, groups // 4
    anywhere = pl.BlockSpec(memory_space=pl.ANY)
    whole = pl.BlockSpec(memory_space=pltpu.VMEM)
    part = (levels, own_rows + 2 * slots * (2 - half) + FACT_ROWS, rank)
    shapes = [part] * (2 * owners) if half == 0 else [(owners, 2) + part]
    return pl.pallas_call(
        functools.partial(rhs_kernel, half=half, owners=owners, own_rows=own_rows),
        in_specs=[pl.BlockSpec(memory_space=pltpu.SMEM)] * 4
        + [anywhere] * 4
        + [whole] * (1 - half),
        out_specs=[whole] * len(shapes),
        out_shape=[jax.ShapeDtypeStruct(shape, bf16) for shape in shapes],
        scratch_shapes=[
            pltpu.VMEM((steps,) + ratings.shape[1:], bf16),
            pltpu.VMEM(runs.shape, jnp.int32),
            pltpu.VMEM(words.shape, bf16),
            pltpu.VMEM(subs.shape, bf16),
            pltpu.VMEM(subs.shape, f32),
            pltpu.VMEM((2, owners * own_rows, rank), f32),
            pltpu.SemaphoreType.DMA((steps,)),
            pltpu.SemaphoreType.DMA((3,)),
        ],
        compiler_params=pltpu.CompilerParams(vmem_limit_bytes=VMEM_LIMIT if half else 50 * MIB),
        cost_estimate=pl.CostEstimate(
            flops=8 * ratings.size * rank, bytes_accessed=8 * ratings.size, transcendentals=0
        ),
        name="rhs",
    )(*scalars, ratings, runs, words, subs, *([given] if half == 0 else []))


def chip_kernel(*refs, own_rows, spans):
    levels, _, rank = refs[0].shape
    parts, outs = refs[:-levels], refs[-levels:]
    lines = outs[0].shape[0] - own_rows - spans * len(parts)
    for up in range(levels):
        total = parts[0][up, :own_rows, :].astype(f32)
        for part in parts[1:]:
            total = total + part[up, :own_rows, :].astype(f32)
        outs[up][:own_rows, :] = total.astype(bf16)
        facts = []
        for k, part in enumerate(parts):
            at = own_rows + spans * k
            outs[up][at : at + spans, :] = part[up, own_rows : own_rows + spans, :]
            facts.append(part[up, own_rows + spans :, :].astype(f32)[:2])
        facts.append(jnp.zeros((lines - 2 * len(parts), rank), f32))
        outs[up][own_rows + spans * len(parts) :, :] = jnp.concatenate(
            facts[: len(facts) - (lines == 2 * len(parts))], axis=0
        ).astype(bf16)


def reduce_chip(parts, shards, owners, own_rows):
    given = []
    for o in range(owners):
        for column in range(2):
            pairs = [
                (shard * owners + k, (shard ^ 2 * column) * owners + (k + o) % owners)
                for shard in range(shards)
                for k in range(owners)
            ]
            part = parts[2 * o + column]
            given.append(lax.ppermute(part, AXES, pairs) if o or column else part)
    levels, rows, rank = parts[0].shape
    spans = rows - own_rows - FACT_ROWS
    lines = -(-2 * len(parts) // FACT_ROWS) * FACT_ROWS
    whole = pl.BlockSpec(memory_space=pltpu.VMEM)
    shape = jax.ShapeDtypeStruct((own_rows + spans * len(parts) + lines, rank), bf16)
    return pl.pallas_call(
        functools.partial(chip_kernel, own_rows=own_rows, spans=spans),
        in_specs=[whole] * len(parts),
        out_specs=[whole] * levels,
        out_shape=[shape] * levels,
        compiler_params=pltpu.CompilerParams(vmem_limit_bytes=16 * MIB),
        name="chip",
    )(*given)


def reduce_levels(total, shards):
    levels = shards // 4
    terms = [total[0]]
    for up in range(1, levels):
        shift = [(shard, (shard + 4 * up) % shards) for shard in range(shards)]
        terms.append(lax.ppermute(total[up], "loop", shift))
    return terms


def steps_kernel(activity, start_in, subs_in, *refs, shards, levels, slots, cached):
    pieces, refs = refs[:shards], refs[shards:]
    terms_in, refs = refs[:levels], refs[levels:]
    first_out, second_out, third_out, dots_out = refs[:4]
    masks, words, start, terms, subs, table, runs, lines = refs[4:12]
    facts, chosen, places, arrived, moved, given = refs[12:18]
    products = refs[-1]
    own_rows, rank = start.shape
    word_tiles, tile, _ = pieces[0].shape
    sources = lines.shape[0] // levels
    spans = 2 * slots * sources

    gifts = [
        pltpu.make_async_copy(term, terms.at[up], given.at[up]) for up, term in enumerate(terms_in)
    ]
    for copy in gifts:
        copy.start()
    copies = [
        pltpu.make_async_copy(
            piece, words.at[k * word_tiles : (k + 1) * word_tiles], arrived.at[k]
        )
        for k, piece in enumerate(pieces)
    ]
    look = pltpu.make_async_copy(subs_in, subs, moved.at[1])
    look.start()
    begin = pltpu.make_async_copy(start_in, start, moved.at[2])
    begin.start()
    for copy in copies:
        copy.start()
    for copy in gifts:
        copy.wait()

    for up in range(levels):
        rest = terms[up, own_rows + spans :, :].astype(f32)
        lines[up * sources : (up + 1) * sources, :] = rest[:sources].astype(jnp.int32)
    move = pltpu.make_async_copy(lines, facts, moved.at[0])
    move.start()
    rhs = jnp.zeros((own_rows, rank), f32)
    for up in range(levels):
        rhs = rhs + terms[up, :own_rows, :].astype(f32)
        runs[up * spans : (up + 1) * spans, :] = terms[
            up, own_rows : own_rows + spans, :
        ].astype(f32)
    begin.wait()
    look.wait()
    table[...] = subs[...].astype(f32)
    move.wait()

    place = lax.axis_index("loop")
    level, seat = lax.div(place, 4), lax.rem(place, 4)
    wanted = lax.div(lax.axis_index("own") * own_rows, tile) + 1
    chips = shards // 2

    def ring_at(level, column):
        return jnp.where(column == 0, level, chips - 1 - level)

    used = 0
    column = lax.div(seat, 2)
    for up in range(levels):
        there = lax.rem(level - up + levels, levels)
        ahead = [
            lax.rem(ring_at(there, side) - ring_at(level, column) + chips, chips)
            for side in (column, 1 - column)
        ]

        def choose(k, n, up=up, ahead=ahead):
            src = up * sources + k
            side = lax.rem(lax.div(k, 2), 2)
            distance = jnp.where(side == 0, ahead[0], ahead[1])
            places[src] = word_tiles * (2 * distance + lax.rem(k, 2))
            for s in range(slots):
                chosen[n] = src * slots + s
                n = n + jnp.where(facts[src, s] == wanted, 1, 0)
            return n

        used = lax.fori_loop(0, sources, choose, used)
    chunks = lax.div(used + CHUNK - 1, CHUNK)

    offset = lax.rem(lax.axis_index("own") * own_rows, tile)
    pick = (
        lax.broadcasted_iota(jnp.int32, (own_rows, tile), 0) + offset
        == lax.broadcasted_iota(jnp.int32, (own_rows, tile), 1)
    ).astype(f32).astype(bf16)

    def mask(chunk):
        parts = []
        for b in range(CHUNK):
            i = chunk * CHUNK + b
            j = chosen[jnp.minimum(i, used - 1)]
            first = runs[pl.ds(2 * j, 1), :].astype(jnp.int32)
            length = runs[pl.ds(2 * j + 1, 1), :].astype(jnp.int32)
            length = jnp.where(i < used, length, 0)
            parts.append(mask_columns(first, length, tile))
        return dot_nt(pick, jnp.concatenate(parts, axis=0)).astype(bf16)

    def product(i):
        j = chosen[jnp.minimum(i, used - 1)]
        src, s = lax.div(j, slots), lax.rem(j, slots)
        sub = 128 * facts[src, 2 * slots + s] + facts[src, 3 * slots + s]
        rows = words[places[src] + facts[src, slots + s]].astype(f32)
        return (rows * table[pl.ds(sub, 1), :]).astype(bf16)

    for copy in copies:
        copy.wait()

    def gram(vector, build=False):
        rounded = vector.astype(bf16)

        def body(chunk, total):
            if build:
                masks[chunk] = mask(chunk)
            if cached and not build:
                block = products[chunk]
            else:
                block = jnp.concatenate(
                    [product(chunk * CHUNK + b) for b in range(CHUNK)], axis=0
                )
                if cached:
                    products[chunk] = block
            weights = dot_nt(rounded, block).astype(bf16) * masks[chunk]
            return total + dot_nn(weights, block)

        return lax.fori_loop(0, chunks, body, jnp.zeros((own_rows, rank), f32))

    def over_row(a, b):
        return jnp.sum(a * b, axis=1, keepdims=True)

    scale = jnp.broadcast_to(activity[...], (rank, own_rows)).T
    first = scale * (rhs - gram(start[...], build=True)) - ridge * start[...]
    second = scale * gram(first) + ridge * first
    norms, overlaps = over_row(first, first), over_row(first, second)
    share = jnp.where(norms > 0.0, overlaps / jnp.where(norms > 0.0, norms, 1.0), 0.0)
    rest = second - share * first
    third = scale * gram(rest) + ridge * rest + share * second
    first_out[...] = first
    second_out[...] = second
    third_out[...] = third
    rows = [norms, overlaps, over_row(second, second), over_row(first, third), over_row(second, third)]
    lane = lax.broadcasted_iota(jnp.int32, (1, rank), 1)
    line = jnp.zeros((1, rank), f32)
    for k, value in enumerate(rows):
        line = line + jnp.where(lane == k, jnp.sum(value, axis=0, keepdims=True), 0.0)
    dots_out[...] = jnp.broadcast_to(line[None], dots_out.shape)


def krylov(start, activity, subs, pieces, terms, slots, devices):
    own_rows, rank = start.shape
    blocks = devices * slots
    word_tiles, tile, _ = pieces[0].shape
    chunks = -(-blocks // CHUNK)
    cached = blocks * tile * rank * 2 <= 16 * 2**20
    whole = pl.BlockSpec(memory_space=pltpu.VMEM)
    anywhere = pl.BlockSpec(memory_space=pl.ANY)
    vector = jax.ShapeDtypeStruct((own_rows, rank), f32)
    scratch = [
        pltpu.VMEM((chunks, own_rows, CHUNK * tile), bf16),
        pltpu.VMEM((len(pieces) * word_tiles, tile, rank), bf16),
        pltpu.VMEM(start.shape, f32),
        pltpu.VMEM((len(terms),) + terms[0].shape, bf16),
        pltpu.VMEM(subs.shape, bf16),
        pltpu.VMEM(subs.shape, f32),
        pltpu.VMEM((2 * blocks, tile), f32),
        pltpu.VMEM((devices, rank), jnp.int32),
        pltpu.SMEM((devices, rank), jnp.int32),
        pltpu.SMEM((blocks,), jnp.int32),
        pltpu.SMEM((devices,), jnp.int32),
        pltpu.SemaphoreType.DMA((len(pieces),)),
        pltpu.SemaphoreType.DMA((3,)),
        pltpu.SemaphoreType.DMA((len(terms),)),
    ]
    if cached:
        scratch.append(pltpu.VMEM((chunks, CHUNK * tile, rank), bf16))
    return pl.pallas_call(
        functools.partial(
            steps_kernel, shards=len(pieces), levels=len(terms), slots=slots, cached=cached
        ),
        in_specs=[whole] + [anywhere] * (2 + len(pieces) + len(terms)),
        out_specs=[whole] * 4,
        out_shape=[vector, vector, vector, jax.ShapeDtypeStruct((devices, 1, rank), f32)],
        scratch_shapes=scratch,
        compiler_params=pltpu.CompilerParams(vmem_limit_bytes=44 * MIB),
        name="krylov",
    )(activity, start, subs, *pieces, *terms)


def last_kernel(dots, start, first, second, third, solution_out, residual_out):
    line = dots[0]
    for k in range(1, dots.shape[0]):
        line = line + dots[k]
    rr, rq, qq, rz, qz = (line[:, k : k + 1] for k in range(5))
    step0 = rr / rq
    next_rr = rr - 2.0 * step0 * rq + step0 * step0 * qq
    grow = 1.0 + next_rr / rr
    slope = grow * (grow * rq - step0 * (rz + qq)) + step0 * step0 * qz
    step1 = next_rr / slope
    near, far = step0 + step1 * grow, step1 * step0
    solution_out[...] = start[...] + near * first[...] - far * second[...]
    residual_out[...] = first[...] - near * second[...] + far * third[...]


def last_step(dots, start, first, second, third):
    whole = pl.BlockSpec(memory_space=pltpu.VMEM)
    vector = jax.ShapeDtypeStruct(start.shape, f32)
    return pl.pallas_call(
        last_kernel,
        in_specs=[whole] * 5,
        out_specs=[whole] * 2,
        out_shape=[vector, vector],
        compiler_params=pltpu.CompilerParams(vmem_limit_bytes=8 * MIB),
        name="last_step",
    )(dots, start, first, second, third)


def ring_round(up, down, held, step, shards):
    chips = shards // 2
    levels = chips // 2
    order = [2 * level for level in range(levels)] + [
        2 * level + 1 for level in reversed(range(levels))
    ]

    def shift(by):
        return [
            (2 * order[p] + core, 2 * order[(p + by) % chips] + core)
            for p in range(chips)
            for core in range(2)
        ]

    up = lax.ppermute(up, "loop", shift(1))
    held[chips - step] = up
    if step < chips - step:
        down = lax.ppermute(down, "loop", shift(-1))
        held[step] = down
    return up, down


def other_core(value, shards):
    return lax.ppermute(value, "loop", [(shard, shard ^ 1) for shard in range(shards)])


def on_device(
    factor_start,
    activity,
    word_factors,
    sub_factors,
    ratings,
    user_tile,
    word_tile,
    subreddit,
    counts,
    runs,
):
    own_rows, rank = factor_start.shape
    owners, shards = lax.axis_size("own"), lax.axis_size("loop")
    slots = ratings.shape[3]
    devices = shards * owners
    chips = shards // 2
    together = lax.optimization_barrier

    scalars = (user_tile[0, 0].T, word_tile[0, 0].T, subreddit[0, 0].T, counts[0])
    mine = word_factors[0]
    held = {0: mine}

    inputs = (scalars, ratings[0, 0], runs[0, 0], mine, sub_factors)
    up, down = ring_round(mine, mine, held, 1, shards)
    (away,) = rhs_sums(*inputs, 1, None, owners, own_rows)
    crossed = {0: other_core(mine, shards)}
    up, down, away, crossed = together((up, down, away, crossed))

    def cross(step):
        for distance in {step, chips - step}:
            crossed[distance] = other_core(held[distance], shards)

    cross(1)
    up, down = ring_round(up, down, held, 2, shards)
    parts = rhs_sums(*inputs, 0, other_core(away, shards), owners, own_rows)
    up, down, parts, crossed = together((up, down, parts, crossed))

    up, down = ring_round(up, down, held, 3, shards)
    total = reduce_chip(parts, shards, owners, own_rows)
    up, down, total = together((up, down, total))

    for step in range(4, chips // 2 + 1):
        up, down = ring_round(up, down, held, step, shards)
    terms = reduce_levels(total, shards)
    held[chips // 2], terms, crossed = together((held[chips // 2], terms, crossed))

    for step in range(2, chips // 2 + 1):
        cross(step)
    pieces = []
    for distance in range(chips):
        pieces += [held[distance], crossed[distance]]
    first, second, third, dots = krylov(
        factor_start, activity[None], sub_factors, pieces, terms, slots, devices
    )
    everyone = lax.all_to_all(dots, AXES, 0, 0, tiled=True)
    return tuple(last_step(everyone, factor_start, first, second, third))


def solution(mesh):
    placed = (
        P(("loop", "own"), None),
        P(("loop", "own")),
        P("loop", None, None, None),
        P(),
        P("loop", "own", None, None, None, None),
        P("loop", "own", None, None),
        P("loop", "own", None, None),
        P("loop", "own", None, None),
        P("loop", "own", None),
        P("loop", "own", None, None, None, None),
    )
    return jax.shard_map(
        on_device,
        mesh=mesh,
        in_specs=placed,
        out_specs=(P(("loop", "own"), None), P(("loop", "own"), None)),
        check_vma=False,
    )
```

```python
import functools

import jax
import jax.numpy as jnp
from jax import lax
from jax.experimental import pallas as pl
from jax.experimental.pallas import tpu as pltpu
from jax.sharding import PartitionSpec as P

AXES = ("loop", "own")
CHUNK = 48
FACT_ROWS = 16
ridge = 0.05
MIB = 2**20
VMEM_LIMIT = 60 * MIB
f32 = jnp.float32
bf16 = jnp.bfloat16


def dot_nt(left, right):
    return lax.dot_general(left, right, (((1,), (1,)), ((), ())), preferred_element_type=f32)


def dot_nn(left, right):
    return jnp.dot(left, right, preferred_element_type=f32)


def mask_columns(first, length, tile):
    column = lax.broadcasted_iota(jnp.int32, (tile, first.shape[-1]), 0)
    inside = ((column - first) & (tile - 1)) < length
    return jnp.where(inside, 1.0, 0.0).astype(bf16)


def fact_line(user_tile, word_tile, subreddit, live, group, slots, rank):
    lane = lax.broadcasted_iota(jnp.int32, (1, rank), 1)
    line = jnp.zeros((1, rank), jnp.int32)
    for s in range(slots):
        sub = subreddit[s, group]
        user = jnp.where(s < live, user_tile[s, group] + 1, 0)
        values = (user, word_tile[s, group], lax.div(sub, 128), lax.rem(sub, 128))
        for k, value in enumerate(values):
            line = jnp.where(lane == k * slots + s, value, line)
    return line.astype(f32)


def rhs_kernel(
    user_tile, word_tile, subreddit, counts, ratings_in, runs_in, words_in, subs_in, *refs,
    half, owners, own_rows,
):
    if half == 0:
        given, refs = refs[0], refs[1:]
    outs, (ratings, runs, words, subs, table, sums, arrived, loaded) = refs[:-8], refs[-8:]
    steps, slots, tile = ratings.shape[0], ratings.shape[1], ratings.shape[2]
    rank = words.shape[-1]
    levels = steps // 2

    place = lax.axis_index("loop")
    level, seat = lax.div(place, 4), lax.rem(place, 4)

    def group_at(step):
        there = lax.rem(seat + 2 * (step // levels), 4)
        if half:
            there = there + 1 - 2 * lax.rem(there, 2)
        return 4 * lax.rem(level + step % levels, levels) + there

    def load(step):
        group = group_at(step)
        return pltpu.make_async_copy(ratings_in.at[group], ratings.at[step], arrived.at[step])

    tables = [
        pltpu.make_async_copy(source, target, loaded.at[k])
        for k, (source, target) in enumerate(
            [(subs_in, subs), (runs_in, runs), (words_in, words)]
        )
    ]
    for copy in tables:
        copy.start()
    for step in range(steps):
        load(step).start()
    tables[0].wait()
    table[...] = subs[...].astype(f32)
    tables[1].wait()
    tables[2].wait()

    eye = (
        lax.broadcasted_iota(jnp.int32, (tile, tile), 0)
        == lax.broadcasted_iota(jnp.int32, (tile, tile), 1)
    ).astype(f32).astype(bf16)
    me = lax.axis_index("own")
    for step in range(steps):
        group = group_at(step)
        live = counts[0, group]
        columns = []
        for s in range(slots):
            pair = runs[group, s]
            columns.append(
                mask_columns(pair[0:1], jnp.where(s < live, pair[1:2], 0), tile)
            )
        seen = dot_nt(eye, jnp.concatenate(columns, axis=0)).astype(bf16)
        load(step).wait()
        sums[step % 2] = jnp.zeros(sums.shape[1:], f32)
        for s in range(slots):
            sub_row = table[pl.ds(subreddit[s, group], 1), :]
            product = (words[word_tile[s, group]].astype(f32) * sub_row).astype(bf16)
            weights = seen[:, s * tile : (s + 1) * tile] * ratings[step, s]
            rows = pl.ds(pl.multiple_of(user_tile[s, group] * tile, tile), tile)
            sums[step % 2, rows, :] += dot_nn(weights, product)
        line = fact_line(user_tile, word_tile, subreddit, live, group, slots, rank)
        spans = jnp.concatenate([runs[group, s] for s in range(slots)], axis=0).astype(f32)
        end = own_rows + 2 * slots
        for o in range(owners):
            owner = lax.rem(me + o, owners)
            rows = pl.ds(pl.multiple_of(owner * own_rows, own_rows), own_rows)
            value = sums[step % 2, rows, :]
            column, up = step // levels, step % levels
            if half == 0:
                other = given[o, column, up].astype(f32)
                value = jnp.concatenate(
                    [
                        value + other[:own_rows],
                        spans,
                        other[own_rows:end],
                        line,
                        other[end : end + 1],
                        jnp.zeros((FACT_ROWS - 2, rank), f32),
                    ],
                    axis=0,
                )
                outs[2 * o + column][up] = value.astype(bf16)
            else:
                value = jnp.concatenate(
                    [value, spans, line, jnp.zeros((FACT_ROWS - 1, rank), f32)], axis=0
                )
                outs[0][o, column, up] = value.astype(bf16)


def rhs_sums(scalars, ratings, runs, words, subs, half, given, owners, own_rows):
    groups, slots, tile, _ = ratings.shape
    rank = words.shape[-1]
    steps, levels = groups // 2, groups // 4
    anywhere = pl.BlockSpec(memory_space=pl.ANY)
    whole = pl.BlockSpec(memory_space=pltpu.VMEM)
    part = (levels, own_rows + 2 * slots * (2 - half) + FACT_ROWS, rank)
    shapes = [part] * (2 * owners) if half == 0 else [(owners, 2) + part]
    return pl.pallas_call(
        functools.partial(rhs_kernel, half=half, owners=owners, own_rows=own_rows),
        in_specs=[pl.BlockSpec(memory_space=pltpu.SMEM)] * 4
        + [anywhere] * 4
        + [whole] * (1 - half),
        out_specs=[whole] * len(shapes),
        out_shape=[jax.ShapeDtypeStruct(shape, bf16) for shape in shapes],
        scratch_shapes=[
            pltpu.VMEM((steps,) + ratings.shape[1:], bf16),
            pltpu.VMEM(runs.shape, jnp.int32),
            pltpu.VMEM(words.shape, bf16),
            pltpu.VMEM(subs.shape, bf16),
            pltpu.VMEM(subs.shape, f32),
            pltpu.VMEM((2, owners * own_rows, rank), f32),
            pltpu.SemaphoreType.DMA((steps,)),
            pltpu.SemaphoreType.DMA((3,)),
        ],
        compiler_params=pltpu.CompilerParams(vmem_limit_bytes=VMEM_LIMIT if half else 50 * MIB),
        cost_estimate=pl.CostEstimate(
            flops=8 * ratings.size * rank, bytes_accessed=8 * ratings.size, transcendentals=0
        ),
        name="rhs",
    )(*scalars, ratings, runs, words, subs, *([given] if half == 0 else []))


def chip_kernel(*refs, own_rows, spans):
    levels, _, rank = refs[0].shape
    parts, outs = refs[:-levels], refs[-levels:]
    lines = outs[0].shape[0] - own_rows - spans * len(parts)
    for up in range(levels):
        total = parts[0][up, :own_rows, :].astype(f32)
        for part in parts[1:]:
            total = total + part[up, :own_rows, :].astype(f32)
        outs[up][:own_rows, :] = total.astype(bf16)
        facts = []
        for k, part in enumerate(parts):
            at = own_rows + spans * k
            outs[up][at : at + spans, :] = part[up, own_rows : own_rows + spans, :]
            facts.append(part[up, own_rows + spans :, :].astype(f32)[:2])
        facts.append(jnp.zeros((lines - 2 * len(parts), rank), f32))
        outs[up][own_rows + spans * len(parts) :, :] = jnp.concatenate(
            facts[: len(facts) - (lines == 2 * len(parts))], axis=0
        ).astype(bf16)


def reduce_chip(parts, shards, owners, own_rows):
    given = []
    for o in range(owners):
        for column in range(2):
            pairs = [
                (shard * owners + k, (shard ^ 2 * column) * owners + (k + o) % owners)
                for shard in range(shards)
                for k in range(owners)
            ]
            part = parts[2 * o + column]
            given.append(lax.ppermute(part, AXES, pairs) if o or column else part)
    levels, rows, rank = parts[0].shape
    spans = rows - own_rows - FACT_ROWS
    lines = -(-2 * len(parts) // FACT_ROWS) * FACT_ROWS
    whole = pl.BlockSpec(memory_space=pltpu.VMEM)
    shape = jax.ShapeDtypeStruct((own_rows + spans * len(parts) + lines, rank), bf16)
    return pl.pallas_call(
        functools.partial(chip_kernel, own_rows=own_rows, spans=spans),
        in_specs=[whole] * len(parts),
        out_specs=[whole] * levels,
        out_shape=[shape] * levels,
        compiler_params=pltpu.CompilerParams(vmem_limit_bytes=16 * MIB),
        name="chip",
    )(*given)


def reduce_levels(total, shards):
    levels = shards // 4
    terms = [total[0]]
    for up in range(1, levels):
        shift = [(shard, (shard + 4 * up) % shards) for shard in range(shards)]
        terms.append(lax.ppermute(total[up], "loop", shift))
    return terms


def steps_kernel(activity, start_in, subs_in, *refs, count, word_tiles, levels, slots, cached):
    pieces, refs = refs[:count], refs[count:]
    terms_in, refs = refs[:levels], refs[levels:]
    first_out, second_out, third_out, dots_out = refs[:4]
    masks, words, start, terms, subs, table, runs, lines = refs[4:12]
    facts, chosen, places, arrived, moved, given = refs[12:18]
    products = refs[-1]
    own_rows, rank = start.shape
    _, tile, _ = pieces[0].shape
    sources = lines.shape[0] // levels
    spans = 2 * slots * sources

    gifts = [
        pltpu.make_async_copy(term, terms.at[up], given.at[up]) for up, term in enumerate(terms_in)
    ]
    for copy in gifts:
        copy.start()
    copies, at = [], 0
    for k, piece in enumerate(pieces):
        place = words.at[at : at + piece.shape[0]]
        copies.append(pltpu.make_async_copy(piece, place, arrived.at[k]))
        at += piece.shape[0]
    look = pltpu.make_async_copy(subs_in, subs, moved.at[1])
    look.start()
    begin = pltpu.make_async_copy(start_in, start, moved.at[2])
    begin.start()
    for copy in copies:
        copy.start()
    for copy in gifts:
        copy.wait()

    for up in range(levels):
        rest = terms[up, own_rows + spans :, :].astype(f32)
        lines[up * sources : (up + 1) * sources, :] = rest[:sources].astype(jnp.int32)
    move = pltpu.make_async_copy(lines, facts, moved.at[0])
    move.start()
    rhs = jnp.zeros((own_rows, rank), f32)
    for up in range(levels):
        rhs = rhs + terms[up, :own_rows, :].astype(f32)
        runs[up * spans : (up + 1) * spans, :] = terms[
            up, own_rows : own_rows + spans, :
        ].astype(f32)
    begin.wait()
    look.wait()
    table[...] = subs[...].astype(f32)
    move.wait()

    place = lax.axis_index("loop")
    level, seat = lax.div(place, 4), lax.rem(place, 4)
    wanted = lax.div(lax.axis_index("own") * own_rows, tile) + 1
    chips = at // word_tiles // 2

    def ring_at(level, column):
        return jnp.where(column == 0, level, chips - 1 - level)

    used = 0
    column = lax.div(seat, 2)
    for up in range(levels):
        there = lax.rem(level - up + levels, levels)
        ahead = [
            lax.rem(ring_at(there, side) - ring_at(level, column) + chips, chips)
            for side in (column, 1 - column)
        ]

        def choose(k, n, up=up, ahead=ahead):
            src = up * sources + k
            side = lax.rem(lax.div(k, 2), 2)
            distance = jnp.where(side == 0, ahead[0], ahead[1])
            places[src] = word_tiles * (2 * distance + lax.rem(k, 2))
            for s in range(slots):
                chosen[n] = src * slots + s
                n = n + jnp.where(facts[src, s] == wanted, 1, 0)
            return n

        used = lax.fori_loop(0, sources, choose, used)
    chunks = lax.div(used + CHUNK - 1, CHUNK)

    offset = lax.rem(lax.axis_index("own") * own_rows, tile)
    pick = (
        lax.broadcasted_iota(jnp.int32, (own_rows, tile), 0) + offset
        == lax.broadcasted_iota(jnp.int32, (own_rows, tile), 1)
    ).astype(f32).astype(bf16)

    def mask(chunk):
        parts = []
        for b in range(CHUNK):
            i = chunk * CHUNK + b
            j = chosen[jnp.minimum(i, used - 1)]
            first = runs[pl.ds(2 * j, 1), :].astype(jnp.int32)
            length = runs[pl.ds(2 * j + 1, 1), :].astype(jnp.int32)
            length = jnp.where(i < used, length, 0)
            parts.append(mask_columns(first, length, tile))
        return dot_nt(pick, jnp.concatenate(parts, axis=0)).astype(bf16)

    def product(i):
        j = chosen[jnp.minimum(i, used - 1)]
        src, s = lax.div(j, slots), lax.rem(j, slots)
        sub = 128 * facts[src, 2 * slots + s] + facts[src, 3 * slots + s]
        rows = words[places[src] + facts[src, slots + s]].astype(f32)
        return (rows * table[pl.ds(sub, 1), :]).astype(bf16)

    for copy in copies:
        copy.wait()

    def gram(vector, build=False):
        rounded = vector.astype(bf16)

        def body(chunk, total):
            if build:
                masks[chunk] = mask(chunk)
            if cached and not build:
                block = products[chunk]
            else:
                block = jnp.concatenate(
                    [product(chunk * CHUNK + b) for b in range(CHUNK)], axis=0
                )
                if cached:
                    products[chunk] = block
            weights = dot_nt(rounded, block).astype(bf16) * masks[chunk]
            return total + dot_nn(weights, block)

        return lax.fori_loop(0, chunks, body, jnp.zeros((own_rows, rank), f32))

    def over_row(a, b):
        return jnp.sum(a * b, axis=1, keepdims=True)

    scale = jnp.broadcast_to(activity[...], (rank, own_rows)).T
    first = scale * (rhs - gram(start[...], build=True)) - ridge * start[...]
    second = scale * gram(first) + ridge * first
    norms, overlaps = over_row(first, first), over_row(first, second)
    share = jnp.where(norms > 0.0, overlaps / jnp.where(norms > 0.0, norms, 1.0), 0.0)
    rest = second - share * first
    third = scale * gram(rest) + ridge * rest + share * second
    first_out[...] = first
    second_out[...] = second
    third_out[...] = third
    rows = [norms, overlaps, over_row(second, second), over_row(first, third), over_row(second, third)]
    lane = lax.broadcasted_iota(jnp.int32, (1, rank), 1)
    line = jnp.zeros((1, rank), f32)
    for k, value in enumerate(rows):
        line = line + jnp.where(lane == k, jnp.sum(value, axis=0, keepdims=True), 0.0)
    dots_out[...] = jnp.broadcast_to(line[None], dots_out.shape)


def krylov(start, activity, subs, pieces, terms, word_tiles, slots, devices):
    own_rows, rank = start.shape
    blocks = devices * slots
    _, tile, _ = pieces[0].shape
    chunks = -(-blocks // CHUNK)
    cached = blocks * tile * rank * 2 <= 16 * 2**20
    whole = pl.BlockSpec(memory_space=pltpu.VMEM)
    anywhere = pl.BlockSpec(memory_space=pl.ANY)
    vector = jax.ShapeDtypeStruct((own_rows, rank), f32)
    scratch = [
        pltpu.VMEM((chunks, own_rows, CHUNK * tile), bf16),
        pltpu.VMEM((sum(piece.shape[0] for piece in pieces), tile, rank), bf16),
        pltpu.VMEM(start.shape, f32),
        pltpu.VMEM((len(terms),) + terms[0].shape, bf16),
        pltpu.VMEM(subs.shape, bf16),
        pltpu.VMEM(subs.shape, f32),
        pltpu.VMEM((2 * blocks, tile), f32),
        pltpu.VMEM((devices, rank), jnp.int32),
        pltpu.SMEM((devices, rank), jnp.int32),
        pltpu.SMEM((blocks,), jnp.int32),
        pltpu.SMEM((devices,), jnp.int32),
        pltpu.SemaphoreType.DMA((len(pieces),)),
        pltpu.SemaphoreType.DMA((3,)),
        pltpu.SemaphoreType.DMA((len(terms),)),
    ]
    if cached:
        scratch.append(pltpu.VMEM((chunks, CHUNK * tile, rank), bf16))
    return pl.pallas_call(
        functools.partial(
            steps_kernel,
            count=len(pieces),
            word_tiles=word_tiles,
            levels=len(terms),
            slots=slots,
            cached=cached,
        ),
        in_specs=[whole] + [anywhere] * (2 + len(pieces) + len(terms)),
        out_specs=[whole] * 4,
        out_shape=[vector, vector, vector, jax.ShapeDtypeStruct((devices, 1, rank), f32)],
        scratch_shapes=scratch,
        compiler_params=pltpu.CompilerParams(vmem_limit_bytes=44 * MIB),
        name="krylov",
    )(activity, start, subs, *pieces, *terms)


def last_kernel(dots, start, first, second, third, solution_out, residual_out):
    line = dots[0]
    for k in range(1, dots.shape[0]):
        line = line + dots[k]
    rr, rq, qq, rz, qz = (line[:, k : k + 1] for k in range(5))
    step0 = rr / rq
    next_rr = rr - 2.0 * step0 * rq + step0 * step0 * qq
    grow = 1.0 + next_rr / rr
    slope = grow * (grow * rq - step0 * (rz + qq)) + step0 * step0 * qz
    step1 = next_rr / slope
    near, far = step0 + step1 * grow, step1 * step0
    solution_out[...] = start[...] + near * first[...] - far * second[...]
    residual_out[...] = first[...] - near * second[...] + far * third[...]


def last_step(dots, start, first, second, third):
    whole = pl.BlockSpec(memory_space=pltpu.VMEM)
    vector = jax.ShapeDtypeStruct(start.shape, f32)
    return pl.pallas_call(
        last_kernel,
        in_specs=[whole] * 5,
        out_specs=[whole] * 2,
        out_shape=[vector, vector],
        compiler_params=pltpu.CompilerParams(vmem_limit_bytes=8 * MIB),
        name="last_step",
    )(dots, start, first, second, third)


def ring_round(up, down, held, step, shards):
    chips = shards // 2
    levels = chips // 2
    order = [2 * level for level in range(levels)] + [
        2 * level + 1 for level in reversed(range(levels))
    ]

    def shift(by):
        return [
            (2 * order[p] + core, 2 * order[(p + by) % chips] + core)
            for p in range(chips)
            for core in range(2)
        ]

    if step == chips - step:
        half = up.shape[0] // 2
        up = lax.ppermute(up[:half], "loop", shift(1))
        down = lax.ppermute(down[half:], "loop", shift(-1))
        held[step] = (up, down)
    else:
        up = lax.ppermute(up, "loop", shift(1))
        down = lax.ppermute(down, "loop", shift(-1))
        held[chips - step], held[step] = (up,), (down,)
    return up, down


def other_core(values, shards):
    pairs = [(shard, shard ^ 1) for shard in range(shards)]
    return tuple(lax.ppermute(value, "loop", pairs) for value in values)


def on_device(
    factor_start,
    activity,
    word_factors,
    sub_factors,
    ratings,
    user_tile,
    word_tile,
    subreddit,
    counts,
    runs,
):
    own_rows, rank = factor_start.shape
    owners, shards = lax.axis_size("own"), lax.axis_size("loop")
    slots = ratings.shape[3]
    devices = shards * owners
    chips = shards // 2
    together = lax.optimization_barrier

    scalars = (user_tile[0, 0].T, word_tile[0, 0].T, subreddit[0, 0].T, counts[0])
    mine = word_factors[0]
    held = {0: (mine,)}

    inputs = (scalars, ratings[0, 0], runs[0, 0], mine, sub_factors)
    up, down = ring_round(mine, mine, held, 1, shards)
    (away,) = rhs_sums(*inputs, 1, None, owners, own_rows)
    crossed = {0: other_core(held[0], shards)}
    up, down, away, crossed = together((up, down, away, crossed))

    def cross(step):
        for distance in {step, chips - step}:
            crossed[distance] = other_core(held[distance], shards)

    cross(1)
    up, down = ring_round(up, down, held, 2, shards)
    (given,) = other_core((away,), shards)
    parts = rhs_sums(*inputs, 0, given, owners, own_rows)
    up, down, parts, crossed = together((up, down, parts, crossed))

    up, down = ring_round(up, down, held, 3, shards)
    total = reduce_chip(parts, shards, owners, own_rows)
    up, down, total, held = together((up, down, total, held))

    for step in range(4, chips // 2 + 1):
        up, down = ring_round(up, down, held, step, shards)
    terms = reduce_levels(total, shards)
    held[chips // 2], terms, crossed = together((held[chips // 2], terms, crossed))

    for step in range(2, chips // 2 + 1):
        cross(step)
    pieces = []
    for distance in range(chips):
        pieces += held[distance] + crossed[distance]
    first, second, third, dots = krylov(
        factor_start, activity[None], sub_factors, pieces, terms, mine.shape[0], slots, devices
    )
    everyone = lax.all_to_all(dots, AXES, 0, 0, tiled=True)
    return tuple(last_step(everyone, factor_start, first, second, third))


def solution(mesh):
    placed = (
        P(("loop", "own"), None),
        P(("loop", "own")),
        P("loop", None, None, None),
        P(),
        P("loop", "own", None, None, None, None),
        P("loop", "own", None, None),
        P("loop", "own", None, None),
        P("loop", "own", None, None),
        P("loop", "own", None),
        P("loop", "own", None, None, None, None),
    )
    return jax.shard_map(
        on_device,
        mesh=mesh,
        in_specs=placed,
        out_specs=(P(("loop", "own"), None), P(("loop", "own"), None)),
        check_vma=False,
    )
```

```python
import functools

import jax
import jax.numpy as jnp
from jax import lax
from jax.experimental import pallas as pl
from jax.experimental.pallas import tpu as pltpu
from jax.sharding import PartitionSpec as P

AXES = ("loop", "own")
CHUNK = 48
FACT_ROWS = 16
ridge = 0.05
MIB = 2**20
VMEM_LIMIT = 60 * MIB
f32 = jnp.float32
bf16 = jnp.bfloat16


def dot_nt(left, right):
    return lax.dot_general(left, right, (((1,), (1,)), ((), ())), preferred_element_type=f32)


def dot_nn(left, right):
    return jnp.dot(left, right, preferred_element_type=f32)


def mask_columns(first, length, tile):
    column = lax.broadcasted_iota(jnp.int32, (tile, first.shape[-1]), 0)
    inside = ((column - first) & (tile - 1)) < length
    return jnp.where(inside, 1.0, 0.0).astype(bf16)


def fact_line(user_tile, word_tile, subreddit, live, group, slots, rank):
    lane = lax.broadcasted_iota(jnp.int32, (1, rank), 1)
    line = jnp.zeros((1, rank), jnp.int32)
    for s in range(slots):
        sub = subreddit[s, group]
        user = jnp.where(s < live, user_tile[s, group] + 1, 0)
        values = (user, word_tile[s, group], lax.div(sub, 128), lax.rem(sub, 128))
        for k, value in enumerate(values):
            line = jnp.where(lane == k * slots + s, value, line)
    return line.astype(f32)


def rhs_kernel(
    user_tile, word_tile, subreddit, counts, ratings_in, runs_in, words_in, subs_in, *refs,
    half, owners, own_rows,
):
    if half == 0:
        given, refs = refs[0], refs[1:]
    outs, (ratings, runs, words, subs, table, sums, arrived, loaded) = refs[:-8], refs[-8:]
    steps, slots, tile = ratings.shape[0], ratings.shape[1], ratings.shape[2]
    rank = words.shape[-1]
    levels = steps // 2

    place = lax.axis_index("loop")
    level, seat = lax.div(place, 4), lax.rem(place, 4)

    def group_at(step):
        there = lax.rem(seat + 2 * (step // levels), 4)
        if half:
            there = there + 1 - 2 * lax.rem(there, 2)
        return 4 * lax.rem(level + step % levels, levels) + there

    def load(step):
        group = group_at(step)
        return pltpu.make_async_copy(ratings_in.at[group], ratings.at[step], arrived.at[step])

    tables = [
        pltpu.make_async_copy(source, target, loaded.at[k])
        for k, (source, target) in enumerate(
            [(subs_in, subs), (runs_in, runs), (words_in, words)]
        )
    ]
    for copy in tables:
        copy.start()
    for step in range(steps):
        load(step).start()
    tables[0].wait()
    table[...] = subs[...].astype(f32)
    tables[1].wait()
    tables[2].wait()

    eye = (
        lax.broadcasted_iota(jnp.int32, (tile, tile), 0)
        == lax.broadcasted_iota(jnp.int32, (tile, tile), 1)
    ).astype(f32).astype(bf16)
    me = lax.axis_index("own")
    for step in range(steps):
        group = group_at(step)
        live = counts[0, group]
        columns = []
        for s in range(slots):
            pair = runs[group, s]
            columns.append(
                mask_columns(pair[0:1], jnp.where(s < live, pair[1:2], 0), tile)
            )
        seen = dot_nt(eye, jnp.concatenate(columns, axis=0)).astype(bf16)
        load(step).wait()
        sums[step % 2] = jnp.zeros(sums.shape[1:], f32)
        for s in range(slots):
            sub_row = table[pl.ds(subreddit[s, group], 1), :]
            product = (words[word_tile[s, group]].astype(f32) * sub_row).astype(bf16)
            weights = seen[:, s * tile : (s + 1) * tile] * ratings[step, s]
            rows = pl.ds(pl.multiple_of(user_tile[s, group] * tile, tile), tile)
            sums[step % 2, rows, :] += dot_nn(weights, product)
        line = fact_line(user_tile, word_tile, subreddit, live, group, slots, rank)
        spans = jnp.concatenate([runs[group, s] for s in range(slots)], axis=0).astype(f32)
        end = own_rows + 2 * slots
        for o in range(owners):
            owner = lax.rem(me + o, owners)
            rows = pl.ds(pl.multiple_of(owner * own_rows, own_rows), own_rows)
            value = sums[step % 2, rows, :]
            column, up = step // levels, step % levels
            if half == 0:
                other = given[o, column, up].astype(f32)
                value = jnp.concatenate(
                    [
                        value + other[:own_rows],
                        spans,
                        other[own_rows:end],
                        line,
                        other[end : end + 1],
                        jnp.zeros((FACT_ROWS - 2, rank), f32),
                    ],
                    axis=0,
                )
                outs[2 * o + column][up] = value.astype(bf16)
            else:
                value = jnp.concatenate(
                    [value, spans, line, jnp.zeros((FACT_ROWS - 1, rank), f32)], axis=0
                )
                outs[0][o, column, up] = value.astype(bf16)


def rhs_sums(scalars, ratings, runs, words, subs, half, given, owners, own_rows):
    groups, slots, tile, _ = ratings.shape
    rank = words.shape[-1]
    steps, levels = groups // 2, groups // 4
    anywhere = pl.BlockSpec(memory_space=pl.ANY)
    whole = pl.BlockSpec(memory_space=pltpu.VMEM)
    part = (levels, own_rows + 2 * slots * (2 - half) + FACT_ROWS, rank)
    shapes = [part] * (2 * owners) if half == 0 else [(owners, 2) + part]
    return pl.pallas_call(
        functools.partial(rhs_kernel, half=half, owners=owners, own_rows=own_rows),
        in_specs=[pl.BlockSpec(memory_space=pltpu.SMEM)] * 4
        + [anywhere] * 4
        + [whole] * (1 - half),
        out_specs=[whole] * len(shapes),
        out_shape=[jax.ShapeDtypeStruct(shape, bf16) for shape in shapes],
        scratch_shapes=[
            pltpu.VMEM((steps,) + ratings.shape[1:], bf16),
            pltpu.VMEM(runs.shape, jnp.int32),
            pltpu.VMEM(words.shape, bf16),
            pltpu.VMEM(subs.shape, bf16),
            pltpu.VMEM(subs.shape, f32),
            pltpu.VMEM((2, owners * own_rows, rank), f32),
            pltpu.SemaphoreType.DMA((steps,)),
            pltpu.SemaphoreType.DMA((3,)),
        ],
        compiler_params=pltpu.CompilerParams(vmem_limit_bytes=VMEM_LIMIT if half else 50 * MIB),
        cost_estimate=pl.CostEstimate(
            flops=8 * ratings.size * rank, bytes_accessed=8 * ratings.size, transcendentals=0
        ),
        name="rhs",
    )(*scalars, ratings, runs, words, subs, *([given] if half == 0 else []))


def chip_kernel(*refs, own_rows, spans):
    levels, _, rank = refs[0].shape
    parts, outs = refs[:-levels], refs[-levels:]
    lines = outs[0].shape[0] - own_rows - spans * len(parts)
    for up in range(levels):
        total = parts[0][up, :own_rows, :].astype(f32)
        for part in parts[1:]:
            total = total + part[up, :own_rows, :].astype(f32)
        outs[up][:own_rows, :] = total.astype(bf16)
        facts = []
        for k, part in enumerate(parts):
            at = own_rows + spans * k
            outs[up][at : at + spans, :] = part[up, own_rows : own_rows + spans, :]
            facts.append(part[up, own_rows + spans :, :].astype(f32)[:2])
        facts.append(jnp.zeros((lines - 2 * len(parts), rank), f32))
        outs[up][own_rows + spans * len(parts) :, :] = jnp.concatenate(
            facts[: len(facts) - (lines == 2 * len(parts))], axis=0
        ).astype(bf16)


def exchange_chips(parts, shards, owners):
    given = []
    for o in range(owners):
        for column in range(2):
            pairs = [
                (shard * owners + k, (shard ^ 2 * column) * owners + (k + o) % owners)
                for shard in range(shards)
                for k in range(owners)
            ]
            part = parts[2 * o + column]
            given.append(lax.ppermute(part, AXES, pairs) if o or column else part)
    return given


def join_chips(parts, own_rows):
    levels, rows, rank = parts[0].shape
    spans = rows - own_rows - FACT_ROWS
    lines = -(-2 * len(parts) // FACT_ROWS) * FACT_ROWS
    whole = pl.BlockSpec(memory_space=pltpu.VMEM)
    shape = jax.ShapeDtypeStruct((own_rows + spans * len(parts) + lines, rank), bf16)
    return pl.pallas_call(
        functools.partial(chip_kernel, own_rows=own_rows, spans=spans),
        in_specs=[whole] * len(parts),
        out_specs=[whole] * levels,
        out_shape=[shape] * levels,
        compiler_params=pltpu.CompilerParams(vmem_limit_bytes=16 * MIB),
        name="chip",
    )(*parts)


def reduce_levels(total, shards):
    levels = shards // 4
    terms = [total[0]]
    for up in range(1, levels):
        shift = [(shard, (shard + 4 * up) % shards) for shard in range(shards)]
        terms.append(lax.ppermute(total[up], "loop", shift))
    return terms


def steps_kernel(activity, start, subs, *refs, count, word_tiles, levels, slots, cached):
    pieces, refs = refs[:count], refs[count:]
    terms, refs = refs[:levels], refs[levels:]
    first_out, second_out, third_out, dots_out = refs[:4]
    masks, words, table, runs, lines, facts, chosen, places, arrived, moved = refs[4:14]
    products = refs[-1]
    own_rows, rank = start.shape
    _, tile, _ = pieces[0].shape
    sources = lines.shape[0] // levels
    spans = 2 * slots * sources

    copies, at = [], 0
    for k, piece in enumerate(pieces):
        place = words.at[at : at + piece.shape[0]]
        copies.append(pltpu.make_async_copy(piece, place, arrived.at[k]))
        at += piece.shape[0]
    for copy in copies:
        copy.start()

    for up in range(levels):
        rest = terms[up][own_rows + spans :, :].astype(f32)
        lines[up * sources : (up + 1) * sources, :] = rest[:sources].astype(jnp.int32)
    move = pltpu.make_async_copy(lines, facts, moved.at[0])
    move.start()
    rhs = jnp.zeros((own_rows, rank), f32)
    for up in range(levels):
        rhs = rhs + terms[up][:own_rows, :].astype(f32)
        runs[up * spans : (up + 1) * spans, :] = terms[up][
            own_rows : own_rows + spans, :
        ].astype(f32)
    table[...] = subs[...].astype(f32)
    move.wait()

    place = lax.axis_index("loop")
    level, seat = lax.div(place, 4), lax.rem(place, 4)
    wanted = lax.div(lax.axis_index("own") * own_rows, tile) + 1
    chips = at // word_tiles // 2

    def ring_at(level, column):
        return jnp.where(column == 0, level, chips - 1 - level)

    used = 0
    column = lax.div(seat, 2)
    for up in range(levels):
        there = lax.rem(level - up + levels, levels)
        ahead = [
            lax.rem(ring_at(there, side) - ring_at(level, column) + chips, chips)
            for side in (column, 1 - column)
        ]

        def choose(k, n, up=up, ahead=ahead):
            src = up * sources + k
            side = lax.rem(lax.div(k, 2), 2)
            distance = jnp.where(side == 0, ahead[0], ahead[1])
            places[src] = word_tiles * (2 * distance + lax.rem(k, 2))
            for s in range(slots):
                chosen[n] = src * slots + s
                n = n + jnp.where(facts[src, s] == wanted, 1, 0)
            return n

        used = lax.fori_loop(0, sources, choose, used)
    chunks = lax.div(used + CHUNK - 1, CHUNK)

    offset = lax.rem(lax.axis_index("own") * own_rows, tile)
    pick = (
        lax.broadcasted_iota(jnp.int32, (own_rows, tile), 0) + offset
        == lax.broadcasted_iota(jnp.int32, (own_rows, tile), 1)
    ).astype(f32).astype(bf16)

    def mask(chunk):
        parts = []
        for b in range(CHUNK):
            i = chunk * CHUNK + b
            j = chosen[jnp.minimum(i, used - 1)]
            first = runs[pl.ds(2 * j, 1), :].astype(jnp.int32)
            length = runs[pl.ds(2 * j + 1, 1), :].astype(jnp.int32)
            length = jnp.where(i < used, length, 0)
            parts.append(mask_columns(first, length, tile))
        return dot_nt(pick, jnp.concatenate(parts, axis=0)).astype(bf16)

    def product(i):
        j = chosen[jnp.minimum(i, used - 1)]
        src, s = lax.div(j, slots), lax.rem(j, slots)
        sub = 128 * facts[src, 2 * slots + s] + facts[src, 3 * slots + s]
        rows = words[places[src] + facts[src, slots + s]].astype(f32)
        return (rows * table[pl.ds(sub, 1), :]).astype(bf16)

    for copy in copies:
        copy.wait()

    def gram(vector, build=False):
        rounded = vector.astype(bf16)

        def body(chunk, total):
            if build:
                masks[chunk] = mask(chunk)
            if cached and not build:
                block = products[chunk]
            else:
                block = jnp.concatenate(
                    [product(chunk * CHUNK + b) for b in range(CHUNK)], axis=0
                )
                if cached:
                    products[chunk] = block
            weights = dot_nt(rounded, block).astype(bf16) * masks[chunk]
            return total + dot_nn(weights, block)

        return lax.fori_loop(0, chunks, body, jnp.zeros((own_rows, rank), f32))

    def over_row(a, b):
        return jnp.sum(a * b, axis=1, keepdims=True)

    scale = jnp.broadcast_to(activity[...], (rank, own_rows)).T
    first = scale * (rhs - gram(start[...], build=True)) - ridge * start[...]
    second = scale * gram(first) + ridge * first
    norms, overlaps = over_row(first, first), over_row(first, second)
    share = jnp.where(norms > 0.0, overlaps / jnp.where(norms > 0.0, norms, 1.0), 0.0)
    rest = second - share * first
    third = scale * gram(rest) + ridge * rest + share * second
    first_out[...] = first
    second_out[...] = second
    third_out[...] = third
    rows = [norms, overlaps, over_row(second, second), over_row(first, third), over_row(second, third)]
    lane = lax.broadcasted_iota(jnp.int32, (1, rank), 1)
    line = jnp.zeros((1, rank), f32)
    for k, value in enumerate(rows):
        line = line + jnp.where(lane == k, jnp.sum(value, axis=0, keepdims=True), 0.0)
    dots_out[...] = jnp.broadcast_to(line[None], dots_out.shape)


def krylov(start, activity, subs, pieces, terms, word_tiles, slots, devices):
    own_rows, rank = start.shape
    blocks = devices * slots
    _, tile, _ = pieces[0].shape
    chunks = -(-blocks // CHUNK)
    cached = blocks * tile * rank * 2 <= 16 * 2**20
    whole = pl.BlockSpec(memory_space=pltpu.VMEM)
    anywhere = pl.BlockSpec(memory_space=pl.ANY)
    vector = jax.ShapeDtypeStruct((own_rows, rank), f32)
    scratch = [
        pltpu.VMEM((chunks, own_rows, CHUNK * tile), bf16),
        pltpu.VMEM((sum(piece.shape[0] for piece in pieces), tile, rank), bf16),
        pltpu.VMEM(subs.shape, f32),
        pltpu.VMEM((2 * blocks, tile), f32),
        pltpu.VMEM((devices, rank), jnp.int32),
        pltpu.SMEM((devices, rank), jnp.int32),
        pltpu.SMEM((blocks,), jnp.int32),
        pltpu.SMEM((devices,), jnp.int32),
        pltpu.SemaphoreType.DMA((len(pieces),)),
        pltpu.SemaphoreType.DMA((1,)),
    ]
    if cached:
        scratch.append(pltpu.VMEM((chunks, CHUNK * tile, rank), bf16))
    return pl.pallas_call(
        functools.partial(
            steps_kernel,
            count=len(pieces),
            word_tiles=word_tiles,
            levels=len(terms),
            slots=slots,
            cached=cached,
        ),
        in_specs=[whole] * 3 + [anywhere] * len(pieces) + [whole] * len(terms),
        out_specs=[whole] * 4,
        out_shape=[vector, vector, vector, jax.ShapeDtypeStruct((devices, 1, rank), f32)],
        scratch_shapes=scratch,
        compiler_params=pltpu.CompilerParams(vmem_limit_bytes=44 * MIB),
        name="krylov",
    )(activity, start, subs, *pieces, *terms)


def last_kernel(dots, start, first, second, third, solution_out, residual_out):
    line = dots[0]
    for k in range(1, dots.shape[0]):
        line = line + dots[k]
    rr, rq, qq, rz, qz = (line[:, k : k + 1] for k in range(5))
    step0 = rr / rq
    next_rr = rr - 2.0 * step0 * rq + step0 * step0 * qq
    grow = 1.0 + next_rr / rr
    slope = grow * (grow * rq - step0 * (rz + qq)) + step0 * step0 * qz
    step1 = next_rr / slope
    near, far = step0 + step1 * grow, step1 * step0
    solution_out[...] = start[...] + near * first[...] - far * second[...]
    residual_out[...] = first[...] - near * second[...] + far * third[...]


def last_step(dots, start, first, second, third):
    whole = pl.BlockSpec(memory_space=pltpu.VMEM)
    vector = jax.ShapeDtypeStruct(start.shape, f32)
    return pl.pallas_call(
        last_kernel,
        in_specs=[whole] * 5,
        out_specs=[whole] * 2,
        out_shape=[vector, vector],
        compiler_params=pltpu.CompilerParams(vmem_limit_bytes=8 * MIB),
        name="last_step",
    )(dots, start, first, second, third)


def ring_round(up, down, held, step, shards):
    chips = shards // 2
    levels = chips // 2
    order = [2 * level for level in range(levels)] + [
        2 * level + 1 for level in reversed(range(levels))
    ]

    def shift(by):
        return [
            (2 * order[p] + core, 2 * order[(p + by) % chips] + core)
            for p in range(chips)
            for core in range(2)
        ]

    if step == chips - step:
        half = up.shape[0] // 2
        up = lax.ppermute(up[:half], "loop", shift(1))
        down = lax.ppermute(down[half:], "loop", shift(-1))
        held[step] = (up, down)
    else:
        up = lax.ppermute(up, "loop", shift(1))
        down = lax.ppermute(down, "loop", shift(-1))
        held[chips - step], held[step] = (up,), (down,)
    return up, down


def other_core(values, shards):
    pairs = [(shard, shard ^ 1) for shard in range(shards)]
    return tuple(lax.ppermute(value, "loop", pairs) for value in values)


def on_device(
    factor_start,
    activity,
    word_factors,
    sub_factors,
    ratings,
    user_tile,
    word_tile,
    subreddit,
    counts,
    runs,
):
    own_rows, rank = factor_start.shape
    owners, shards = lax.axis_size("own"), lax.axis_size("loop")
    slots = ratings.shape[3]
    devices = shards * owners
    chips = shards // 2
    together = lax.optimization_barrier

    scalars = (user_tile[0, 0].T, word_tile[0, 0].T, subreddit[0, 0].T, counts[0])
    mine = word_factors[0]
    held = {0: (mine,)}

    inputs = (scalars, ratings[0, 0], runs[0, 0], mine, sub_factors)
    up, down = ring_round(mine, mine, held, 1, shards)
    (away,) = rhs_sums(*inputs, 1, None, owners, own_rows)
    crossed = {0: other_core(held[0], shards)}
    up, down, away, crossed = together((up, down, away, crossed))

    def cross(step):
        for distance in {step, chips - step}:
            crossed[distance] = other_core(held[distance], shards)

    cross(1)
    up, down = ring_round(up, down, held, 2, shards)
    (given,) = other_core((away,), shards)
    parts = rhs_sums(*inputs, 0, given, owners, own_rows)
    up, down, parts, crossed = together((up, down, parts, crossed))

    up, down = ring_round(up, down, held, 3, shards)
    given = exchange_chips(parts, shards, owners)
    total = join_chips(given, own_rows)
    up, down, total, held = together((up, down, total, held))

    for step in range(4, chips // 2 + 1):
        up, down = ring_round(up, down, held, step, shards)
    terms = reduce_levels(total, shards)
    held[chips // 2], terms, crossed = together((held[chips // 2], terms, crossed))

    for step in range(2, chips // 2 + 1):
        cross(step)
    pieces = []
    for distance in range(chips):
        pieces += held[distance] + crossed[distance]
    first, second, third, dots = krylov(
        factor_start, activity[None], sub_factors, pieces, terms, mine.shape[0], slots, devices
    )
    everyone = lax.all_to_all(dots, AXES, 0, 0, tiled=True)
    return tuple(last_step(everyone, factor_start, first, second, third))


def solution(mesh):
    placed = (
        P(("loop", "own"), None),
        P(("loop", "own")),
        P("loop", None, None, None),
        P(),
        P("loop", "own", None, None, None, None),
        P("loop", "own", None, None),
        P("loop", "own", None, None),
        P("loop", "own", None, None),
        P("loop", "own", None),
        P("loop", "own", None, None, None, None),
    )
    return jax.shard_map(
        on_device,
        mesh=mesh,
        in_specs=placed,
        out_specs=(P(("loop", "own"), None), P(("loop", "own"), None)),
        check_vma=False,
    )
```

```python
import functools

import jax
import jax.numpy as jnp
from jax import lax
from jax.experimental import pallas as pl
from jax.experimental.pallas import tpu as pltpu
from jax.sharding import PartitionSpec as P

AXES = ("loop", "own")
CHUNK = 48
FACT_ROWS = 16
ridge = 0.05
MIB = 2**20
VMEM_LIMIT = 60 * MIB
f32 = jnp.float32
bf16 = jnp.bfloat16


def dot_nt(left, right):
    return lax.dot_general(left, right, (((1,), (1,)), ((), ())), preferred_element_type=f32)


def dot_nn(left, right):
    return jnp.dot(left, right, preferred_element_type=f32)


def mask_columns(first, length, tile):
    column = lax.broadcasted_iota(jnp.int32, (tile, first.shape[-1]), 0)
    inside = ((column - first) & (tile - 1)) < length
    return jnp.where(inside, 1.0, 0.0).astype(bf16)


def fact_line(user_tile, word_tile, subreddit, live, group, slots, rank):
    lane = lax.broadcasted_iota(jnp.int32, (1, rank), 1)
    line = jnp.zeros((1, rank), jnp.int32)
    for s in range(slots):
        sub = subreddit[s, group]
        user = jnp.where(s < live, user_tile[s, group] + 1, 0)
        values = (user, word_tile[s, group], lax.div(sub, 128), lax.rem(sub, 128))
        for k, value in enumerate(values):
            line = jnp.where(lane == k * slots + s, value, line)
    return line.astype(f32)


def rhs_kernel(
    user_tile, word_tile, subreddit, counts, ratings_in, runs_in, words_in, subs_in, *refs,
    half, owners, own_rows,
):
    if half == 0:
        given, refs = refs[0], refs[1:]
    outs, (ratings, runs, words, subs, table, sums, arrived, loaded) = refs[:-8], refs[-8:]
    steps, slots, tile = ratings.shape[0], ratings.shape[1], ratings.shape[2]
    rank = words.shape[-1]
    levels = steps // 2

    place = lax.axis_index("loop")
    level, seat = lax.div(place, 4), lax.rem(place, 4)

    def group_at(step):
        there = lax.rem(seat + 2 * (step // levels), 4)
        if half:
            there = there + 1 - 2 * lax.rem(there, 2)
        return 4 * lax.rem(level + step % levels, levels) + there

    def load(step):
        group = group_at(step)
        return pltpu.make_async_copy(ratings_in.at[group], ratings.at[step], arrived.at[step])

    tables = [
        pltpu.make_async_copy(source, target, loaded.at[k])
        for k, (source, target) in enumerate(
            [(subs_in, subs), (runs_in, runs), (words_in, words)]
        )
    ]
    for copy in tables:
        copy.start()
    for step in range(steps):
        load(step).start()
    tables[0].wait()
    table[...] = subs[...].astype(f32)
    tables[1].wait()
    tables[2].wait()

    eye = (
        lax.broadcasted_iota(jnp.int32, (tile, tile), 0)
        == lax.broadcasted_iota(jnp.int32, (tile, tile), 1)
    ).astype(f32).astype(bf16)
    me = lax.axis_index("own")
    for step in range(steps):
        group = group_at(step)
        live = counts[0, group]
        columns = []
        for s in range(slots):
            pair = runs[group, s]
            columns.append(
                mask_columns(pair[0:1], jnp.where(s < live, pair[1:2], 0), tile)
            )
        seen = dot_nt(eye, jnp.concatenate(columns, axis=0)).astype(bf16)
        load(step).wait()
        sums[step % 2] = jnp.zeros(sums.shape[1:], f32)
        for s in range(slots):
            sub_row = table[pl.ds(subreddit[s, group], 1), :]
            product = (words[word_tile[s, group]].astype(f32) * sub_row).astype(bf16)
            weights = seen[:, s * tile : (s + 1) * tile] * ratings[step, s]
            rows = pl.ds(pl.multiple_of(user_tile[s, group] * tile, tile), tile)
            sums[step % 2, rows, :] += dot_nn(weights, product)
        line = fact_line(user_tile, word_tile, subreddit, live, group, slots, rank)
        spans = jnp.concatenate([runs[group, s] for s in range(slots)], axis=0).astype(f32)
        end = own_rows + 2 * slots
        for o in range(owners):
            owner = lax.rem(me + o, owners)
            rows = pl.ds(pl.multiple_of(owner * own_rows, own_rows), own_rows)
            value = sums[step % 2, rows, :]
            column, up = step // levels, step % levels
            if half == 0:
                other = given[o, column, up].astype(f32)
                value = jnp.concatenate(
                    [
                        value + other[:own_rows],
                        spans,
                        other[own_rows:end],
                        line,
                        other[end : end + 1],
                        jnp.zeros((FACT_ROWS - 2, rank), f32),
                    ],
                    axis=0,
                )
                outs[2 * o + column][up] = value.astype(bf16)
            else:
                value = jnp.concatenate(
                    [value, spans, line, jnp.zeros((FACT_ROWS - 1, rank), f32)], axis=0
                )
                outs[0][o, column, up] = value.astype(bf16)


def rhs_sums(scalars, ratings, runs, words, subs, half, given, owners, own_rows):
    groups, slots, tile, _ = ratings.shape
    rank = words.shape[-1]
    steps, levels = groups // 2, groups // 4
    anywhere = pl.BlockSpec(memory_space=pl.ANY)
    whole = pl.BlockSpec(memory_space=pltpu.VMEM)
    part = (levels, own_rows + 2 * slots * (2 - half) + FACT_ROWS, rank)
    shapes = [part] * (2 * owners) if half == 0 else [(owners, 2) + part]
    return pl.pallas_call(
        functools.partial(rhs_kernel, half=half, owners=owners, own_rows=own_rows),
        in_specs=[pl.BlockSpec(memory_space=pltpu.SMEM)] * 4
        + [anywhere] * 4
        + [whole] * (1 - half),
        out_specs=[whole] * len(shapes),
        out_shape=[jax.ShapeDtypeStruct(shape, bf16) for shape in shapes],
        scratch_shapes=[
            pltpu.VMEM((steps,) + ratings.shape[1:], bf16),
            pltpu.VMEM(runs.shape, jnp.int32),
            pltpu.VMEM(words.shape, bf16),
            pltpu.VMEM(subs.shape, bf16),
            pltpu.VMEM(subs.shape, f32),
            pltpu.VMEM((2, owners * own_rows, rank), f32),
            pltpu.SemaphoreType.DMA((steps,)),
            pltpu.SemaphoreType.DMA((3,)),
        ],
        compiler_params=pltpu.CompilerParams(vmem_limit_bytes=VMEM_LIMIT if half else 50 * MIB),
        cost_estimate=pl.CostEstimate(
            flops=8 * ratings.size * rank, bytes_accessed=8 * ratings.size, transcendentals=0
        ),
        name="rhs",
    )(*scalars, ratings, runs, words, subs, *([given] if half == 0 else []))


def chip_kernel(*refs, own_rows, spans):
    levels, _, rank = refs[0].shape
    parts, outs = refs[:-levels], refs[-levels:]
    lines = outs[0].shape[0] - own_rows - spans * len(parts)
    for up in range(levels):
        total = parts[0][up, :own_rows, :].astype(f32)
        for part in parts[1:]:
            total = total + part[up, :own_rows, :].astype(f32)
        outs[up][:own_rows, :] = total.astype(bf16)
        facts = []
        for k, part in enumerate(parts):
            at = own_rows + spans * k
            outs[up][at : at + spans, :] = part[up, own_rows : own_rows + spans, :]
            facts.append(part[up, own_rows + spans :, :].astype(f32)[:2])
        facts.append(jnp.zeros((lines - 2 * len(parts), rank), f32))
        outs[up][own_rows + spans * len(parts) :, :] = jnp.concatenate(
            facts[: len(facts) - (lines == 2 * len(parts))], axis=0
        ).astype(bf16)


def exchange_chips(parts, shards, owners):
    given = []
    for o in range(owners):
        for column in range(2):
            pairs = [
                (shard * owners + k, (shard ^ 2 * column) * owners + (k + o) % owners)
                for shard in range(shards)
                for k in range(owners)
            ]
            part = parts[2 * o + column]
            given.append(lax.ppermute(part, AXES, pairs) if o or column else part)
    return given


def join_chips(parts, own_rows):
    levels, rows, rank = parts[0].shape
    spans = rows - own_rows - FACT_ROWS
    lines = -(-2 * len(parts) // FACT_ROWS) * FACT_ROWS
    whole = pl.BlockSpec(memory_space=pltpu.VMEM)
    shape = jax.ShapeDtypeStruct((own_rows + spans * len(parts) + lines, rank), bf16)
    return pl.pallas_call(
        functools.partial(chip_kernel, own_rows=own_rows, spans=spans),
        in_specs=[whole] * len(parts),
        out_specs=[whole] * levels,
        out_shape=[shape] * levels,
        compiler_params=pltpu.CompilerParams(vmem_limit_bytes=16 * MIB),
        name="chip",
    )(*parts)


def reduce_levels(total, shards):
    levels = shards // 4
    terms = [total[0]]
    for up in range(1, levels):
        shift = [(shard, (shard + 4 * up) % shards) for shard in range(shards)]
        terms.append(lax.ppermute(total[up], "loop", shift))
    return terms


def steps_kernel(activity, start, subs, *refs, count, word_tiles, levels, slots, cached):
    pieces, refs = refs[:count], refs[count:]
    terms, refs = refs[:levels], refs[levels:]
    first_out, second_out, third_out, dots_out = refs[:4]
    masks, words, table, runs, lines, facts, chosen, places, arrived, moved = refs[4:14]
    products = refs[-1]
    own_rows, rank = start.shape
    _, tile, _ = pieces[0].shape
    sources = lines.shape[0] // levels
    spans = 2 * slots * sources

    copies, at = [], 0
    for k, piece in enumerate(pieces):
        place = words.at[at : at + piece.shape[0]]
        copies.append(pltpu.make_async_copy(piece, place, arrived.at[k]))
        at += piece.shape[0]
    for copy in copies:
        copy.start()

    for up in range(levels):
        rest = terms[up][own_rows + spans :, :].astype(f32)
        lines[up * sources : (up + 1) * sources, :] = rest[:sources].astype(jnp.int32)
    move = pltpu.make_async_copy(lines, facts, moved.at[0])
    move.start()
    rhs = jnp.zeros((own_rows, rank), f32)
    for up in range(levels):
        rhs = rhs + terms[up][:own_rows, :].astype(f32)
        runs[up * spans : (up + 1) * spans, :] = terms[up][
            own_rows : own_rows + spans, :
        ].astype(f32)
    table[...] = subs[...].astype(f32)
    move.wait()

    place = lax.axis_index("loop")
    level, seat = lax.div(place, 4), lax.rem(place, 4)
    wanted = lax.div(lax.axis_index("own") * own_rows, tile) + 1
    chips = at // word_tiles // 2

    def ring_at(level, column):
        return jnp.where(column == 0, level, chips - 1 - level)

    used = 0
    column = lax.div(seat, 2)
    for up in range(levels):
        there = lax.rem(level - up + levels, levels)
        ahead = [
            lax.rem(ring_at(there, side) - ring_at(level, column) + chips, chips)
            for side in (column, 1 - column)
        ]

        def choose(k, n, up=up, ahead=ahead):
            src = up * sources + k
            side = lax.rem(lax.div(k, 2), 2)
            distance = jnp.where(side == 0, ahead[0], ahead[1])
            places[src] = word_tiles * (2 * distance + lax.rem(k, 2))
            for s in range(slots):
                chosen[n] = src * slots + s
                n = n + jnp.where(facts[src, s] == wanted, 1, 0)
            return n

        used = lax.fori_loop(0, sources, choose, used)
    chunks = lax.div(used + CHUNK - 1, CHUNK)

    offset = lax.rem(lax.axis_index("own") * own_rows, tile)
    pick = (
        lax.broadcasted_iota(jnp.int32, (own_rows, tile), 0) + offset
        == lax.broadcasted_iota(jnp.int32, (own_rows, tile), 1)
    ).astype(f32).astype(bf16)

    def mask(chunk):
        parts = []
        for b in range(CHUNK):
            i = chunk * CHUNK + b
            j = chosen[jnp.minimum(i, used - 1)]
            first = runs[pl.ds(2 * j, 1), :].astype(jnp.int32)
            length = runs[pl.ds(2 * j + 1, 1), :].astype(jnp.int32)
            length = jnp.where(i < used, length, 0)
            parts.append(mask_columns(first, length, tile))
        return dot_nt(pick, jnp.concatenate(parts, axis=0)).astype(bf16)

    def product(i):
        j = chosen[jnp.minimum(i, used - 1)]
        src, s = lax.div(j, slots), lax.rem(j, slots)
        sub = 128 * facts[src, 2 * slots + s] + facts[src, 3 * slots + s]
        rows = words[places[src] + facts[src, slots + s]].astype(f32)
        return (rows * table[pl.ds(sub, 1), :]).astype(bf16)

    for copy in copies:
        copy.wait()

    def gram(vector, build=False):
        rounded = vector.astype(bf16)

        def body(chunk, total):
            if build:
                masks[chunk] = mask(chunk)
            if cached and not build:
                block = products[chunk]
            else:
                block = jnp.concatenate(
                    [product(chunk * CHUNK + b) for b in range(CHUNK)], axis=0
                )
                if cached:
                    products[chunk] = block
            weights = dot_nt(rounded, block).astype(bf16) * masks[chunk]
            return total + dot_nn(weights, block)

        return lax.fori_loop(0, chunks, body, jnp.zeros((own_rows, rank), f32))

    def over_row(a, b):
        return jnp.sum(a * b, axis=1, keepdims=True)

    scale = jnp.broadcast_to(activity[...], (rank, own_rows)).T
    first = scale * (rhs - gram(start[...], build=True)) - ridge * start[...]
    second = scale * gram(first) + ridge * first
    norms, overlaps = over_row(first, first), over_row(first, second)
    share = jnp.where(norms > 0.0, overlaps / jnp.where(norms > 0.0, norms, 1.0), 0.0)
    rest = second - share * first
    third = scale * gram(rest) + ridge * rest + share * second
    first_out[...] = first
    second_out[...] = second
    third_out[...] = third
    rows = [norms, overlaps, over_row(second, second), over_row(first, third), over_row(second, third)]
    lane = lax.broadcasted_iota(jnp.int32, (1, rank), 1)
    line = jnp.zeros((1, rank), f32)
    for k, value in enumerate(rows):
        line = line + jnp.where(lane == k, jnp.sum(value, axis=0, keepdims=True), 0.0)
    dots_out[...] = jnp.broadcast_to(line[None], dots_out.shape)


def krylov(start, activity, subs, pieces, terms, word_tiles, slots, devices):
    own_rows, rank = start.shape
    blocks = devices * slots
    _, tile, _ = pieces[0].shape
    chunks = -(-blocks // CHUNK)
    cached = blocks * tile * rank * 2 <= 16 * 2**20
    whole = pl.BlockSpec(memory_space=pltpu.VMEM)
    anywhere = pl.BlockSpec(memory_space=pl.ANY)
    vector = jax.ShapeDtypeStruct((own_rows, rank), f32)
    scratch = [
        pltpu.VMEM((chunks, own_rows, CHUNK * tile), bf16),
        pltpu.VMEM((sum(piece.shape[0] for piece in pieces), tile, rank), bf16),
        pltpu.VMEM(subs.shape, f32),
        pltpu.VMEM((2 * blocks, tile), f32),
        pltpu.VMEM((devices, rank), jnp.int32),
        pltpu.SMEM((devices, rank), jnp.int32),
        pltpu.SMEM((blocks,), jnp.int32),
        pltpu.SMEM((devices,), jnp.int32),
        pltpu.SemaphoreType.DMA((len(pieces),)),
        pltpu.SemaphoreType.DMA((1,)),
    ]
    if cached:
        scratch.append(pltpu.VMEM((chunks, CHUNK * tile, rank), bf16))
    return pl.pallas_call(
        functools.partial(
            steps_kernel,
            count=len(pieces),
            word_tiles=word_tiles,
            levels=len(terms),
            slots=slots,
            cached=cached,
        ),
        in_specs=[whole] * 3 + [anywhere] * len(pieces) + [whole] * len(terms),
        out_specs=[whole] * 4,
        out_shape=[vector, vector, vector, jax.ShapeDtypeStruct((devices, 1, rank), f32)],
        scratch_shapes=scratch,
        compiler_params=pltpu.CompilerParams(vmem_limit_bytes=44 * MIB),
        name="krylov",
    )(activity, start, subs, *pieces, *terms)


def last_kernel(dots, start, first, second, third, solution_out, residual_out):
    line = dots[0]
    for k in range(1, dots.shape[0]):
        line = line + dots[k]
    rr, rq, qq, rz, qz = (line[:, k : k + 1] for k in range(5))
    step0 = rr / rq
    next_rr = rr - 2.0 * step0 * rq + step0 * step0 * qq
    grow = 1.0 + next_rr / rr
    slope = grow * (grow * rq - step0 * (rz + qq)) + step0 * step0 * qz
    step1 = next_rr / slope
    near, far = step0 + step1 * grow, step1 * step0
    solution_out[...] = start[...] + near * first[...] - far * second[...]
    residual_out[...] = first[...] - near * second[...] + far * third[...]


def last_step(dots, start, first, second, third):
    whole = pl.BlockSpec(memory_space=pltpu.VMEM)
    vector = jax.ShapeDtypeStruct(start.shape, f32)
    return pl.pallas_call(
        last_kernel,
        in_specs=[whole] * 5,
        out_specs=[whole] * 2,
        out_shape=[vector, vector],
        compiler_params=pltpu.CompilerParams(vmem_limit_bytes=8 * MIB),
        name="last_step",
    )(dots, start, first, second, third)


def ring_round(up, down, held, step, shards):
    chips = shards // 2
    levels = chips // 2
    order = [2 * level for level in range(levels)] + [
        2 * level + 1 for level in reversed(range(levels))
    ]

    def shift(by):
        return [
            (2 * order[p] + core, 2 * order[(p + by) % chips] + core)
            for p in range(chips)
            for core in range(2)
        ]

    if step == chips - step:
        half = up.shape[0] // 2
        up = lax.ppermute(up[:half], "loop", shift(1))
        down = lax.ppermute(down[half:], "loop", shift(-1))
        held[step] = (up, down)
    else:
        up = lax.ppermute(up, "loop", shift(1))
        down = lax.ppermute(down, "loop", shift(-1))
        held[chips - step], held[step] = (up,), (down,)
    return up, down


def other_core(values, shards):
    pairs = [(shard, shard ^ 1) for shard in range(shards)]
    return tuple(lax.ppermute(value, "loop", pairs) for value in values)


def on_device(
    factor_start,
    activity,
    word_factors,
    sub_factors,
    ratings,
    user_tile,
    word_tile,
    subreddit,
    counts,
    runs,
):
    own_rows, rank = factor_start.shape
    owners, shards = lax.axis_size("own"), lax.axis_size("loop")
    slots = ratings.shape[3]
    devices = shards * owners
    chips = shards // 2
    together = lax.optimization_barrier

    scalars = (user_tile[0, 0].T, word_tile[0, 0].T, subreddit[0, 0].T, counts[0])
    mine = word_factors[0]
    held = {0: (mine,)}

    inputs = (scalars, ratings[0, 0], runs[0, 0], mine, sub_factors)
    up, down = ring_round(mine, mine, held, 1, shards)
    (away,) = rhs_sums(*inputs, 1, None, owners, own_rows)
    crossed = {0: other_core(held[0], shards)}
    up, down, away, crossed = together((up, down, away, crossed))

    def cross(step):
        for distance in {step, chips - step}:
            crossed[distance] = other_core(held[distance], shards)

    cross(1)
    up, down = ring_round(up, down, held, 2, shards)
    (given,) = other_core((away,), shards)
    parts = rhs_sums(*inputs, 0, given, owners, own_rows)
    up, down, parts, crossed = together((up, down, parts, crossed))

    up, down = ring_round(up, down, held, 3, shards)
    given = exchange_chips(parts, shards, owners)
    total = join_chips(given, own_rows)
    up, down, total, held = together((up, down, total, held))

    for step in range(4, chips // 2 + 1):
        up, down = ring_round(up, down, held, step, shards)
    terms = reduce_levels(total, shards)
    for step in range(2, chips // 2 + 1):
        cross(step)
    pieces = []
    for distance in range(chips):
        pieces += held[distance] + crossed[distance]
    first, second, third, dots = krylov(
        factor_start, activity[None], sub_factors, pieces, terms, mine.shape[0], slots, devices
    )
    everyone = lax.all_to_all(dots, AXES, 0, 0, tiled=True)
    return tuple(last_step(everyone, factor_start, first, second, third))


def solution(mesh):
    placed = (
        P(("loop", "own"), None),
        P(("loop", "own")),
        P("loop", None, None, None),
        P(),
        P("loop", "own", None, None, None, None),
        P("loop", "own", None, None),
        P("loop", "own", None, None),
        P("loop", "own", None, None),
        P("loop", "own", None),
        P("loop", "own", None, None, None, None),
    )
    return jax.shard_map(
        on_device,
        mesh=mesh,
        in_specs=placed,
        out_specs=(P(("loop", "own"), None), P(("loop", "own"), None)),
        check_vma=False,
    )
```

```python
import functools

import jax
import jax.numpy as jnp
from jax import lax
from jax.experimental import pallas as pl
from jax.experimental.pallas import tpu as pltpu
from jax.sharding import PartitionSpec as P

AXES = ("loop", "own")
CHUNK = 48
FACT_ROWS = 16
ridge = 0.05
MIB = 2**20
VMEM_LIMIT = 60 * MIB
f32 = jnp.float32
bf16 = jnp.bfloat16


def dot_nt(left, right):
    return lax.dot_general(left, right, (((1,), (1,)), ((), ())), preferred_element_type=f32)


def dot_nn(left, right):
    return jnp.dot(left, right, preferred_element_type=f32)


def mask_columns(first, length, tile):
    column = lax.broadcasted_iota(jnp.int32, (tile, first.shape[-1]), 0)
    inside = ((column - first) & (tile - 1)) < length
    return jnp.where(inside, 1.0, 0.0).astype(bf16)


def fact_line(user_tile, word_tile, subreddit, live, group, slots, rank):
    lane = lax.broadcasted_iota(jnp.int32, (1, rank), 1)
    line = jnp.zeros((1, rank), jnp.int32)
    for s in range(slots):
        sub = subreddit[s, group]
        user = jnp.where(s < live, user_tile[s, group] + 1, 0)
        values = (user, word_tile[s, group], lax.div(sub, 128), lax.rem(sub, 128))
        for k, value in enumerate(values):
            line = jnp.where(lane == k * slots + s, value, line)
    return line.astype(f32)


def rhs_kernel(
    user_tile, word_tile, subreddit, counts, ratings_in, runs_in, words_in, subs_in, *refs,
    half, owners, own_rows,
):
    if half == 0:
        given, refs = refs[0], refs[1:]
    else:
        refs, (ready, sent) = refs[:-2], refs[-2:]
    outs, (ratings, runs, words, subs, table, sums, arrived, loaded) = refs[:-8], refs[-8:]
    steps, slots, tile = ratings.shape[0], ratings.shape[1], ratings.shape[2]
    rank = words.shape[-1]
    levels = steps // 2

    place = lax.axis_index("loop")
    level, seat = lax.div(place, 4), lax.rem(place, 4)

    def group_at(step):
        there = lax.rem(seat + 2 * (step // levels), 4)
        if half:
            there = there + 1 - 2 * lax.rem(there, 2)
        return 4 * lax.rem(level + step % levels, levels) + there

    def load(step):
        group = group_at(step)
        return pltpu.make_async_copy(ratings_in.at[group], ratings.at[step], arrived.at[step])

    tables = [
        pltpu.make_async_copy(source, target, loaded.at[k])
        for k, (source, target) in enumerate(
            [(subs_in, subs), (runs_in, runs), (words_in, words)]
        )
    ]
    for copy in tables:
        copy.start()
    for step in range(steps):
        load(step).start()
    tables[0].wait()
    table[...] = subs[...].astype(f32)
    tables[1].wait()
    tables[2].wait()

    eye = (
        lax.broadcasted_iota(jnp.int32, (tile, tile), 0)
        == lax.broadcasted_iota(jnp.int32, (tile, tile), 1)
    ).astype(f32).astype(bf16)
    me = lax.axis_index("own")
    sends = []
    for step in range(steps):
        group = group_at(step)
        live = counts[0, group]
        columns = []
        for s in range(slots):
            pair = runs[group, s]
            columns.append(
                mask_columns(pair[0:1], jnp.where(s < live, pair[1:2], 0), tile)
            )
        seen = dot_nt(eye, jnp.concatenate(columns, axis=0)).astype(bf16)
        load(step).wait()
        sums[step % 2] = jnp.zeros(sums.shape[1:], f32)
        for s in range(slots):
            sub_row = table[pl.ds(subreddit[s, group], 1), :]
            product = (words[word_tile[s, group]].astype(f32) * sub_row).astype(bf16)
            weights = seen[:, s * tile : (s + 1) * tile] * ratings[step, s]
            rows = pl.ds(pl.multiple_of(user_tile[s, group] * tile, tile), tile)
            sums[step % 2, rows, :] += dot_nn(weights, product)
        line = fact_line(user_tile, word_tile, subreddit, live, group, slots, rank)
        spans = jnp.concatenate([runs[group, s] for s in range(slots)], axis=0).astype(f32)
        end = own_rows + 2 * slots
        for o in range(owners):
            owner = lax.rem(me + o, owners)
            rows = pl.ds(pl.multiple_of(owner * own_rows, own_rows), own_rows)
            value = sums[step % 2, rows, :]
            column, up = step // levels, step % levels
            if half == 0:
                other = given[o, column, up].astype(f32)
                value = jnp.concatenate(
                    [
                        value + other[:own_rows],
                        spans,
                        other[own_rows:end],
                        line,
                        other[end : end + 1],
                        jnp.zeros((FACT_ROWS - 2, rank), f32),
                    ],
                    axis=0,
                )
                outs[2 * o + column][up] = value.astype(bf16)
            else:
                value = jnp.concatenate(
                    [value, spans, line, jnp.zeros((FACT_ROWS - 1, rank), f32)], axis=0
                )
                ready[o, column, up] = value.astype(bf16)
                here = (o, column, up)
                send = pltpu.make_async_copy(
                    ready.at[here], outs[0].at[here], sent.at[step * owners + o]
                )
                send.start()
                sends.append(send)
    for send in sends:
        send.wait()


def rhs_sums(scalars, ratings, runs, words, subs, half, given, owners, own_rows):
    groups, slots, tile, _ = ratings.shape
    rank = words.shape[-1]
    steps, levels = groups // 2, groups // 4
    anywhere = pl.BlockSpec(memory_space=pl.ANY)
    whole = pl.BlockSpec(memory_space=pltpu.VMEM)
    part = (levels, own_rows + 2 * slots * (2 - half) + FACT_ROWS, rank)
    shapes = [part] * (2 * owners) if half == 0 else [(owners, 2) + part]
    return pl.pallas_call(
        functools.partial(rhs_kernel, half=half, owners=owners, own_rows=own_rows),
        in_specs=[pl.BlockSpec(memory_space=pltpu.SMEM)] * 4
        + [anywhere] * 4
        + [whole] * (1 - half),
        out_specs=[anywhere if half else whole] * len(shapes),
        out_shape=[jax.ShapeDtypeStruct(shape, bf16) for shape in shapes],
        scratch_shapes=[
            pltpu.VMEM((steps,) + ratings.shape[1:], bf16),
            pltpu.VMEM(runs.shape, jnp.int32),
            pltpu.VMEM(words.shape, bf16),
            pltpu.VMEM(subs.shape, bf16),
            pltpu.VMEM(subs.shape, f32),
            pltpu.VMEM((2, owners * own_rows, rank), f32),
            pltpu.SemaphoreType.DMA((steps,)),
            pltpu.SemaphoreType.DMA((3,)),
        ]
        + [pltpu.VMEM(shapes[0], bf16), pltpu.SemaphoreType.DMA((steps * owners,))] * half,
        compiler_params=pltpu.CompilerParams(vmem_limit_bytes=VMEM_LIMIT if half else 50 * MIB),
        cost_estimate=pl.CostEstimate(
            flops=8 * ratings.size * rank, bytes_accessed=8 * ratings.size, transcendentals=0
        ),
        name="rhs",
    )(*scalars, ratings, runs, words, subs, *([given] if half == 0 else []))


def chip_kernel(*refs, own_rows, spans):
    levels, _, rank = refs[0].shape
    parts, outs = refs[:-levels], refs[-levels:]
    lines = outs[0].shape[0] - own_rows - spans * len(parts)
    for up in range(levels):
        total = parts[0][up, :own_rows, :].astype(f32)
        for part in parts[1:]:
            total = total + part[up, :own_rows, :].astype(f32)
        outs[up][:own_rows, :] = total.astype(bf16)
        facts = []
        for k, part in enumerate(parts):
            at = own_rows + spans * k
            outs[up][at : at + spans, :] = part[up, own_rows : own_rows + spans, :]
            facts.append(part[up, own_rows + spans :, :].astype(f32)[:2])
        facts.append(jnp.zeros((lines - 2 * len(parts), rank), f32))
        outs[up][own_rows + spans * len(parts) :, :] = jnp.concatenate(
            facts[: len(facts) - (lines == 2 * len(parts))], axis=0
        ).astype(bf16)


def exchange_chips(parts, shards, owners):
    given = []
    for o in range(owners):
        for column in range(2):
            pairs = [
                (shard * owners + k, (shard ^ 2 * column) * owners + (k + o) % owners)
                for shard in range(shards)
                for k in range(owners)
            ]
            part = parts[2 * o + column]
            given.append(lax.ppermute(part, AXES, pairs) if o or column else part)
    return given


def join_chips(parts, own_rows):
    levels, rows, rank = parts[0].shape
    spans = rows - own_rows - FACT_ROWS
    lines = -(-2 * len(parts) // FACT_ROWS) * FACT_ROWS
    whole = pl.BlockSpec(memory_space=pltpu.VMEM)
    shape = jax.ShapeDtypeStruct((own_rows + spans * len(parts) + lines, rank), bf16)
    return pl.pallas_call(
        functools.partial(chip_kernel, own_rows=own_rows, spans=spans),
        in_specs=[whole] * len(parts),
        out_specs=[whole] * levels,
        out_shape=[shape] * levels,
        compiler_params=pltpu.CompilerParams(vmem_limit_bytes=16 * MIB),
        name="chip",
    )(*parts)


def reduce_levels(total, shards):
    levels = shards // 4
    terms = [total[0]]
    for up in range(1, levels):
        shift = [(shard, (shard + 4 * up) % shards) for shard in range(shards)]
        terms.append(lax.ppermute(total[up], "loop", shift))
    return terms


def steps_kernel(activity, start, subs, *refs, count, word_tiles, levels, slots, cached):
    pieces, refs = refs[:count], refs[count:]
    terms, refs = refs[:levels], refs[levels:]
    first_out, second_out, third_out, dots_out = refs[:4]
    masks, words, table, runs, lines, facts, chosen, places, arrived, moved = refs[4:14]
    products = refs[-1]
    own_rows, rank = start.shape
    _, tile, _ = pieces[0].shape
    sources = lines.shape[0] // levels
    spans = 2 * slots * sources

    copies, at = [], 0
    for k, piece in enumerate(pieces):
        place = words.at[at : at + piece.shape[0]]
        copies.append(pltpu.make_async_copy(piece, place, arrived.at[k]))
        at += piece.shape[0]
    for copy in copies:
        copy.start()

    for up in range(levels):
        rest = terms[up][own_rows + spans :, :].astype(f32)
        lines[up * sources : (up + 1) * sources, :] = rest[:sources].astype(jnp.int32)
    move = pltpu.make_async_copy(lines, facts, moved.at[0])
    move.start()
    rhs = jnp.zeros((own_rows, rank), f32)
    for up in range(levels):
        rhs = rhs + terms[up][:own_rows, :].astype(f32)
        runs[up * spans : (up + 1) * spans, :] = terms[up][
            own_rows : own_rows + spans, :
        ].astype(f32)
    table[...] = subs[...].astype(f32)
    move.wait()

    place = lax.axis_index("loop")
    level, seat = lax.div(place, 4), lax.rem(place, 4)
    wanted = lax.div(lax.axis_index("own") * own_rows, tile) + 1
    chips = at // word_tiles // 2

    def ring_at(level, column):
        return jnp.where(column == 0, level, chips - 1 - level)

    used = 0
    column = lax.div(seat, 2)
    for up in range(levels):
        there = lax.rem(level - up + levels, levels)
        ahead = [
            lax.rem(ring_at(there, side) - ring_at(level, column) + chips, chips)
            for side in (column, 1 - column)
        ]

        def choose(k, n, up=up, ahead=ahead):
            src = up * sources + k
            side = lax.rem(lax.div(k, 2), 2)
            distance = jnp.where(side == 0, ahead[0], ahead[1])
            places[src] = word_tiles * (2 * distance + lax.rem(k, 2))
            for s in range(slots):
                chosen[n] = src * slots + s
                n = n + jnp.where(facts[src, s] == wanted, 1, 0)
            return n

        used = lax.fori_loop(0, sources, choose, used)
    chunks = lax.div(used + CHUNK - 1, CHUNK)

    offset = lax.rem(lax.axis_index("own") * own_rows, tile)
    pick = (
        lax.broadcasted_iota(jnp.int32, (own_rows, tile), 0) + offset
        == lax.broadcasted_iota(jnp.int32, (own_rows, tile), 1)
    ).astype(f32).astype(bf16)

    def mask(chunk):
        parts = []
        for b in range(CHUNK):
            i = chunk * CHUNK + b
            j = chosen[jnp.minimum(i, used - 1)]
            first = runs[pl.ds(2 * j, 1), :].astype(jnp.int32)
            length = runs[pl.ds(2 * j + 1, 1), :].astype(jnp.int32)
            length = jnp.where(i < used, length, 0)
            parts.append(mask_columns(first, length, tile))
        return dot_nt(pick, jnp.concatenate(parts, axis=0)).astype(bf16)

    def product(i):
        j = chosen[jnp.minimum(i, used - 1)]
        src, s = lax.div(j, slots), lax.rem(j, slots)
        sub = 128 * facts[src, 2 * slots + s] + facts[src, 3 * slots + s]
        rows = words[places[src] + facts[src, slots + s]].astype(f32)
        return (rows * table[pl.ds(sub, 1), :]).astype(bf16)

    for copy in copies:
        copy.wait()

    def gram(vector, build=False):
        rounded = vector.astype(bf16)

        def body(chunk, total):
            if build:
                masks[chunk] = mask(chunk)
            if cached and not build:
                block = products[chunk]
            else:
                block = jnp.concatenate(
                    [product(chunk * CHUNK + b) for b in range(CHUNK)], axis=0
                )
                if cached:
                    products[chunk] = block
            weights = dot_nt(rounded, block).astype(bf16) * masks[chunk]
            return total + dot_nn(weights, block)

        return lax.fori_loop(0, chunks, body, jnp.zeros((own_rows, rank), f32))

    def over_row(a, b):
        return jnp.sum(a * b, axis=1, keepdims=True)

    scale = jnp.broadcast_to(activity[...], (rank, own_rows)).T
    first = scale * (rhs - gram(start[...], build=True)) - ridge * start[...]
    second = scale * gram(first) + ridge * first
    norms, overlaps = over_row(first, first), over_row(first, second)
    share = jnp.where(norms > 0.0, overlaps / jnp.where(norms > 0.0, norms, 1.0), 0.0)
    rest = second - share * first
    third = scale * gram(rest) + ridge * rest + share * second
    first_out[...] = first
    second_out[...] = second
    third_out[...] = third
    rows = [norms, overlaps, over_row(second, second), over_row(first, third), over_row(second, third)]
    lane = lax.broadcasted_iota(jnp.int32, (1, rank), 1)
    line = jnp.zeros((1, rank), f32)
    for k, value in enumerate(rows):
        line = line + jnp.where(lane == k, jnp.sum(value, axis=0, keepdims=True), 0.0)
    dots_out[...] = jnp.broadcast_to(line[None], dots_out.shape)


def krylov(start, activity, subs, pieces, terms, word_tiles, slots, devices):
    own_rows, rank = start.shape
    blocks = devices * slots
    _, tile, _ = pieces[0].shape
    chunks = -(-blocks // CHUNK)
    cached = blocks * tile * rank * 2 <= 16 * 2**20
    whole = pl.BlockSpec(memory_space=pltpu.VMEM)
    anywhere = pl.BlockSpec(memory_space=pl.ANY)
    vector = jax.ShapeDtypeStruct((own_rows, rank), f32)
    scratch = [
        pltpu.VMEM((chunks, own_rows, CHUNK * tile), bf16),
        pltpu.VMEM((sum(piece.shape[0] for piece in pieces), tile, rank), bf16),
        pltpu.VMEM(subs.shape, f32),
        pltpu.VMEM((2 * blocks, tile), f32),
        pltpu.VMEM((devices, rank), jnp.int32),
        pltpu.SMEM((devices, rank), jnp.int32),
        pltpu.SMEM((blocks,), jnp.int32),
        pltpu.SMEM((devices,), jnp.int32),
        pltpu.SemaphoreType.DMA((len(pieces),)),
        pltpu.SemaphoreType.DMA((1,)),
    ]
    if cached:
        scratch.append(pltpu.VMEM((chunks, CHUNK * tile, rank), bf16))
    return pl.pallas_call(
        functools.partial(
            steps_kernel,
            count=len(pieces),
            word_tiles=word_tiles,
            levels=len(terms),
            slots=slots,
            cached=cached,
        ),
        in_specs=[whole] * 3 + [anywhere] * len(pieces) + [whole] * len(terms),
        out_specs=[whole] * 4,
        out_shape=[vector, vector, vector, jax.ShapeDtypeStruct((devices, 1, rank), f32)],
        scratch_shapes=scratch,
        compiler_params=pltpu.CompilerParams(vmem_limit_bytes=44 * MIB),
        name="krylov",
    )(activity, start, subs, *pieces, *terms)


def last_kernel(dots, start, first, second, third, solution_out, residual_out):
    line = dots[0]
    for k in range(1, dots.shape[0]):
        line = line + dots[k]
    rr, rq, qq, rz, qz = (line[:, k : k + 1] for k in range(5))
    step0 = rr / rq
    next_rr = rr - 2.0 * step0 * rq + step0 * step0 * qq
    grow = 1.0 + next_rr / rr
    slope = grow * (grow * rq - step0 * (rz + qq)) + step0 * step0 * qz
    step1 = next_rr / slope
    near, far = step0 + step1 * grow, step1 * step0
    solution_out[...] = start[...] + near * first[...] - far * second[...]
    residual_out[...] = first[...] - near * second[...] + far * third[...]


def last_step(dots, start, first, second, third):
    whole = pl.BlockSpec(memory_space=pltpu.VMEM)
    vector = jax.ShapeDtypeStruct(start.shape, f32)
    return pl.pallas_call(
        last_kernel,
        in_specs=[whole] * 5,
        out_specs=[whole] * 2,
        out_shape=[vector, vector],
        compiler_params=pltpu.CompilerParams(vmem_limit_bytes=8 * MIB),
        name="last_step",
    )(dots, start, first, second, third)


def ring_round(up, down, held, step, shards):
    chips = shards // 2
    levels = chips // 2
    order = [2 * level for level in range(levels)] + [
        2 * level + 1 for level in reversed(range(levels))
    ]

    def shift(by):
        return [
            (2 * order[p] + core, 2 * order[(p + by) % chips] + core)
            for p in range(chips)
            for core in range(2)
        ]

    if step == chips - step:
        half = up.shape[0] // 2
        up = lax.ppermute(up[:half], "loop", shift(1))
        down = lax.ppermute(down[half:], "loop", shift(-1))
        held[step] = (up, down)
    else:
        up = lax.ppermute(up, "loop", shift(1))
        down = lax.ppermute(down, "loop", shift(-1))
        held[chips - step], held[step] = (up,), (down,)
    return up, down


def other_core(values, shards):
    pairs = [(shard, shard ^ 1) for shard in range(shards)]
    return tuple(lax.ppermute(value, "loop", pairs) for value in values)


def on_device(
    factor_start,
    activity,
    word_factors,
    sub_factors,
    ratings,
    user_tile,
    word_tile,
    subreddit,
    counts,
    runs,
):
    own_rows, rank = factor_start.shape
    owners, shards = lax.axis_size("own"), lax.axis_size("loop")
    slots = ratings.shape[3]
    devices = shards * owners
    chips = shards // 2
    together = lax.optimization_barrier

    scalars = (user_tile[0, 0].T, word_tile[0, 0].T, subreddit[0, 0].T, counts[0])
    mine = word_factors[0]
    held = {0: (mine,)}

    inputs = (scalars, ratings[0, 0], runs[0, 0], mine, sub_factors)
    up, down = ring_round(mine, mine, held, 1, shards)
    (away,) = rhs_sums(*inputs, 1, None, owners, own_rows)
    crossed = {0: other_core(held[0], shards)}
    up, down, away, crossed = together((up, down, away, crossed))

    def cross(step):
        for distance in {step, chips - step}:
            crossed[distance] = other_core(held[distance], shards)

    cross(1)
    up, down = ring_round(up, down, held, 2, shards)
    (given,) = other_core((away,), shards)
    parts = rhs_sums(*inputs, 0, given, owners, own_rows)
    up, down, parts, crossed = together((up, down, parts, crossed))

    up, down = ring_round(up, down, held, 3, shards)
    given = exchange_chips(parts, shards, owners)
    total = join_chips(given, own_rows)
    up, down, total, held = together((up, down, total, held))

    for step in range(4, chips // 2 + 1):
        up, down = ring_round(up, down, held, step, shards)
    terms = reduce_levels(total, shards)
    for step in range(2, chips // 2 + 1):
        cross(step)
    pieces = []
    for distance in range(chips):
        pieces += held[distance] + crossed[distance]
    first, second, third, dots = krylov(
        factor_start, activity[None], sub_factors, pieces, terms, mine.shape[0], slots, devices
    )
    everyone = lax.all_to_all(dots, AXES, 0, 0, tiled=True)
    return tuple(last_step(everyone, factor_start, first, second, third))


def solution(mesh):
    placed = (
        P(("loop", "own"), None),
        P(("loop", "own")),
        P("loop", None, None, None),
        P(),
        P("loop", "own", None, None, None, None),
        P("loop", "own", None, None),
        P("loop", "own", None, None),
        P("loop", "own", None, None),
        P("loop", "own", None),
        P("loop", "own", None, None, None, None),
    )
    return jax.shard_map(
        on_device,
        mesh=mesh,
        in_specs=placed,
        out_specs=(P(("loop", "own"), None), P(("loop", "own"), None)),
        check_vma=False,
    )
```

```python
import functools

import jax
import jax.numpy as jnp
from jax import lax
from jax.experimental import pallas as pl
from jax.experimental.pallas import tpu as pltpu
from jax.sharding import PartitionSpec as P

AXES = ("loop", "own")
CHUNK = 48
FACT_ROWS = 16
ridge = 0.05
MIB = 2**20
VMEM_LIMIT = 60 * MIB
f32 = jnp.float32
bf16 = jnp.bfloat16


def dot_nt(left, right):
    return lax.dot_general(left, right, (((1,), (1,)), ((), ())), preferred_element_type=f32)


def dot_nn(left, right):
    return jnp.dot(left, right, preferred_element_type=f32)


def mask_columns(first, length, tile):
    column = lax.broadcasted_iota(jnp.int32, (tile, first.shape[-1]), 0)
    inside = ((column - first) & (tile - 1)) < length
    return jnp.where(inside, 1.0, 0.0).astype(bf16)


def fact_line(user_tile, word_tile, subreddit, live, group, slots, rank):
    lane = lax.broadcasted_iota(jnp.int32, (1, rank), 1)
    line = jnp.zeros((1, rank), jnp.int32)
    for s in range(slots):
        sub = subreddit[s, group]
        user = jnp.where(s < live, user_tile[s, group] + 1, 0)
        values = (user, word_tile[s, group], lax.div(sub, 128), lax.rem(sub, 128))
        for k, value in enumerate(values):
            line = jnp.where(lane == k * slots + s, value, line)
    return line.astype(f32)


def rhs_kernel(
    user_tile, word_tile, subreddit, counts, ratings_in, runs_in, words_in, subs_in, *refs,
    half, owners, own_rows,
):
    if half == 0:
        given, refs = refs[0], refs[1:]
    outs, (ratings, runs, words, subs, table, sums, arrived, loaded) = refs[:-8], refs[-8:]
    steps, slots, tile = ratings.shape[0], ratings.shape[1], ratings.shape[2]
    rank = words.shape[-1]
    levels = steps // 2

    place = lax.axis_index("loop")
    level, seat = lax.div(place, 4), lax.rem(place, 4)

    def group_at(step):
        there = lax.rem(seat + 2 * (step // levels), 4)
        if half:
            there = there + 1 - 2 * lax.rem(there, 2)
        return 4 * lax.rem(level + step % levels, levels) + there

    def load(step):
        group = group_at(step)
        return pltpu.make_async_copy(ratings_in.at[group], ratings.at[step], arrived.at[step])

    tables = [
        pltpu.make_async_copy(source, target, loaded.at[k])
        for k, (source, target) in enumerate(
            [(subs_in, subs), (runs_in, runs), (words_in, words)]
        )
    ]
    for copy in tables:
        copy.start()
    for step in range(steps):
        load(step).start()
    tables[0].wait()
    table[...] = subs[...].astype(f32)
    tables[1].wait()
    tables[2].wait()

    eye = (
        lax.broadcasted_iota(jnp.int32, (tile, tile), 0)
        == lax.broadcasted_iota(jnp.int32, (tile, tile), 1)
    ).astype(f32).astype(bf16)
    me = lax.axis_index("own")
    for step in range(steps):
        group = group_at(step)
        live = counts[0, group]
        columns = []
        for s in range(slots):
            pair = runs[group, s]
            columns.append(
                mask_columns(pair[0:1], jnp.where(s < live, pair[1:2], 0), tile)
            )
        seen = dot_nt(eye, jnp.concatenate(columns, axis=0)).astype(bf16)
        load(step).wait()
        sums[step % 2] = jnp.zeros(sums.shape[1:], f32)
        for s in range(slots):
            sub_row = table[pl.ds(subreddit[s, group], 1), :]
            product = (words[word_tile[s, group]].astype(f32) * sub_row).astype(bf16)
            weights = seen[:, s * tile : (s + 1) * tile] * ratings[step, s]
            rows = pl.ds(pl.multiple_of(user_tile[s, group] * tile, tile), tile)
            sums[step % 2, rows, :] += dot_nn(weights, product)
        line = fact_line(user_tile, word_tile, subreddit, live, group, slots, rank)
        spans = jnp.concatenate([runs[group, s] for s in range(slots)], axis=0).astype(f32)
        end = own_rows + 2 * slots
        for o in range(owners):
            owner = lax.rem(me + o, owners)
            rows = pl.ds(pl.multiple_of(owner * own_rows, own_rows), own_rows)
            value = sums[step % 2, rows, :]
            column, up = step // levels, step % levels
            if half == 0:
                other = given[o, column, up].astype(f32)
                value = jnp.concatenate(
                    [
                        value + other[:own_rows],
                        spans,
                        other[own_rows:end],
                        line,
                        other[end : end + 1],
                        jnp.zeros((FACT_ROWS - 2, rank), f32),
                    ],
                    axis=0,
                )
                outs[2 * o + column][up] = value.astype(bf16)
            else:
                value = jnp.concatenate(
                    [value, spans, line, jnp.zeros((FACT_ROWS - 1, rank), f32)], axis=0
                )
                outs[0][o, column, up] = value.astype(bf16)


def rhs_sums(scalars, ratings, runs, words, subs, half, given, owners, own_rows):
    groups, slots, tile, _ = ratings.shape
    rank = words.shape[-1]
    steps, levels = groups // 2, groups // 4
    anywhere = pl.BlockSpec(memory_space=pl.ANY)
    whole = pl.BlockSpec(memory_space=pltpu.VMEM)
    part = (levels, own_rows + 2 * slots * (2 - half) + FACT_ROWS, rank)
    shapes = [part] * (2 * owners) if half == 0 else [(owners, 2) + part]
    return pl.pallas_call(
        functools.partial(rhs_kernel, half=half, owners=owners, own_rows=own_rows),
        in_specs=[pl.BlockSpec(memory_space=pltpu.SMEM)] * 4
        + [anywhere] * 4
        + [whole] * (1 - half),
        out_specs=[whole] * len(shapes),
        out_shape=[jax.ShapeDtypeStruct(shape, bf16) for shape in shapes],
        scratch_shapes=[
            pltpu.VMEM((steps,) + ratings.shape[1:], bf16),
            pltpu.VMEM(runs.shape, jnp.int32),
            pltpu.VMEM(words.shape, bf16),
            pltpu.VMEM(subs.shape, bf16),
            pltpu.VMEM(subs.shape, f32),
            pltpu.VMEM((2, owners * own_rows, rank), f32),
            pltpu.SemaphoreType.DMA((steps,)),
            pltpu.SemaphoreType.DMA((3,)),
        ],
        compiler_params=pltpu.CompilerParams(vmem_limit_bytes=VMEM_LIMIT if half else 50 * MIB),
        cost_estimate=pl.CostEstimate(
            flops=8 * ratings.size * rank, bytes_accessed=8 * ratings.size, transcendentals=0
        ),
        name="rhs",
    )(*scalars, ratings, runs, words, subs, *([given] if half == 0 else []))


def far_first(count):
    return [0] + list(range(count - 1, 0, -2)) + list(range(2, count, 2))


def chip_kernel(*refs, own_rows, spans):
    levels, _, rank = refs[0].shape
    given, outs = refs[:-levels], refs[-levels:]
    parts = [given[far_first(len(given)).index(k)] for k in range(len(given))]
    lines = outs[0].shape[0] - own_rows - spans * len(parts)
    for up in range(levels):
        total = parts[0][up, :own_rows, :].astype(f32)
        for part in parts[1:]:
            total = total + part[up, :own_rows, :].astype(f32)
        outs[up][:own_rows, :] = total.astype(bf16)
        facts = []
        for k, part in enumerate(parts):
            at = own_rows + spans * k
            outs[up][at : at + spans, :] = part[up, own_rows : own_rows + spans, :]
            facts.append(part[up, own_rows + spans :, :].astype(f32)[:2])
        facts.append(jnp.zeros((lines - 2 * len(parts), rank), f32))
        outs[up][own_rows + spans * len(parts) :, :] = jnp.concatenate(
            facts[: len(facts) - (lines == 2 * len(parts))], axis=0
        ).astype(bf16)


def exchange_chips(parts, shards, owners):
    given = []
    for o in range(owners):
        for column in range(2):
            pairs = [
                (shard * owners + k, (shard ^ 2 * column) * owners + (k + o) % owners)
                for shard in range(shards)
                for k in range(owners)
            ]
            part = parts[2 * o + column]
            given.append(lax.ppermute(part, AXES, pairs) if o or column else part)
    return given


def join_chips(parts, own_rows):
    levels, rows, rank = parts[0].shape
    spans = rows - own_rows - FACT_ROWS
    lines = -(-2 * len(parts) // FACT_ROWS) * FACT_ROWS
    whole = pl.BlockSpec(memory_space=pltpu.VMEM)
    shape = jax.ShapeDtypeStruct((own_rows + spans * len(parts) + lines, rank), bf16)
    return pl.pallas_call(
        functools.partial(chip_kernel, own_rows=own_rows, spans=spans),
        in_specs=[whole] * len(parts),
        out_specs=[whole] * levels,
        out_shape=[shape] * levels,
        compiler_params=pltpu.CompilerParams(vmem_limit_bytes=16 * MIB),
        name="chip",
    )(*[parts[k] for k in far_first(len(parts))])


def reduce_levels(total, shards):
    levels = shards // 4
    terms = [total[0]]
    for up in range(1, levels):
        shift = [(shard, (shard + 4 * up) % shards) for shard in range(shards)]
        terms.append(lax.ppermute(total[up], "loop", shift))
    return terms


def steps_kernel(activity, start, subs, *refs, count, word_tiles, levels, slots, cached):
    pieces, refs = refs[:count], refs[count:]
    terms, refs = refs[:levels], refs[levels:]
    first_out, second_out, third_out, dots_out = refs[:4]
    masks, words, table, runs, lines, facts, chosen, places, arrived, moved = refs[4:14]
    products = refs[-1]
    own_rows, rank = start.shape
    _, tile, _ = pieces[0].shape
    sources = lines.shape[0] // levels
    spans = 2 * slots * sources

    copies, at = [], 0
    for k, piece in enumerate(pieces):
        place = words.at[at : at + piece.shape[0]]
        copies.append(pltpu.make_async_copy(piece, place, arrived.at[k]))
        at += piece.shape[0]
    for copy in copies:
        copy.start()

    for up in range(levels):
        rest = terms[up][own_rows + spans :, :].astype(f32)
        lines[up * sources : (up + 1) * sources, :] = rest[:sources].astype(jnp.int32)
    move = pltpu.make_async_copy(lines, facts, moved.at[0])
    move.start()
    rhs = jnp.zeros((own_rows, rank), f32)
    for up in range(levels):
        rhs = rhs + terms[up][:own_rows, :].astype(f32)
        runs[up * spans : (up + 1) * spans, :] = terms[up][
            own_rows : own_rows + spans, :
        ].astype(f32)
    table[...] = subs[...].astype(f32)
    move.wait()

    place = lax.axis_index("loop")
    level, seat = lax.div(place, 4), lax.rem(place, 4)
    wanted = lax.div(lax.axis_index("own") * own_rows, tile) + 1
    chips = at // word_tiles // 2

    def ring_at(level, column):
        return jnp.where(column == 0, level, chips - 1 - level)

    used = 0
    column = lax.div(seat, 2)
    for up in range(levels):
        there = lax.rem(level - up + levels, levels)
        ahead = [
            lax.rem(ring_at(there, side) - ring_at(level, column) + chips, chips)
            for side in (column, 1 - column)
        ]

        def choose(k, n, up=up, ahead=ahead):
            src = up * sources + k
            side = lax.rem(lax.div(k, 2), 2)
            distance = jnp.where(side == 0, ahead[0], ahead[1])
            places[src] = word_tiles * (2 * distance + lax.rem(k, 2))
            for s in range(slots):
                chosen[n] = src * slots + s
                n = n + jnp.where(facts[src, s] == wanted, 1, 0)
            return n

        used = lax.fori_loop(0, sources, choose, used)
    chunks = lax.div(used + CHUNK - 1, CHUNK)

    offset = lax.rem(lax.axis_index("own") * own_rows, tile)
    pick = (
        lax.broadcasted_iota(jnp.int32, (own_rows, tile), 0) + offset
        == lax.broadcasted_iota(jnp.int32, (own_rows, tile), 1)
    ).astype(f32).astype(bf16)

    def mask(chunk):
        parts = []
        for b in range(CHUNK):
            i = chunk * CHUNK + b
            j = chosen[jnp.minimum(i, used - 1)]
            first = runs[pl.ds(2 * j, 1), :].astype(jnp.int32)
            length = runs[pl.ds(2 * j + 1, 1), :].astype(jnp.int32)
            length = jnp.where(i < used, length, 0)
            parts.append(mask_columns(first, length, tile))
        return dot_nt(pick, jnp.concatenate(parts, axis=0)).astype(bf16)

    def product(i):
        j = chosen[jnp.minimum(i, used - 1)]
        src, s = lax.div(j, slots), lax.rem(j, slots)
        sub = 128 * facts[src, 2 * slots + s] + facts[src, 3 * slots + s]
        rows = words[places[src] + facts[src, slots + s]].astype(f32)
        return (rows * table[pl.ds(sub, 1), :]).astype(bf16)

    for copy in copies:
        copy.wait()

    def gram(vector, build=False):
        rounded = vector.astype(bf16)

        def body(chunk, total):
            if build:
                masks[chunk] = mask(chunk)
            if cached and not build:
                block = products[chunk]
            else:
                block = jnp.concatenate(
                    [product(chunk * CHUNK + b) for b in range(CHUNK)], axis=0
                )
                if cached:
                    products[chunk] = block
            weights = dot_nt(rounded, block).astype(bf16) * masks[chunk]
            return total + dot_nn(weights, block)

        return lax.fori_loop(0, chunks, body, jnp.zeros((own_rows, rank), f32))

    def over_row(a, b):
        return jnp.sum(a * b, axis=1, keepdims=True)

    scale = jnp.broadcast_to(activity[...], (rank, own_rows)).T
    first = scale * (rhs - gram(start[...], build=True)) - ridge * start[...]
    second = scale * gram(first) + ridge * first
    norms, overlaps = over_row(first, first), over_row(first, second)
    share = jnp.where(norms > 0.0, overlaps / jnp.where(norms > 0.0, norms, 1.0), 0.0)
    rest = second - share * first
    third = scale * gram(rest) + ridge * rest + share * second
    first_out[...] = first
    second_out[...] = second
    third_out[...] = third
    rows = [norms, overlaps, over_row(second, second), over_row(first, third), over_row(second, third)]
    lane = lax.broadcasted_iota(jnp.int32, (1, rank), 1)
    line = jnp.zeros((1, rank), f32)
    for k, value in enumerate(rows):
        line = line + jnp.where(lane == k, jnp.sum(value, axis=0, keepdims=True), 0.0)
    dots_out[...] = jnp.broadcast_to(line[None], dots_out.shape)


def krylov(start, activity, subs, pieces, terms, word_tiles, slots, devices):
    own_rows, rank = start.shape
    blocks = devices * slots
    _, tile, _ = pieces[0].shape
    chunks = -(-blocks // CHUNK)
    cached = blocks * tile * rank * 2 <= 16 * 2**20
    whole = pl.BlockSpec(memory_space=pltpu.VMEM)
    anywhere = pl.BlockSpec(memory_space=pl.ANY)
    vector = jax.ShapeDtypeStruct((own_rows, rank), f32)
    scratch = [
        pltpu.VMEM((chunks, own_rows, CHUNK * tile), bf16),
        pltpu.VMEM((sum(piece.shape[0] for piece in pieces), tile, rank), bf16),
        pltpu.VMEM(subs.shape, f32),
        pltpu.VMEM((2 * blocks, tile), f32),
        pltpu.VMEM((devices, rank), jnp.int32),
        pltpu.SMEM((devices, rank), jnp.int32),
        pltpu.SMEM((blocks,), jnp.int32),
        pltpu.SMEM((devices,), jnp.int32),
        pltpu.SemaphoreType.DMA((len(pieces),)),
        pltpu.SemaphoreType.DMA((1,)),
    ]
    if cached:
        scratch.append(pltpu.VMEM((chunks, CHUNK * tile, rank), bf16))
    return pl.pallas_call(
        functools.partial(
            steps_kernel,
            count=len(pieces),
            word_tiles=word_tiles,
            levels=len(terms),
            slots=slots,
            cached=cached,
        ),
        in_specs=[whole] * 3 + [anywhere] * len(pieces) + [whole] * len(terms),
        out_specs=[whole] * 4,
        out_shape=[vector, vector, vector, jax.ShapeDtypeStruct((devices, 1, rank), f32)],
        scratch_shapes=scratch,
        compiler_params=pltpu.CompilerParams(vmem_limit_bytes=44 * MIB),
        name="krylov",
    )(activity, start, subs, *pieces, *terms)


def last_kernel(dots, start, first, second, third, solution_out, residual_out):
    line = dots[0]
    for k in range(1, dots.shape[0]):
        line = line + dots[k]
    rr, rq, qq, rz, qz = (line[:, k : k + 1] for k in range(5))
    step0 = rr / rq
    next_rr = rr - 2.0 * step0 * rq + step0 * step0 * qq
    grow = 1.0 + next_rr / rr
    slope = grow * (grow * rq - step0 * (rz + qq)) + step0 * step0 * qz
    step1 = next_rr / slope
    near, far = step0 + step1 * grow, step1 * step0
    solution_out[...] = start[...] + near * first[...] - far * second[...]
    residual_out[...] = first[...] - near * second[...] + far * third[...]


def last_step(dots, start, first, second, third):
    whole = pl.BlockSpec(memory_space=pltpu.VMEM)
    vector = jax.ShapeDtypeStruct(start.shape, f32)
    return pl.pallas_call(
        last_kernel,
        in_specs=[whole] * 5,
        out_specs=[whole] * 2,
        out_shape=[vector, vector],
        compiler_params=pltpu.CompilerParams(vmem_limit_bytes=8 * MIB),
        name="last_step",
    )(dots, start, first, second, third)


def ring_round(up, down, held, step, shards):
    chips = shards // 2
    levels = chips // 2
    order = [2 * level for level in range(levels)] + [
        2 * level + 1 for level in reversed(range(levels))
    ]

    def shift(by):
        return [
            (2 * order[p] + core, 2 * order[(p + by) % chips] + core)
            for p in range(chips)
            for core in range(2)
        ]

    if step == chips - step:
        half = up.shape[0] // 2
        up = lax.ppermute(up[:half], "loop", shift(1))
        down = lax.ppermute(down[half:], "loop", shift(-1))
        held[step] = (up, down)
    else:
        up = lax.ppermute(up, "loop", shift(1))
        down = lax.ppermute(down, "loop", shift(-1))
        held[chips - step], held[step] = (up,), (down,)
    return up, down


def other_core(values, shards):
    pairs = [(shard, shard ^ 1) for shard in range(shards)]
    return tuple(lax.ppermute(value, "loop", pairs) for value in values)


def on_device(
    factor_start,
    activity,
    word_factors,
    sub_factors,
    ratings,
    user_tile,
    word_tile,
    subreddit,
    counts,
    runs,
):
    own_rows, rank = factor_start.shape
    owners, shards = lax.axis_size("own"), lax.axis_size("loop")
    slots = ratings.shape[3]
    devices = shards * owners
    chips = shards // 2
    together = lax.optimization_barrier

    scalars = (user_tile[0, 0].T, word_tile[0, 0].T, subreddit[0, 0].T, counts[0])
    mine = word_factors[0]
    held = {0: (mine,)}

    inputs = (scalars, ratings[0, 0], runs[0, 0], mine, sub_factors)
    up, down = ring_round(mine, mine, held, 1, shards)
    (away,) = rhs_sums(*inputs, 1, None, owners, own_rows)
    crossed = {0: other_core(held[0], shards)}
    up, down, away, crossed = together((up, down, away, crossed))

    def cross(step):
        for distance in {step, chips - step}:
            crossed[distance] = other_core(held[distance], shards)

    cross(1)
    up, down = ring_round(up, down, held, 2, shards)
    (given,) = other_core((away,), shards)
    parts = rhs_sums(*inputs, 0, given, owners, own_rows)
    up, down, parts, crossed = together((up, down, parts, crossed))

    up, down = ring_round(up, down, held, 3, shards)
    given = exchange_chips(parts, shards, owners)
    total = join_chips(given, own_rows)
    up, down, total, held = together((up, down, total, held))

    for step in range(4, chips // 2 + 1):
        up, down = ring_round(up, down, held, step, shards)
    terms = reduce_levels(total, shards)
    for step in range(2, chips // 2 + 1):
        cross(step)
    pieces = []
    for distance in range(chips):
        pieces += held[distance] + crossed[distance]
    first, second, third, dots = krylov(
        factor_start, activity[None], sub_factors, pieces, terms, mine.shape[0], slots, devices
    )
    everyone = lax.all_to_all(dots, AXES, 0, 0, tiled=True)
    return tuple(last_step(everyone, factor_start, first, second, third))


def solution(mesh):
    placed = (
        P(("loop", "own"), None),
        P(("loop", "own")),
        P("loop", None, None, None),
        P(),
        P("loop", "own", None, None, None, None),
        P("loop", "own", None, None),
        P("loop", "own", None, None),
        P("loop", "own", None, None),
        P("loop", "own", None),
        P("loop", "own", None, None, None, None),
    )
    return jax.shard_map(
        on_device,
        mesh=mesh,
        in_specs=placed,
        out_specs=(P(("loop", "own"), None), P(("loop", "own"), None)),
        check_vma=False,
    )
```
